32 devices in a mesh: batch: 8 (over z, x), chan: 4 (over y, core).
Axes of the slice: x: 2, y: 2, z: 4, core: 2. Of those that a mesh axis runs over, the one named last changes fastest.
Arguments:
- block_input: bfloat16 [128, 14, 14, 1024], P('batch', None, None, 'chan'), may hold values from -6 to 6
- first_reduce: float32 [1024, 512], P('batch', 'chan'), may hold values from -0.1875 to 0.1875
- first_spatial: float32 [3, 3, 512, 512], P(None, None, 'batch', 'chan'), may hold values from -0.09375 to 0.09375
- first_expand: float32 [512, 2048], P('chan', 'batch'), may hold values from -0.25 to 0.25
- first_shortcut: float32 [1024, 2048], P('batch', 'chan'), may hold values from -0.1875 to 0.1875
- second_reduce: float32 [2048, 512], P('batch', 'chan'), may hold values from -0.125 to 0.125
- second_spatial: float32 [3, 3, 512, 512], P(None, None, 'batch', 'chan'), may hold values from -0.09375 to 0.09375
- second_expand: float32 [512, 2048], P('chan', 'batch'), may hold values from -0.25 to 0.25
- first_mid_gain: float32 [2, 512], P(None, 'chan'), may hold values from 0.5 to 1.5
- first_mid_bias: float32 [2, 512], P(None, 'chan'), may hold values from -2.5 to 2.5
- first_wide_gain: float32 [2, 2048], P(None, 'chan'), may hold values from 0.5 to 1.5
- first_wide_bias: float32 [2, 2048], P(None, 'chan'), may hold values from -2.5 to 2.5
- second_mid_gain: float32 [2, 512], P(None, 'chan'), may hold values from 0.5 to 1.5
- second_mid_bias: float32 [2, 512], P(None, 'chan'), may hold values from -2.5 to 2.5
- second_wide_gain: float32 [2048], P('chan'), may hold values from 0.5 to 1.5
- second_wide_bias: float32 [2048], P('chan'), may hold values from -2.5 to 2.5
- subnet_widths: int32 [3], replicated, may hold values from 256 to 480, as said below
- subnet_ids: int32 [128], replicated, may hold values from 0 to 2, as said below
- crop_sides: int32 [128], replicated, may hold values from 2 to 14, as said below
- cotangent: bfloat16 [128, 7, 7, 2048], P('batch', None, None, 'chan'), may hold values from -6 to 6
Outputs:
- output: float32 [128, 7, 7, 2048], P('batch', None, None, 'chan')
- input_grad: float32 [128, 14, 14, 1024], P('batch', None, None, 'chan')
- first_reduce_grad: float32 [1024, 512], P('batch', 'chan')
- first_spatial_grad: float32 [3, 3, 512, 512], P(None, None, 'batch', 'chan')
- first_expand_grad: float32 [512, 2048], P('chan', 'batch')
- first_shortcut_grad: float32 [1024, 2048], P('batch', 'chan')
- second_reduce_grad: float32 [2048, 512], P('batch', 'chan')
- second_spatial_grad: float32 [3, 3, 512, 512], P(None, None, 'batch', 'chan')
- second_expand_grad: float32 [512, 2048], P('chan', 'batch')
- first_mid_gain_grad: float32 [2, 512], P(None, 'chan')
- first_mid_bias_grad: float32 [2, 512], P(None, 'chan')
- first_wide_gain_grad: float32 [2, 2048], P(None, 'chan')
- first_wide_bias_grad: float32 [2, 2048], P(None, 'chan')
- second_mid_gain_grad: float32 [2, 512], P(None, 'chan')
- second_mid_bias_grad: float32 [2, 512], P(None, 'chan')
- second_wide_gain_grad: float32 [2048], P('chan')
- second_wide_bias_grad: float32 [2048], P('chan')
The draws below stay inside these ranges and needn't reach their ends.
Inputs may be any that keep to these rules, and one draw needn't show every extreme that they name: `subnet_widths`: multiples of 32; the smallest student has 256 channels and the largest 512 - 512 // 16. `subnet_ids`: every subnet trains at least one crop. `crop_sides`: even; crops 8k and 8k + 1 (an image's two large crops) have 14 - 2 or 14, the six others at most 6.
All inputs are finite; a program needn't handle non-finite values.
Results may differ from the reference program's by a relative error of at most 0.025.
Values may be sent and summed in bfloat16 or wider, within the bound.
No kernel may reach another device: no remote copies, remote signals or barrier semaphores. Data moves between devices by JAX's collectives and lax.ppermute only.
A program may use at most 192 MiB of HBM per device.

```python
import jax
import jax.numpy as jnp
from jax import lax

IN = 1024
MID = 512
OUT = 2048
SIDE = 14
HALF = 7
SUBNETS = 3
CROPS = 128


def draw_subnet_widths(key, part):
    key = jax.random.fold_in(key, 11)
    key_draw, key_order = jax.random.split(key)
    width_step = MID // 16
    widths = width_step * jax.random.randint(key_draw, (SUBNETS,), 8, 16)
    ordering = jax.random.permutation(key_order, SUBNETS)
    widths = widths.at[ordering[0]].set(width_step * 8)
    widths = widths.at[ordering[1]].set(width_step * 15)
    return widths.astype(jnp.int32)


def draw_subnet_ids(key, part):
    key = jax.random.fold_in(key, 12)
    key_draw, key_place = jax.random.split(key)
    labels = jax.random.randint(key_draw, (CROPS,), 0, SUBNETS)
    places = jax.random.permutation(key_place, CROPS)[:SUBNETS]
    labels = labels.at[places].set(jnp.arange(SUBNETS, dtype=jnp.int32))
    return labels.astype(jnp.int32)


def draw_crop_sides(key, part):
    key = jax.random.fold_in(key, 13)
    key_large, key_small = jax.random.split(key)
    large = 2 * jax.random.randint(key_large, (CROPS,), SIDE // 2 - 1, SIDE // 2 + 1)
    small = 2 * jax.random.randint(key_small, (CROPS,), 1, SIDE // 4 + 1)
    position = jnp.arange(CROPS, dtype=jnp.int32) % 8
    sides = jnp.where(position < 2, large, small)
    sides = sides.at[0].set(SIDE)
    sides = sides.at[2].set(2)
    return sides.astype(jnp.int32)


def block_scale(key, shape, pieces, low, high):
    loudness, own = 1.0, jax.random.fold_in(key, 6)
    for dim, shards_of in pieces:
        steps = jnp.exp(jax.random.uniform(jax.random.fold_in(own, dim), (shards_of,), jnp.float32, low / len(pieces), high / len(pieces)))
        loudness = loudness * jnp.repeat(steps, shape[dim] // shards_of).reshape([-1 if axis == dim else 1 for axis in range(len(shape))])
    return loudness


def normal_values(key, shape, width, most, shards=(), held_as=jnp.bfloat16):
    drawn = jax.random.normal(key, shape, jnp.float32) * width
    if len(shards) > 0:
        drawn = block_scale(key, shape, shards, -0.22, 0.18) * drawn
    return jnp.clip(drawn, min=-most, max=most).astype(held_as)


def setup_inputs(seed: int = 0) -> dict:
    streams_of = jax.random.split(jax.random.key(seed), 21)
    block_input = normal_values(streams_of[0], (CROPS, SIDE, SIDE, IN), 1.0, 6.0, ((0, 8), (3, 4)))
    first_reduce = normal_values(streams_of[1], (IN, MID), IN ** -0.5, 0.1875, ((0, 8), (1, 4)), jnp.float32)
    first_spatial = normal_values(streams_of[2], (3, 3, MID, MID), (9 * MID) ** -0.5, 0.09375, ((2, 8), (3, 4)), jnp.float32)
    first_expand = normal_values(streams_of[3], (MID, OUT), MID ** -0.5, 0.25, ((0, 4), (1, 8)), jnp.float32)
    first_shortcut = normal_values(streams_of[4], (IN, OUT), IN ** -0.5, 0.1875, ((0, 8), (1, 4)), jnp.float32)
    second_reduce = normal_values(streams_of[5], (OUT, MID), OUT ** -0.5, 0.125, ((0, 8), (1, 4)), jnp.float32)
    second_spatial = normal_values(streams_of[6], (3, 3, MID, MID), (9 * MID) ** -0.5, 0.09375, ((2, 8), (3, 4)), jnp.float32)
    second_expand = normal_values(streams_of[7], (MID, OUT), MID ** -0.5, 0.25, ((0, 4), (1, 8)), jnp.float32)
    first_mid_gain = jnp.clip(1.0 + 0.1 * jax.random.normal(streams_of[8], (2, MID), jnp.float32), 0.5, 1.5)
    first_mid_bias = normal_values(streams_of[9], (2, MID), 0.5, 2.5, ((1, 4),), jnp.float32)
    first_wide_gain = jnp.clip(1.0 + 0.1 * jax.random.normal(streams_of[10], (2, OUT), jnp.float32), 0.5, 1.5)
    first_wide_bias = normal_values(streams_of[11], (2, OUT), 0.5, 2.5, ((1, 4),), jnp.float32)
    second_mid_gain = jnp.clip(1.0 + 0.1 * jax.random.normal(streams_of[12], (2, MID), jnp.float32), 0.5, 1.5)
    second_mid_bias = normal_values(streams_of[13], (2, MID), 0.5, 2.5, ((1, 4),), jnp.float32)
    second_wide_gain = jnp.clip(1.0 + 0.1 * jax.random.normal(streams_of[14], (OUT,), jnp.float32), 0.5, 1.5)
    second_wide_bias = normal_values(streams_of[15], (OUT,), 0.5, 2.5, ((0, 4),), jnp.float32)
    subnet_widths = draw_subnet_widths(jax.random.fold_in(streams_of[20], 71), 0)
    subnet_ids = draw_subnet_ids(jax.random.fold_in(streams_of[20], 71), 0)
    crop_sides = draw_crop_sides(jax.random.fold_in(streams_of[20], 71), 0)
    cotangent = normal_values(streams_of[19], (CROPS, HALF, HALF, OUT), 1.0, 6.0, ((0, 8), (3, 4)))
    return dict(block_input=block_input, first_reduce=first_reduce, first_spatial=first_spatial, first_expand=first_expand, first_shortcut=first_shortcut, second_reduce=second_reduce, second_spatial=second_spatial, second_expand=second_expand, first_mid_gain=first_mid_gain, first_mid_bias=first_mid_bias, first_wide_gain=first_wide_gain, first_wide_bias=first_wide_bias, second_mid_gain=second_mid_gain, second_mid_bias=second_mid_bias, second_wide_gain=second_wide_gain, second_wide_bias=second_wide_bias, subnet_widths=subnet_widths, subnet_ids=subnet_ids, crop_sides=crop_sides, cotangent=cotangent)


epsilon = 1e-05
precise = lax.Precision.HIGHEST

@jax.custom_vjp
def low(v):
    return lax.optimization_barrier(v.astype(jnp.bfloat16)).astype(jnp.float32)

@jax.custom_vjp
def low_back(v):
    return v

def low_keep(v):
    return (low(v), None)

def low_pass(kept, grad):
    return (grad,)

def back_keep(v):
    return (v, None)

def back_low(kept, grad):
    return (low(grad),)
low.defvjp(low_keep, low_pass)
low_back.defvjp(back_keep, back_low)

def pointwise(values, weight):
    return jnp.einsum('chwk,km->chwm', values, weight, precision=precise)

def spatial(values, weight, stride):
    return lax.conv_general_dilated(values, weight, (stride, stride), ((1, 1), (1, 1)), dimension_numbers=('NHWC', 'HWIO', 'NHWC'), precision=precise)

def normalize(values, pixel_mask, member, counts, scaling, offset):
    masked = values * pixel_mask[..., None]
    first_sum = lax.optimization_barrier(jnp.sum(masked, axis=(1, 2)))
    second_sum = lax.optimization_barrier(jnp.sum(masked * values, axis=(1, 2)))
    average = jnp.dot(member, first_sum, precision=precise) / counts[:, None]
    squares = jnp.dot(member, second_sum, precision=precise) / counts[:, None]
    inverse = lax.rsqrt(squares - average * average + epsilon)
    crop_average = jnp.dot(member.T, average, precision=precise)
    crop_inverse = jnp.dot(member.T, inverse, precision=precise)
    return scaling * (values - crop_average[:, None, None, :]) * crop_inverse[:, None, None, :] + offset

def forward(params, mask_full, mask_half, member, count_full, count_half, active):
    block_input, first_reduce, first_spatial, first_expand, first_shortcut, second_reduce, second_spatial, second_expand, first_mid_gain, first_mid_bias, first_wide_gain, first_wide_bias, second_mid_gain, second_mid_bias, second_wide_gain, second_wide_bias = params
    keep_full = mask_full[..., None] * active[:, None, None, :]
    keep_half = mask_half[..., None] * active[:, None, None, :]
    entry = low(block_input * mask_full[..., None])
    pre_one = low_back(pointwise(entry, low(first_reduce)))
    act_one = low(jax.nn.silu(normalize(pre_one, mask_full, member, count_full, first_mid_gain[0], first_mid_bias[0])) * keep_full)
    pre_two = low_back(spatial(act_one, low(first_spatial), 2))
    act_two = low(jax.nn.silu(normalize(pre_two, mask_half, member, count_half, first_mid_gain[1], first_mid_bias[1])) * keep_half)
    pre_three = low_back(pointwise(act_two, low(first_expand)))
    pre_short = low_back(pointwise(entry[:, ::2, ::2, :], low(first_shortcut)))
    sum_one = normalize(pre_three, mask_half, member, count_half, first_wide_gain[0], first_wide_bias[0]) + normalize(pre_short, mask_half, member, count_half, first_wide_gain[1], first_wide_bias[1])
    section_out = jax.nn.silu(sum_one) * mask_half[..., None]
    section_low = low(section_out)
    pre_four = low_back(pointwise(section_low, low(second_reduce)))
    act_four = low(jax.nn.silu(normalize(pre_four, mask_half, member, count_half, second_mid_gain[0], second_mid_bias[0])) * keep_half)
    pre_five = low_back(spatial(act_four, low(second_spatial), 1))
    act_five = low(jax.nn.silu(normalize(pre_five, mask_half, member, count_half, second_mid_gain[1], second_mid_bias[1])) * keep_half)
    pre_six = low_back(pointwise(act_five, low(second_expand)))
    sum_two = normalize(pre_six, mask_half, member, count_half, second_wide_gain, second_wide_bias) + section_out
    return jax.nn.silu(sum_two) * mask_half[..., None]

def reference(block_input, first_reduce, first_spatial, first_expand, first_shortcut, second_reduce, second_spatial, second_expand, first_mid_gain, first_mid_bias, first_wide_gain, first_wide_bias, second_mid_gain, second_mid_bias, second_wide_gain, second_wide_bias, subnet_widths, subnet_ids, crop_sides, cotangent):
    rows_full = jnp.arange(SIDE, dtype=jnp.int32)
    inside_full = (rows_full[None, :] < crop_sides[:, None]).astype(jnp.float32)
    mask_full = inside_full[:, :, None] * inside_full[:, None, :]
    rows_half = jnp.arange(HALF, dtype=jnp.int32)
    half_sides = crop_sides // 2
    inside_half = (rows_half[None, :] < half_sides[:, None]).astype(jnp.float32)
    mask_half = inside_half[:, :, None] * inside_half[:, None, :]
    labels = jnp.arange(SUBNETS, dtype=jnp.int32)
    member = (subnet_ids[None, :] == labels[:, None]).astype(jnp.float32)
    count_full = lax.optimization_barrier(jnp.sum(member * (crop_sides * crop_sides).astype(jnp.float32)[None, :], axis=1))
    count_half = lax.optimization_barrier(jnp.sum(member * (half_sides * half_sides).astype(jnp.float32)[None, :], axis=1))
    crop_width = lax.optimization_barrier(jnp.sum(member * subnet_widths.astype(jnp.float32)[:, None], axis=0))
    channel_index = jnp.arange(MID, dtype=jnp.int32).astype(jnp.float32)
    active = (channel_index[None, :] < crop_width[:, None]).astype(jnp.float32)
    params = (block_input.astype(jnp.float32), first_reduce, first_spatial, first_expand, first_shortcut, second_reduce, second_spatial, second_expand, first_mid_gain, first_mid_bias, first_wide_gain, first_wide_bias, second_mid_gain, second_mid_bias, second_wide_gain, second_wide_bias)

    def wrapped(*values):
        return forward(values, mask_full, mask_half, member, count_full, count_half, active)
    output, pullback = jax.vjp(wrapped, *params)
    grads = pullback(cotangent.astype(jnp.float32))
    return (output, grads[0], grads[1], grads[2], grads[3], grads[4], grads[5], grads[6], grads[7], grads[8], grads[9], grads[10], grads[11], grads[12], grads[13], grads[14], grads[15])
```

```python
import functools

import jax
import jax.numpy as jnp
import numpy as np
from jax import lax
from jax.experimental import pallas as pl
from jax.experimental.pallas import tpu as pltpu
from jax.sharding import PartitionSpec as P

F32, BF16 = jnp.float32, jnp.bfloat16
EPS = 1e-05
SMALL = 6
ALL = ("batch", "chan")


def silu_slope(v):
    s = jax.nn.sigmoid(v)
    return s * (1.0 + v * (1.0 - s))


class Geometry:
    def __init__(self, crops, side):
        self.crops, self.side = crops, side
        self.half, self.small = side // 2, SMALL // 2
        self.images = crops // 8
        self.large_n, self.small_n = 2 * self.images, 6 * self.images
        order = [8 * m + k for m in range(self.images) for k in range(2)]
        order += [8 * m + k for m in range(self.images) for k in range(2, 8)]
        rows = []
        for n, crop in enumerate(order):
            extent = self.half if n < self.large_n else self.small
            rows += [(crop, i, j) for i in range(extent) for j in range(extent)]
        self.rows = np.array(rows, np.int32)
        self.pixels = len(rows)
        where = {tuple(r): n for n, r in enumerate(rows)}
        shifts = np.zeros((9, self.pixels, self.pixels), np.float32)
        for n, (crop, i, j) in enumerate(rows):
            for tap in range(9):
                src = where.get((crop, i + tap // 3 - 1, j + tap % 3 - 1))
                if src is not None:
                    shifts[tap, n, src] = 1.0
        self.shifts = shifts

    def split(self, x):
        x = x.reshape((self.images, 8) + x.shape[1:])
        large = x[:, :2].reshape((self.large_n,) + x.shape[2:])
        small = x[:, 2:].reshape((self.small_n,) + x.shape[2:])
        return large, small

    def pack_full(self, x):
        c = x.shape[-1]
        large, small = self.split(x)
        small = small[:, :SMALL, :SMALL]
        h, s = self.half, self.small
        large = large.reshape(self.large_n, h, 2, h, 2, c).transpose(2, 4, 0, 1, 3, 5)
        small = small.reshape(self.small_n, s, 2, s, 2, c).transpose(2, 4, 0, 1, 3, 5)
        return jnp.concatenate([large.reshape(4, -1, c), small.reshape(4, -1, c)], axis=1)

    def pack_half(self, x):
        c = x.shape[-1]
        large, small = self.split(x)
        small = small[:, : self.small, : self.small]
        return jnp.concatenate([large.reshape(-1, c), small.reshape(-1, c)], axis=0)

    def join(self, large, small):
        tail = large.shape[1:]
        large = large.reshape((self.images, 2) + tail)
        small = small.reshape((self.images, 6) + tail)
        return jnp.concatenate([large, small], axis=1).reshape((self.crops,) + tail)

    def unpack_half(self, x):
        c = x.shape[-1]
        h, s = self.half, self.small
        cut = self.large_n * h * h
        large = x[:cut].reshape(self.large_n, h, h, c)
        small = x[cut:].reshape(self.small_n, s, s, c)
        small = jnp.pad(small, ((0, 0), (0, h - s), (0, h - s), (0, 0)))
        return self.join(large, small)

    def unpack_full(self, x):
        c = x.shape[-1]
        h, s = self.half, self.small
        cut = self.large_n * h * h
        large = x[:, :cut].reshape(2, 2, self.large_n, h, h, c).transpose(2, 3, 0, 4, 1, 5)
        small = x[:, cut:].reshape(2, 2, self.small_n, s, s, c).transpose(2, 3, 0, 4, 1, 5)
        large = large.reshape(self.large_n, 2 * h, 2 * h, c)
        small = small.reshape(self.small_n, 2 * s, 2 * s, c)
        pad = 2 * h - 2 * s
        return self.join(large, jnp.pad(small, ((0, 0), (0, pad), (0, pad), (0, 0))))


def strided_tap(tap):
    r, c = divmod(tap, 3)
    plane = 2 * int(r != 1) + int(c != 1)
    shift = 3 * (0 if r == 0 else 1) + (0 if c == 0 else 1)
    return plane, shift


def unit_tap(tap):
    return 0, tap


VMEM_LIMIT = 56 * 1024 * 1024
PARAMS = pltpu.CompilerParams(vmem_limit_bytes=VMEM_LIMIT)
WHOLE = pl.BlockSpec(memory_space=pltpu.VMEM)


def conv_forward(taps, act, shifts, weight):
    planes, rows, depth = act.shape
    width = weight.shape[2]

    def kernel(act_ref, shift_ref, weight_ref, out_ref, cols_ref):
        total = jnp.zeros((rows, width), F32)
        for tap in range(9):
            plane, shift = taps(tap)
            a = act_ref[plane]
            if shift != 4:
                a = jnp.dot(shift_ref[shift], a, preferred_element_type=F32).astype(BF16)
            cols_ref[tap] = a
            total = total + jnp.dot(a, weight_ref[tap], preferred_element_type=F32)
        out_ref[...] = total

    return pl.pallas_call(
        kernel,
        out_shape=(
            jax.ShapeDtypeStruct((rows, width), F32),
            jax.ShapeDtypeStruct((9, rows, depth), BF16),
        ),
        in_specs=[WHOLE] * 3,
        out_specs=(WHOLE, WHOLE),
        compiler_params=PARAMS,
    )(act, shifts, weight)


def conv_backward(taps, planes, grad, shifts, weight):
    rows = grad.shape[0]
    depth = weight.shape[1]

    def kernel(grad_ref, shift_ref, weight_ref, out_ref):
        for plane in range(planes):
            total = None
            for tap in range(9):
                at, shift = taps(tap)
                if at != plane:
                    continue
                g = grad_ref[...]
                if shift != 4:
                    g = jnp.dot(shift_ref[8 - shift], g, preferred_element_type=F32).astype(BF16)
                part = lax.dot_general(
                    g, weight_ref[tap], (((1,), (1,)), ((), ())), preferred_element_type=F32
                )
                total = part if total is None else total + part
            out_ref[plane] = total.astype(BF16)

    return pl.pallas_call(
        kernel,
        out_shape=jax.ShapeDtypeStruct((planes, rows, depth), BF16),
        in_specs=[WHOLE] * 3,
        out_specs=WHOLE,
        compiler_params=PARAMS,
    )(grad, shifts, weight)


def dot(a, b):
    return jnp.dot(a, b, preferred_element_type=F32)


def dot_nt(a, b):
    return lax.dot_general(a, b, (((1,), (1,)), ((), ())), preferred_element_type=F32)


def dot_tn(a, b):
    return lax.dot_general(a, b, (((0,), (0,)), ((), ())), preferred_element_type=F32)


def local(
    block_input,
    first_reduce,
    first_spatial,
    first_expand,
    first_shortcut,
    second_reduce,
    second_spatial,
    second_expand,
    first_mid_gain,
    first_mid_bias,
    first_wide_gain,
    first_wide_bias,
    second_mid_gain,
    second_mid_bias,
    second_wide_gain,
    second_wide_bias,
    subnet_widths,
    subnet_ids,
    crop_sides,
    cotangent,
):
    nb, nc = lax.axis_size("batch"), lax.axis_size("chan")
    spread = nb // nc
    crops, side = block_input.shape[0], block_input.shape[1]
    geo = Geometry(crops, side)
    px = geo.pixels
    subs = subnet_widths.shape[0]
    me = lax.axis_index("chan")
    mid = first_reduce.shape[1]
    wide = first_shortcut.shape[1]
    part_in = block_input.shape[3]

    def chan_swap(x, r):
        return lax.ppermute(x, "chan", [(i, i ^ r) for i in range(nc)])

    def gather_chan(x, axis=1):
        size = x.shape[axis]
        shape = list(x.shape)
        shape[axis] = size * nc
        out = jnp.zeros(shape, x.dtype)
        for r in range(nc):
            piece = x if r == 0 else chan_swap(x, r)
            out = lax.dynamic_update_slice_in_dim(out, piece, (me ^ r) * size, axis)
        return out

    def scatter_chan(x, axis=1):
        size = x.shape[axis] // nc
        total = None
        for r in range(nc):
            piece = lax.dynamic_slice_in_dim(x, (me ^ r) * size, size, axis)
            if r:
                piece = chan_swap(piece, r)
            piece = piece.astype(F32)
            total = piece if total is None else total + piece
        return total

    def sum_batch(x):
        y = lax.all_to_all(jnp.broadcast_to(x[None], (nb,) + x.shape), "batch", 0, 0, tiled=True)
        return jnp.sum(y, axis=0)

    turn = []
    for zc in range(nc):
        for j in range(spread):
            for c in range(nc):
                turn.append(((zc * spread + j) * nc + c, (c * spread + j) * nc + zc))

    def turn_share(x):
        return lax.ppermute(x, ALL, turn)

    start = lax.axis_index("batch") * crops
    sides = lax.dynamic_slice_in_dim(crop_sides, start, crops)
    ids = lax.dynamic_slice_in_dim(subnet_ids, start, crops)
    labels = jnp.arange(subs, dtype=jnp.int32)
    member_all = (subnet_ids[None, :] == labels[:, None]).astype(F32)
    halves = crop_sides // 2
    count_full = jnp.sum(member_all * (crop_sides * crop_sides).astype(F32)[None, :], axis=1)
    count_half = jnp.sum(member_all * (halves * halves).astype(F32)[None, :], axis=1)
    pick = jnp.asarray(geo.rows[:, 0:1] == np.arange(crops)[None, :])
    side_row = jnp.sum(jnp.where(pick, sides[None, :], 0), axis=1)
    id_row = jnp.sum(jnp.where(pick, ids[None, :], 0), axis=1)
    row_i, row_j = geo.rows[:, 1], geo.rows[:, 2]
    inside_half = (row_i < side_row // 2) & (row_j < side_row // 2)
    own = id_row[:, None] == labels[None, :]
    seg_half = (own & inside_half[:, None]).astype(F32)
    planes = []
    for p in range(2):
        for q in range(2):
            inside = (2 * row_i + p < side_row) & (2 * row_j + q < side_row)
            planes.append((own & inside[:, None]).astype(F32))
    seg_full = jnp.concatenate(planes, axis=0)
    mask_half = jnp.sum(seg_half, axis=1, keepdims=True)
    mask_full = jnp.sum(seg_full, axis=1, keepdims=True)
    channel = (me * mid + jnp.arange(mid, dtype=jnp.int32))[None, :]
    active = (channel < subnet_widths[:, None]).astype(F32)

    def select(seg, table):
        total = seg[:, 0:1] * table[0:1]
        for s in range(1, subs):
            total = total + seg[:, s : s + 1] * table[s : s + 1]
        return total

    def sums(seg, *fields):
        return jnp.concatenate(
            [jnp.sum(f * seg[:, s : s + 1], axis=0, keepdims=True) for f in fields for s in range(subs)],
            axis=0,
        )

    def forward_tables(totals, counts):
        average = totals[:subs] / counts[:, None]
        squares = totals[subs:] / counts[:, None]
        return average, lax.rsqrt(squares - average * average + EPS)

    def normed(v, seg, average, inverse):
        return (v - select(seg, average)) * select(seg, inverse)

    def norm_grad(u, xhat, seg, inverse, gain, gsum, xsum, counts):
        scale = select(seg, gain[None, :] * inverse)
        return scale * (
            u - (select(seg, gsum / counts[:, None]) + xhat * select(seg, xsum / counts[:, None]))
        )

    rows128 = lambda w: jnp.concatenate([w[:, k : k + mid] for k in range(0, w.shape[1], mid)], axis=0)
    r1, s1, e1, sc, r2, s2, e2 = (
        w.astype(BF16)
        for w in (first_reduce, first_spatial, first_expand, first_shortcut, second_reduce, second_spatial, second_expand)
    )
    s_rows = s1.shape[2]
    e_cols = e1.shape[1]

    def gather_batch(x):
        return lax.all_gather(x, "batch", axis=0, tiled=False)

    group_a = gather_batch(jnp.concatenate([r1, s1.reshape(9 * s_rows, mid)], axis=0))
    r1_w = group_a[:, : r1.shape[0]].reshape(-1, mid)
    s1_w = group_a[:, r1.shape[0] :].reshape(nb, 9, s_rows, mid).transpose(1, 0, 2, 3).reshape(9, nb * s_rows, mid)
    turned = turn_share(
        jnp.concatenate([jnp.swapaxes(e1, 0, 1), r2, jnp.swapaxes(e2, 0, 1)], axis=0)
    )
    t_e1, t_r2, t_e2 = turned[:e_cols], turned[e_cols : e_cols + r2.shape[0]], turned[e_cols + r2.shape[0] :]
    group_b = gather_batch(jnp.concatenate([t_e1, t_r2, rows128(sc)], axis=0))
    group_c = gather_batch(jnp.concatenate([s2.reshape(9 * s_rows, mid), t_e2], axis=0))

    def expand_weight(x):
        return x.reshape(nc, spread, e_cols, mid).transpose(1, 2, 0, 3).reshape(spread * e_cols, nc * mid)

    e1_t = expand_weight(group_b[:, :e_cols])
    r2_w = group_b[:, e_cols : e_cols + r2.shape[0]].reshape(nc, wide, mid).transpose(1, 0, 2).reshape(wide, nc * mid)
    sc_part = group_b[:, e_cols + r2.shape[0] :]
    sc_w = sc_part.reshape(nb, wide // mid, -1, mid).transpose(0, 2, 1, 3).reshape(-1, wide)
    s2_w = group_c[:, : 9 * s_rows].reshape(nb, 9, s_rows, mid).transpose(1, 0, 2, 3).reshape(9, nb * s_rows, mid)
    e2_t = expand_weight(group_c[:, 9 * s_rows :])

    shifts = jnp.asarray(geo.shifts, BF16)

    entry = geo.pack_full(block_input).reshape(4 * px, part_in)
    entry = jnp.where(mask_full > 0, entry, jnp.zeros_like(entry))
    whole_entry = gather_chan(entry)
    pre_one = dot(whole_entry, r1_w)
    avg_one, inv_one = forward_tables(sum_batch(sums(seg_full, pre_one, pre_one * pre_one)), count_full)
    xhat_one = normed(pre_one, seg_full, avg_one, inv_one)
    norm_one = first_mid_gain[0] * xhat_one + first_mid_bias[0]
    keep_full = select(seg_full, active)
    act_one = (jax.nn.silu(norm_one) * keep_full).astype(BF16)
    slope_one = silu_slope(norm_one) * keep_full
    whole_one = gather_chan(act_one).reshape(4, px, -1)
    pre_two, cols_one = conv_forward(strided_tap, whole_one, shifts, s1_w)

    short_in = whole_entry[:px]
    pre_short = dot(short_in, sc_w)

    keep_half = select(seg_half, active)

    def mid_forward(pre, gain, bias):
        avg, inv = forward_tables(sum_batch(sums(seg_half, pre, pre * pre)), count_half)
        xhat = normed(pre, seg_half, avg, inv)
        norm = gain * xhat + bias
        act = (jax.nn.silu(norm) * keep_half).astype(BF16)
        return act, xhat, inv, silu_slope(norm) * keep_half

    act_two, xhat_two, inv_two, slope_two = mid_forward(pre_two, first_mid_gain[1], first_mid_bias[1])
    whole_two = gather_chan(act_two)
    pre_three = dot_nt(whole_two, e1_t)
    tot_wide = sum_batch(
        sums(seg_half, pre_three, pre_three * pre_three, pre_short, pre_short * pre_short)
    )
    avg_three, inv_three = forward_tables(tot_wide[: 2 * subs], count_half)
    avg_short, inv_short = forward_tables(tot_wide[2 * subs :], count_half)
    xhat_three = normed(pre_three, seg_half, avg_three, inv_three)
    xhat_short = normed(pre_short, seg_half, avg_short, inv_short)
    sum_one = (
        first_wide_gain[0] * xhat_three
        + first_wide_bias[0]
        + first_wide_gain[1] * xhat_short
        + first_wide_bias[1]
    )
    section_out = jax.nn.silu(sum_one) * mask_half
    slope_section = silu_slope(sum_one) * mask_half
    section_low = section_out.astype(BF16)

    pre_four = scatter_chan(dot(section_low, r2_w).astype(BF16))
    act_four, xhat_four, inv_four, slope_four = mid_forward(pre_four, second_mid_gain[0], second_mid_bias[0])
    pre_five, cols_four = conv_forward(unit_tap, gather_chan(act_four)[None], shifts, s2_w)
    act_five, xhat_five, inv_five, slope_five = mid_forward(pre_five, second_mid_gain[1], second_mid_bias[1])
    whole_five = gather_chan(act_five)
    pre_six = dot_nt(whole_five, e2_t)
    avg_six, inv_six = forward_tables(sum_batch(sums(seg_half, pre_six, pre_six * pre_six)), count_half)
    xhat_six = normed(pre_six, seg_half, avg_six, inv_six)
    sum_two = second_wide_gain * xhat_six + second_wide_bias + section_out
    output = geo.unpack_half(jax.nn.silu(sum_two) * mask_half)

    grad_final = geo.pack_half(cotangent).astype(F32) * mask_half * silu_slope(sum_two)

    def backward(u, xhat, seg, inv, gain, counts):
        totals = sum_batch(sums(seg, u, u * xhat))
        gsum, xsum = totals[:subs], totals[subs:]
        grad = norm_grad(u, xhat, seg, inv, gain, gsum, xsum, counts).astype(BF16)
        return grad, jnp.sum(xsum, axis=0), jnp.sum(gsum, axis=0)

    grad_six, wide_two_gain, wide_two_bias = backward(
        grad_final, xhat_six, seg_half, inv_six, second_wide_gain, count_half
    )
    u_five = scatter_chan(dot(grad_six, e2_t).astype(BF16)) * slope_five
    e2_grad = dot_tn(grad_six, whole_five).astype(BF16)
    grad_five, mid_five_gain, mid_five_bias = backward(
        u_five, xhat_five, seg_half, inv_five, second_mid_gain[1], count_half
    )
    back_four = scatter_chan(conv_backward(unit_tap, 1, grad_five, shifts, s2_w)[0])
    s2_grad = lax.dot_general(
        cols_four, grad_five, (((1,), (0,)), ((), ())), preferred_element_type=F32
    ).astype(BF16)
    grad_four, mid_four_gain, mid_four_bias = backward(
        back_four * slope_four, xhat_four, seg_half, inv_four, second_mid_gain[0], count_half
    )
    whole_grad_four = gather_chan(grad_four)
    back_section = dot_nt(whole_grad_four, r2_w) + grad_final
    r2_grad = dot_tn(section_low, whole_grad_four).astype(BF16)

    u_wide = back_section * slope_section
    tot_back = sum_batch(sums(seg_half, u_wide, u_wide * xhat_three, u_wide * xhat_short))
    gsum_wide, xsum_three, xsum_short = tot_back[:subs], tot_back[subs : 2 * subs], tot_back[2 * subs :]
    grad_three = norm_grad(
        u_wide, xhat_three, seg_half, inv_three, first_wide_gain[0], gsum_wide, xsum_three, count_half
    ).astype(BF16)
    grad_short = norm_grad(
        u_wide, xhat_short, seg_half, inv_short, first_wide_gain[1], gsum_wide, xsum_short, count_half
    ).astype(BF16)
    wide_one_bias = jnp.sum(gsum_wide, axis=0)
    back_two = scatter_chan(dot(grad_three, e1_t).astype(BF16))
    e1_grad = dot_tn(grad_three, whole_two).astype(BF16)
    sc_grad = dot_tn(short_in, grad_short).astype(BF16)
    from_short = dot_nt(grad_short, sc_w)
    grad_two, mid_two_gain, mid_two_bias = backward(
        back_two * slope_two, xhat_two, seg_half, inv_two, first_mid_gain[1], count_half
    )
    back_one = scatter_chan(
        conv_backward(strided_tap, 4, grad_two, shifts, s1_w).reshape(4 * px, nc * mid)
    )
    s1_grad = lax.dot_general(
        cols_one, grad_two, (((1,), (0,)), ((), ())), preferred_element_type=F32
    ).astype(BF16)
    grad_one, mid_one_gain, mid_one_bias = backward(
        back_one * slope_one, xhat_one, seg_full, inv_one, first_mid_gain[0], count_full
    )
    r1_grad = dot_tn(whole_entry, grad_one).astype(BF16)
    from_reduce = dot_nt(grad_one, r1_w)
    from_reduce = jnp.concatenate([from_reduce[:px] + from_short, from_reduce[px:]], axis=0)
    input_grad = geo.unpack_full(
        (scatter_chan(from_reduce.astype(BF16)) * mask_full).reshape(4, px, part_in)
    )

    def to_owners(*parts):
        cat = jnp.concatenate(parts, axis=1)
        out = lax.psum_scatter(cat, "batch", scatter_dimension=0, tiled=False)
        cuts = np.cumsum([p.shape[1] for p in parts])[:-1]
        return jnp.split(out, cuts, axis=0)

    def expand_shares(g):
        return g.reshape(spread, e_cols, nc, mid).transpose(2, 0, 1, 3).reshape(nb, e_cols, mid)

    def spatial_shares(g):
        return g.reshape(9, nb, s_rows, mid).transpose(1, 0, 2, 3).reshape(nb, 9 * s_rows, mid)

    r2_shares = r2_grad.reshape(wide, nc, mid).transpose(1, 0, 2).reshape(nb, wide // spread, mid)
    sc_shares = sc_grad.reshape(nb, -1, wide // mid, mid).transpose(0, 2, 1, 3).reshape(nb, -1, mid)
    e2_out, s2_out, r2_out = to_owners(expand_shares(e2_grad), spatial_shares(s2_grad), r2_shares)
    e1_out, sc_out = to_owners(expand_shares(e1_grad), sc_shares)
    s1_out, r1_out = to_owners(spatial_shares(s1_grad), r1_grad.reshape(nb, -1, mid))
    back = turn_share(jnp.concatenate([e1_out, r2_out, e2_out], axis=0)).astype(F32)
    e1_own, r2_own, e2_own = jnp.split(back, [e_cols, e_cols + r2.shape[0]], axis=0)
    sc_own = sc_out.astype(F32).reshape(wide // mid, -1, mid).transpose(1, 0, 2).reshape(-1, wide)
    return (
        output,
        input_grad,
        r1_out.astype(F32),
        s1_out.astype(F32).reshape(3, 3, s_rows, mid),
        e1_own.T,
        sc_own,
        r2_own,
        s2_out.astype(F32).reshape(3, 3, s_rows, mid),
        e2_own.T,
        jnp.stack([mid_one_gain, mid_two_gain]),
        jnp.stack([mid_one_bias, mid_two_bias]),
        jnp.stack([jnp.sum(xsum_three, axis=0), jnp.sum(xsum_short, axis=0)]),
        jnp.stack([wide_one_bias, wide_one_bias]),
        jnp.stack([mid_four_gain, mid_five_gain]),
        jnp.stack([mid_four_bias, mid_five_bias]),
        wide_two_gain,
        wide_two_bias,
    )


def solution(mesh):
    placed = (
        P("batch", None, None, "chan"),
        P("batch", "chan"),
        P(None, None, "batch", "chan"),
        P("chan", "batch"),
        P("batch", "chan"),
        P("batch", "chan"),
        P(None, None, "batch", "chan"),
        P("chan", "batch"),
        P(None, "chan"),
        P(None, "chan"),
        P(None, "chan"),
        P(None, "chan"),
        P(None, "chan"),
        P(None, "chan"),
        P("chan"),
        P("chan"),
        P(),
        P(),
        P(),
        P("batch", None, None, "chan"),
    )
    outs = (
        P("batch", None, None, "chan"),
        P("batch", None, None, "chan"),
        P("batch", "chan"),
        P(None, None, "batch", "chan"),
        P("chan", "batch"),
        P("batch", "chan"),
        P("batch", "chan"),
        P(None, None, "batch", "chan"),
        P("chan", "batch"),
        P(None, "chan"),
        P(None, "chan"),
        P(None, "chan"),
        P(None, "chan"),
        P(None, "chan"),
        P(None, "chan"),
        P("chan"),
        P("chan"),
    )
    return jax.shard_map(local, mesh=mesh, in_specs=placed, out_specs=outs, check_vma=False)
```

```python
import jax
import jax.numpy as jnp
import numpy as np
from jax import lax
from jax.experimental import pallas as pl
from jax.experimental.pallas import tpu as pltpu
from jax.sharding import PartitionSpec as P

F32, BF16 = jnp.float32, jnp.bfloat16
EPS = 1e-05
SMALL = 6
LANES = 128
ALL = ("batch", "chan")


class Geometry:
    def __init__(self, crops, side):
        self.crops, self.side = crops, side
        self.half, self.small = side // 2, SMALL // 2
        self.images = crops // 8
        self.large_n, self.small_n = 2 * self.images, 6 * self.images
        order = [8 * m + k for m in range(self.images) for k in range(2)]
        order += [8 * m + k for m in range(self.images) for k in range(2, 8)]
        rows = []
        for n, crop in enumerate(order):
            extent = self.half if n < self.large_n else self.small
            rows += [(crop, i, j) for i in range(extent) for j in range(extent)]
        self.rows = np.array(rows, np.int32)
        self.pixels = len(rows)
        where = {tuple(r): n for n, r in enumerate(rows)}
        source = np.full((self.pixels, 16), -1, np.int32)
        for n, (crop, i, j) in enumerate(rows):
            for shift in range(9):
                source[n, shift] = where.get((crop, i + shift // 3 - 1, j + shift % 3 - 1), -1)
        self.source = source

    def split(self, x):
        x = x.reshape((self.images, 8) + x.shape[1:])
        large = x[:, :2].reshape((self.large_n,) + x.shape[2:])
        small = x[:, 2:].reshape((self.small_n,) + x.shape[2:])
        return large, small

    def pack_full(self, x):
        c = x.shape[-1]
        large, small = self.split(x)
        small = small[:, :SMALL, :SMALL]
        h, s = self.half, self.small
        large = large.reshape(self.large_n, h, 2, h, 2, c).transpose(2, 4, 0, 1, 3, 5)
        small = small.reshape(self.small_n, s, 2, s, 2, c).transpose(2, 4, 0, 1, 3, 5)
        return jnp.concatenate([large.reshape(4, -1, c), small.reshape(4, -1, c)], axis=1)

    def pack_half(self, x):
        c = x.shape[-1]
        large, small = self.split(x)
        small = small[:, : self.small, : self.small]
        return jnp.concatenate([large.reshape(-1, c), small.reshape(-1, c)], axis=0)

    def join(self, large, small):
        tail = large.shape[1:]
        large = large.reshape((self.images, 2) + tail)
        small = small.reshape((self.images, 6) + tail)
        return jnp.concatenate([large, small], axis=1).reshape((self.crops,) + tail)

    def unpack_half(self, x):
        c = x.shape[-1]
        h, s = self.half, self.small
        cut = self.large_n * h * h
        large = x[:cut].reshape(self.large_n, h, h, c)
        small = x[cut:].reshape(self.small_n, s, s, c)
        small = jnp.pad(small, ((0, 0), (0, h - s), (0, h - s), (0, 0)))
        return self.join(large, small)

    def unpack_full(self, x):
        c = x.shape[-1]
        h, s = self.half, self.small
        cut = self.large_n * h * h
        large = x[:, :cut].reshape(2, 2, self.large_n, h, h, c).transpose(2, 3, 0, 4, 1, 5)
        small = x[:, cut:].reshape(2, 2, self.small_n, s, s, c).transpose(2, 3, 0, 4, 1, 5)
        large = large.reshape(self.large_n, 2 * h, 2 * h, c)
        small = small.reshape(self.small_n, 2 * s, 2 * s, c)
        pad = 2 * h - 2 * s
        return self.join(large, jnp.pad(small, ((0, 0), (0, pad), (0, pad), (0, 0))))


UNIT_TAPS = [(0, tap) for tap in range(9)]
STRIDED_TAPS = [
    (2 * int(r != 1) + int(c != 1), 3 * (0 if r == 0 else 1) + (0 if c == 0 else 1))
    for r in range(3)
    for c in range(3)
]
STRIDED_ORDER = [tap for plane in range(4) for tap in range(9) if STRIDED_TAPS[tap][0] == plane]

SM = pl.BlockSpec(memory_space=pltpu.SMEM)


def struct(shape, dtype=F32):
    return jax.ShapeDtypeStruct(tuple(shape), dtype)


def whole_block(shape):
    zeros = (0,) * len(shape)
    return pl.BlockSpec(tuple(shape), lambda _: zeros)


def call(kernel, outs, place, *args, flops=10**8, mib=60):
    moved = sum(a.size * a.dtype.itemsize for a in args)
    moved += sum(int(np.prod(o.shape)) * o.dtype.itemsize for o in outs)
    return pl.pallas_call(
        kernel,
        grid=(1,),
        out_shape=tuple(outs),
        in_specs=[SM] + [whole_block(a.shape) for a in args],
        out_specs=tuple(whole_block(o.shape) for o in outs),
        compiler_params=pltpu.CompilerParams(vmem_limit_bytes=mib * 1024 * 1024),
        cost_estimate=pl.CostEstimate(flops=flops, bytes_accessed=moved, transcendentals=0),
    )(place, *args)


def dot(a, b):
    return jnp.dot(a, b, preferred_element_type=F32)


def dot_nt(a, b):
    return lax.dot_general(a, b, (((1,), (1,)), ((), ())), preferred_element_type=F32)


def dot_tn(a, b):
    return lax.dot_general(a, b, (((0,), (0,)), ((), ())), preferred_element_type=F32)


def columns_of(seg, subs):
    return [jnp.broadcast_to(seg[:, s : s + 1], (seg.shape[0], LANES)) for s in range(subs)]


def select(seg, rows):
    total = seg[0] * rows[0]
    for s in range(1, len(rows)):
        total = total + seg[s] * rows[s]
    return total


def sums(seg, field):
    return [jnp.sum(field * g, axis=0, keepdims=True) for g in seg]


def moments(total, count, subs):
    average = [total[s] / count[s] for s in range(subs)]
    inverse = [
        lax.rsqrt(total[subs + s] / count[s] - average[s] * average[s] + EPS) for s in range(subs)
    ]
    return average, inverse


def silu_and_slope(norm):
    sigmoid = jax.nn.sigmoid(norm)
    return norm * sigmoid, sigmoid * (1.0 + norm * (1.0 - sigmoid))


def shifted(source, shift, value):
    if shift == 4:
        return value
    rows = value.shape[0]
    at = lax.broadcasted_iota(jnp.int32, (rows, rows), 1)
    move = jnp.where(at == source[:, shift : shift + 1], 1.0, 0.0).astype(BF16)
    return dot(move, value).astype(BF16)


def put_rows(ref, at, rows):
    for n, row in enumerate(rows):
        ref[at, n : n + 1, :] = row


def spread_rows(ref, lanes, rows):
    ref[0, :, lanes] = jnp.zeros((ref.shape[1], LANES), F32)
    for n, row in enumerate(rows):
        ref[0, n : n + 1, lanes] = row
    block = ref[0, :, lanes]
    for b in range(1, ref.shape[0]):
        ref[b, :, lanes] = block


def block_lanes(k):
    return slice(k * LANES, (k + 1) * LANES)


def row_list(block, first, count):
    return [block[n : n + 1] for n in range(first, first + count)]


def local(
    block_input,
    first_reduce,
    first_spatial,
    first_expand,
    first_shortcut,
    second_reduce,
    second_spatial,
    second_expand,
    first_mid_gain,
    first_mid_bias,
    first_wide_gain,
    first_wide_bias,
    second_mid_gain,
    second_mid_bias,
    second_wide_gain,
    second_wide_bias,
    subnet_widths,
    subnet_ids,
    crop_sides,
    cotangent,
):
    nb, nc = lax.axis_size("batch"), lax.axis_size("chan")
    spread = nb // nc
    crops, side = block_input.shape[0], block_input.shape[1]
    geo = Geometry(crops, side)
    px = geo.pixels
    subs = subnet_widths.shape[0]
    me, ber = lax.axis_index("chan"), lax.axis_index("batch")
    mid = first_reduce.shape[1]
    wide = first_shortcut.shape[1]
    part_in = block_input.shape[3]
    whole_mid = nc * mid
    wide_blocks = wide // LANES

    def chan_swap(x, r):
        return lax.ppermute(x, "chan", [(i, i ^ r) for i in range(nc)])

    def slots_of(x):
        return [x] + [chan_swap(x, r) for r in range(1, nc)]

    def swap_slots(x):
        return [x[0]] + [chan_swap(x[r], r) for r in range(1, nc)]

    def gather_chan(x, axis=1):
        size = x.shape[axis]
        shape = list(x.shape)
        shape[axis] = size * nc
        out = jnp.zeros(shape, x.dtype)
        for r, piece in enumerate(slots_of(x)):
            out = lax.dynamic_update_slice_in_dim(out, piece, (me ^ r) * size, axis)
        return out

    def scatter_chan(x, axis=1):
        size = x.shape[axis] // nc
        total = None
        for r in range(nc):
            piece = lax.dynamic_slice_in_dim(x, (me ^ r) * size, size, axis)
            if r:
                piece = chan_swap(piece, r)
            piece = piece.astype(F32)
            total = piece if total is None else total + piece
        return total

    def to_batch(x):
        return lax.all_to_all(x, "batch", 0, 0, tiled=True)

    def to_all(x):
        return lax.all_to_all(x, ALL, 0, 0, tiled=True)

    turn = []
    for zc in range(nc):
        for j in range(spread):
            for c in range(nc):
                turn.append(((zc * spread + j) * nc + c, (c * spread + j) * nc + zc))

    def turn_share(x):
        return lax.ppermute(x, ALL, turn)

    def batch_bits():
        bits, m = [], 1
        while m < nb:
            bits.append(m)
            m *= 2
        return bits

    def gather_by_doubling(x):
        x = x[None]
        for m in reversed(batch_bits()):
            x = jnp.concatenate([x, lax.ppermute(x, "batch", [(i, i ^ m) for i in range(nb)])], axis=0)
        return x

    def doubling_order():
        bits = list(reversed(batch_bits()))
        held = [sum(m for n, m in enumerate(bits) if s >> n & 1) for s in range(nb)]
        return jnp.asarray(np.argsort(held), jnp.int32)[ber ^ jnp.arange(nb)]

    def scatter_by_halving(x):
        for m in batch_bits():
            pairs = x.reshape((-1, 2) + x.shape[1:])
            bit = (ber // m) % 2
            keep = lax.dynamic_index_in_dim(pairs, bit, 1, False)
            send = lax.dynamic_index_in_dim(pairs, 1 - bit, 1, False)
            got = lax.ppermute(send, "batch", [(i, i ^ m) for i in range(nb)])
            x = keep.astype(F32) + got.astype(F32)
            if m * 2 < nb:
                x = x.astype(BF16)
        return x[0]

    rows_of = lambda w: jnp.concatenate([w[:, k : k + LANES] for k in range(0, w.shape[1], LANES)], axis=0)
    r1, s1, e1, sc, r2, s2, e2 = (
        w.astype(BF16)
        for w in (first_reduce, first_spatial, first_expand, first_shortcut, second_reduce, second_spatial, second_expand)
    )
    s_rows, e_cols, r2_rows = s1.shape[2], e1.shape[1], r2.shape[0]

    def gather_batch(x):
        return lax.all_gather(x, "batch", axis=0, tiled=False)

    pieces = nb if s_rows % 16 == 0 else nc
    per = pieces // nc

    def spatial_weight(x):
        x = x.reshape(nb, 9, s_rows, mid)
        if pieces == nb:
            return x
        return x.reshape(nc, spread, 9, s_rows, mid).transpose(0, 2, 1, 3, 4).reshape(nc, 9, mid, mid)

    r1_w = to_batch(jnp.broadcast_to(r1[None], (nb,) + r1.shape)).reshape(-1, mid)
    turned = turn_share(jnp.concatenate([jnp.swapaxes(e1, 0, 1), r2, jnp.swapaxes(e2, 0, 1)], axis=0))
    t_e1, t_r2, t_e2 = turned[:e_cols], turned[e_cols : e_cols + r2_rows], turned[e_cols + r2_rows :]
    s1_got, order = gather_by_doubling(s1.reshape(9 * s_rows, mid)), doubling_order()
    if pieces != nb:
        s1_got, order = s1_got[order], jnp.arange(nb)
    s1_w = spatial_weight(s1_got)
    place = jnp.concatenate([jnp.stack([me, ber]), order]).astype(jnp.int32)
    group_b = gather_batch(jnp.concatenate([t_e1, t_r2, rows_of(sc)], axis=0))
    group_c = gather_batch(jnp.concatenate([s2.reshape(9 * s_rows, mid), t_e2], axis=0))
    e1_w = group_b[:, :e_cols].reshape(nc, wide, mid)
    r2_w = group_b[:, e_cols : e_cols + r2_rows].reshape(nc, wide, mid)
    sc_w = group_b[:, e_cols + r2_rows :].reshape(nb, wide_blocks, -1, LANES).transpose(0, 2, 1, 3).reshape(-1, wide)
    s2_w = spatial_weight(group_c[:, : 9 * s_rows])
    e2_w = group_c[:, 9 * s_rows :].reshape(nc, wide, mid)

    start = ber * crops
    sides = lax.dynamic_slice_in_dim(crop_sides, start, crops)
    ids = lax.dynamic_slice_in_dim(subnet_ids, start, crops)
    labels = jnp.arange(8, dtype=jnp.int32)
    member_all = (subnet_ids[None, :] == labels[:subs, None]).astype(F32)
    halves = crop_sides // 2
    count_full = jnp.sum(member_all * (crop_sides * crop_sides).astype(F32)[None, :], axis=1)
    count_half = jnp.sum(member_all * (halves * halves).astype(F32)[None, :], axis=1)
    counts = jnp.broadcast_to(
        jnp.concatenate([count_half, count_full, jnp.ones((8 - 2 * subs,), F32)])[:, None], (8, LANES)
    )
    pick = jnp.asarray(geo.rows[:, 0:1] == np.arange(crops)[None, :])
    side_row = jnp.sum(jnp.where(pick, sides[None, :], 0), axis=1, keepdims=True)
    id_row = jnp.sum(jnp.where(pick, ids[None, :], 0), axis=1, keepdims=True)
    row_i, row_j = jnp.asarray(geo.rows[:, 1:2]), jnp.asarray(geo.rows[:, 2:3])
    own = id_row == labels[None, :]
    seg_half = (own & (row_i < side_row // 2) & (row_j < side_row // 2)).astype(F32)
    seg_full = jnp.stack(
        [
            (own & (2 * row_i + p < side_row) & (2 * row_j + q < side_row)).astype(F32)
            for p in range(2)
            for q in range(2)
        ]
    )
    mask_full = jnp.sum(seg_full, axis=2, keepdims=True)
    channel = jnp.arange(whole_mid, dtype=jnp.int32).reshape(nc, 1, mid)
    limits = jnp.concatenate([subnet_widths, jnp.zeros((8 - subs,), jnp.int32)])
    active = (channel < limits[None, :, None]).astype(F32)
    source = jnp.asarray(geo.source)
    own_params = jnp.concatenate([first_mid_gain, first_mid_bias, second_mid_gain, second_mid_bias], axis=0)
    params = jnp.stack(slots_of(own_params))

    def norm_slots(p_ref, raw, st_ref, par_ref, active_ref, seg, count, which, put, keep_own):
        block, layer = which
        chan = p_ref[0]
        for r in range(nc):
            ch = chan ^ r
            total = st_ref[ch]
            for b in range(1, nb):
                total = total + st_ref[b * nc + ch]
            average, inverse = moments(row_list(total, 0, 2 * subs), count, subs)
            gain = par_ref[r, 4 * block + layer : 4 * block + layer + 1, :]
            bias = par_ref[r, 4 * block + 2 + layer : 4 * block + 3 + layer, :]
            act_rows = row_list(active_ref[ch], 0, subs)
            xhat = (raw(r).astype(F32) - select(seg, average)) * select(seg, inverse)
            keep = select(seg, act_rows)
            value, slope = silu_and_slope(gain * xhat + bias)
            put(r, (value * keep).astype(BF16))
            if r == 0:
                keep_own(xhat, slope * keep, inverse)

    def send_sums(st_ref, seg, raw):
        value = raw.astype(F32)
        spread_rows(st_ref, slice(0, LANES), sums(seg, value) + sums(seg, value * value))

    every = nb * nc

    def joined(ref, *at):
        return jnp.concatenate([ref[(*at, r)] for r in range(nc)], axis=1)

    def joined_weight(p_ref, ref):
        return jnp.concatenate([ref[p_ref[0] ^ r] for r in range(nc)], axis=1)

    def tap_weight(p_ref, ref, tap, ordered):
        parts = []
        for r in range(nc):
            for j in range(per):
                at = (p_ref[0] ^ r) * per + j
                parts.append(ref[p_ref[2 + at] if ordered else at, tap])
        return jnp.concatenate(parts, axis=0)

    def reduce_kernel(p_ref, entry_ref, w_ref, seg_ref, raw_ref, st_ref):
        w = w_ref[...]
        rows = [jnp.zeros((1, LANES), F32)] * (2 * subs)
        for k in range(4):
            raw = dot(entry_ref[k], w).astype(BF16)
            raw_ref[k] = raw
            value = raw.astype(F32)
            seg = columns_of(seg_ref[k], subs)
            new = sums(seg, value) + sums(seg, value * value)
            rows = [a + b for a, b in zip(rows, new)]
        spread_rows(st_ref, slice(0, LANES), rows)

    def spatial_one_kernel(
        p_ref, r0, r1_, r2_, r3, st_ref, par_ref, act_ref, segf_ref, segh_ref, cnt_ref, src_ref, w_ref,
        out_ref, xhat_ref, slope_ref, inv_ref, raw_ref, sto_ref,
    ):
        refs = (r0, r1_, r2_, r3)
        count = row_list(cnt_ref[...], subs, subs)
        for k in range(4):
            seg = columns_of(segf_ref[k], subs)

            def put(r, value):
                out_ref[k, r] = value

            def keep_own(xhat, slope, inverse):
                xhat_ref[k] = xhat
                slope_ref[k] = slope
                if k == 0:
                    for n, row in enumerate(inverse):
                        inv_ref[n : n + 1, :] = row

            norm_slots(
                p_ref, lambda r: refs[r][k], st_ref, par_ref, act_ref, seg, count, (0, 0), put, keep_own
            )
        src = src_ref[...]
        total = jnp.zeros((px, mid), F32)
        for tap in range(9):
            plane, shift = STRIDED_TAPS[tap]
            total = total + dot(shifted(src, shift, joined(out_ref, plane)), tap_weight(p_ref, w_ref, tap, True))
        raw = total.astype(BF16)
        raw_ref[...] = raw
        send_sums(sto_ref, columns_of(segh_ref[...], subs), raw)

    def mid_inputs(raws, st):
        return (*raws, st, params, active, seg_half, counts)

    def mid_outs():
        return (
            struct((nc, px, mid), BF16),
            struct((px, mid)),
            struct((px, mid)),
            struct((8, mid)),
        )

    def mid_part(which, p_ref, refs, st_ref, par_ref, act_ref, segh_ref, cnt_ref, out_ref, xhat_ref, slope_ref, inv_ref):
        seg = columns_of(segh_ref[...], subs)

        def put(r, value):
            out_ref[r] = value

        def keep_own(xhat, slope, inverse):
            xhat_ref[...] = xhat
            slope_ref[...] = slope
            for n, row in enumerate(inverse):
                inv_ref[n : n + 1, :] = row

        norm_slots(
            p_ref, lambda r: refs[r][...], st_ref, par_ref, act_ref, seg,
            row_list(cnt_ref[...], 0, subs), which, put, keep_own,
        )
        return seg

    def wide_sums(st_ref, seg, fields):
        for k in range(wide_blocks):
            spread_rows(st_ref, block_lanes(k), fields(k))

    def expand_one_kernel(
        p_ref, r0, r1_, r2_, r3, st_ref, par_ref, act_ref, segh_ref, cnt_ref, w_ref, short_ref,
        out_ref, xhat_ref, slope_ref, inv_ref, pre_ref, sto_ref,
    ):
        seg = mid_part(
            (0, 1), p_ref, (r0, r1_, r2_, r3), st_ref, par_ref, act_ref, segh_ref, cnt_ref,
            out_ref, xhat_ref, slope_ref, inv_ref,
        )
        pre_ref[...] = dot_nt(joined(out_ref), joined_weight(p_ref, w_ref))

        def fields(k):
            a, b = pre_ref[:, block_lanes(k)], short_ref[:, block_lanes(k)]
            return sums(seg, a) + sums(seg, a * a) + sums(seg, b) + sums(seg, b * b)

        wide_sums(sto_ref, seg, fields)

    def summed(st_ref, lanes):
        total = st_ref[0, :, lanes]
        for b in range(1, nb):
            total = total + st_ref[b, :, lanes]
        return total

    def to_slots(slot_ref, value):
        for r in range(nc):
            slot_ref[r] = value[:, r * mid : (r + 1) * mid].astype(BF16)

    def section_kernel(
        p_ref, st_ref, three_ref, short_ref, gain_ref, bias_ref, segh_ref, cnt_ref, w_ref,
        xh3_ref, xhs_ref, out_ref, slope_ref, inv_ref, low_ref, slot_ref,
    ):
        seg = columns_of(segh_ref[...], subs)
        mask = seg[0]
        for s in range(1, subs):
            mask = mask + seg[s]
        count = row_list(cnt_ref[...], 0, subs)
        for k in range(wide_blocks):
            ln = block_lanes(k)
            total = summed(st_ref, ln)
            both = None
            for n, (pre, keep) in enumerate(((three_ref, xh3_ref), (short_ref, xhs_ref))):
                average, inverse = moments(row_list(total, 2 * subs * n, 2 * subs), count, subs)
                xhat = (pre[:, ln] - select(seg, average)) * select(seg, inverse)
                keep[:, ln] = xhat
                for s in range(subs):
                    inv_ref[n * subs + s : n * subs + s + 1, ln] = inverse[s]
                norm = gain_ref[n : n + 1, ln] * xhat + bias_ref[n : n + 1, ln]
                both = norm if both is None else both + norm
            value, slope = silu_and_slope(both)
            value = value * mask
            out_ref[:, ln] = value
            slope_ref[:, ln] = slope * mask
            low_ref[:, ln] = value.astype(BF16)
        to_slots(slot_ref, dot(low_ref[...], joined_weight(p_ref, w_ref)))

    def four_kernel(p_ref, s0, s1_, s2_, s3, segh_ref, raw_ref, sto_ref):
        total = s0[...].astype(F32)
        for ref in (s1_, s2_, s3):
            total = total + ref[...].astype(F32)
        raw = total.astype(BF16)
        raw_ref[...] = raw
        send_sums(sto_ref, columns_of(segh_ref[...], subs), raw)

    def spatial_two_kernel(
        p_ref, r0, r1_, r2_, r3, st_ref, par_ref, act_ref, segh_ref, cnt_ref, src_ref, w_ref,
        out_ref, xhat_ref, slope_ref, inv_ref, raw_ref, sto_ref,
    ):
        seg = mid_part(
            (1, 0), p_ref, (r0, r1_, r2_, r3), st_ref, par_ref, act_ref, segh_ref, cnt_ref,
            out_ref, xhat_ref, slope_ref, inv_ref,
        )
        src = src_ref[...]
        total = jnp.zeros((px, mid), F32)
        whole = joined(out_ref)
        for tap in range(9):
            total = total + dot(shifted(src, tap, whole), tap_weight(p_ref, w_ref, tap, False))
        raw = total.astype(BF16)
        raw_ref[...] = raw
        send_sums(sto_ref, seg, raw)

    def expand_two_kernel(
        p_ref, r0, r1_, r2_, r3, st_ref, par_ref, act_ref, segh_ref, cnt_ref, w_ref,
        out_ref, xhat_ref, slope_ref, inv_ref, pre_ref, sto_ref,
    ):
        seg = mid_part(
            (1, 1), p_ref, (r0, r1_, r2_, r3), st_ref, par_ref, act_ref, segh_ref, cnt_ref,
            out_ref, xhat_ref, slope_ref, inv_ref,
        )
        pre_ref[...] = dot_nt(joined(out_ref), joined_weight(p_ref, w_ref))

        def fields(k):
            a = pre_ref[:, block_lanes(k)]
            return sums(seg, a) + sums(seg, a * a)

        wide_sums(sto_ref, seg, fields)

    def final_kernel(
        p_ref, st_ref, pre_ref, section_ref, cot_ref, gain_ref, bias_ref, segh_ref, cnt_ref,
        out_ref, grad_ref, xhat_ref, inv_ref, sto_ref,
    ):
        seg = columns_of(segh_ref[...], subs)
        mask = seg[0]
        for s in range(1, subs):
            mask = mask + seg[s]
        count = row_list(cnt_ref[...], 0, subs)
        for k in range(wide_blocks):
            ln = block_lanes(k)
            average, inverse = moments(row_list(summed(st_ref, ln), 0, 2 * subs), count, subs)
            xhat = (pre_ref[:, ln] - select(seg, average)) * select(seg, inverse)
            xhat_ref[:, ln] = xhat
            for s in range(subs):
                inv_ref[s : s + 1, ln] = inverse[s]
            both = gain_ref[:, ln] * xhat + bias_ref[:, ln] + section_ref[:, ln]
            value, slope = silu_and_slope(both)
            out_ref[:, ln] = value * mask
            grad = cot_ref[:, ln].astype(F32) * mask * slope
            grad_ref[:, ln] = grad
            spread_rows(sto_ref, ln, sums(seg, grad) + sums(seg, grad * xhat))

    def norm_back(total, at, gain, inverse, u, xhat, seg, count):
        g = [total[s : s + 1] / count[s] for s in range(subs)]
        x = [total[at + s : at + s + 1] / count[s] for s in range(subs)]
        scale = select(seg, [gain * row for row in inverse])
        return (scale * (u - (select(seg, g) + xhat * select(seg, x)))).astype(BF16)

    def put_param_grads(ref, ln, total, pairs):
        for n, first in enumerate(pairs):
            row = total[first : first + 1]
            for s in range(1, subs):
                row = row + total[first + s : first + s + 1]
            ref[n : n + 1, ln] = row

    def back_six_kernel(
        p_ref, st_ref, u_ref, xhat_ref, inv_ref, gain_ref, segh_ref, cnt_ref, w_ref, low_ref, par_ref, slot_ref
    ):
        seg = columns_of(segh_ref[...], subs)
        count = row_list(cnt_ref[...], 0, subs)
        for k in range(wide_blocks):
            ln = block_lanes(k)
            total = summed(st_ref, ln)
            put_param_grads(par_ref, ln, total, (subs, 0))
            low_ref[:, ln] = norm_back(
                total, subs, gain_ref[:, ln], row_list(inv_ref[:, ln], 0, subs), u_ref[:, ln], xhat_ref[:, ln], seg, count
            )
        to_slots(slot_ref, dot(low_ref[...], joined_weight(p_ref, w_ref)))

    def upstream_kernel(p_ref, s0, s1_, s2_, s3, slope_ref, xhat_ref, segh_ref, u_ref, sto_ref):
        total = s0[...].astype(F32)
        for ref in (s1_, s2_, s3):
            total = total + ref[...].astype(F32)
        u = total * slope_ref[...]
        u_ref[...] = u
        seg = columns_of(segh_ref[...], subs)
        spread_rows(sto_ref, slice(0, LANES), sums(seg, u) + sums(seg, u * xhat_ref[...]))

    def own_gain(ref, which):
        block, layer = which
        return ref[0, 4 * block + layer : 4 * block + layer + 1, :]

    def back_spatial_kernel(which, taps, order, ordered):
        def kernel(
            p_ref, st_ref, u_ref, xhat_ref, inv_ref, params_ref, segh_ref, cnt_ref, src_ref, w_ref,
            cols_ref, par_ref, slot_ref,
        ):
            seg = columns_of(segh_ref[...], subs)
            count = row_list(cnt_ref[...], 0, subs)
            total = summed(st_ref, slice(0, LANES))
            put_param_grads(par_ref, slice(0, LANES), total, (subs, 0))
            low = norm_back(
                total, subs, own_gain(params_ref, which), row_list(inv_ref[...], 0, subs), u_ref[...], xhat_ref[...], seg, count
            )
            src = src_ref[...]
            part, at = None, None
            for n, tap in enumerate(order):
                plane, shift = taps[tap]
                g = shifted(src, 8 - shift, low)
                cols_ref[:, n * mid : (n + 1) * mid] = g
                new = dot_nt(g, tap_weight(p_ref, w_ref, tap, ordered))
                part = new if plane != at else part + new
                at = plane
                if n == 8 or taps[order[n + 1]][0] != plane:
                    for r in range(nc):
                        slot_ref[r, plane] = part[:, r * mid : (r + 1) * mid].astype(BF16)

        return kernel

    def back_plain_kernel(which):
        def kernel(p_ref, st_ref, u_ref, xhat_ref, inv_ref, params_ref, segh_ref, cnt_ref, low_ref, par_ref):
            seg = columns_of(segh_ref[...], subs)
            count = row_list(cnt_ref[...], 0, subs)
            total = summed(st_ref, slice(0, LANES))
            put_param_grads(par_ref, slice(0, LANES), total, (subs, 0))
            low_ref[...] = norm_back(
                total, subs, own_gain(params_ref, which), row_list(inv_ref[...], 0, subs), u_ref[...], xhat_ref[...], seg, count
            )

        return kernel

    def back_section_kernel(
        p_ref, g0, g1, g2, g3, w_ref, grad_ref, slope_ref, xh3_ref, xhs_ref, segh_ref,
        whole_ref, u_ref, sto_ref,
    ):
        for r, ref in enumerate((g0, g1, g2, g3)):
            whole_ref[r] = ref[...]
        u_ref[...] = dot_nt(joined(whole_ref), joined_weight(p_ref, w_ref))
        seg = columns_of(segh_ref[...], subs)
        for k in range(wide_blocks):
            ln = block_lanes(k)
            u = (u_ref[:, ln] + grad_ref[:, ln]) * slope_ref[:, ln]
            u_ref[:, ln] = u
            spread_rows(
                sto_ref, ln, sums(seg, u) + sums(seg, u * xh3_ref[:, ln]) + sums(seg, u * xhs_ref[:, ln])
            )

    def back_wide_kernel(
        p_ref, st_ref, u_ref, xh3_ref, xhs_ref, inv_ref, gain_ref, segh_ref, cnt_ref, w_ref,
        three_ref, short_ref, par_ref, slot_ref,
    ):
        seg = columns_of(segh_ref[...], subs)
        count = row_list(cnt_ref[...], 0, subs)
        for k in range(wide_blocks):
            ln = block_lanes(k)
            total = summed(st_ref, ln)
            put_param_grads(par_ref, ln, total, (subs, 2 * subs, 0))
            u = u_ref[:, ln]
            inverse = inv_ref[:, ln]
            three_ref[:, ln] = norm_back(
                total, subs, gain_ref[0:1, ln], row_list(inverse, 0, subs), u, xh3_ref[:, ln], seg, count
            )
            short_ref[:, ln] = norm_back(
                total, 2 * subs, gain_ref[1:2, ln], row_list(inverse, subs, subs), u, xhs_ref[:, ln], seg, count
            )
        to_slots(slot_ref, dot(three_ref[...], joined_weight(p_ref, w_ref)))

    def upstream_one_kernel(p_ref, s0, s1_, s2_, s3, slope_ref, xhat_ref, segf_ref, u_ref, sto_ref):
        rows = [jnp.zeros((1, LANES), F32)] * (2 * subs)
        for k in range(4):
            total = s0[k].astype(F32)
            for ref in (s1_, s2_, s3):
                total = total + ref[k].astype(F32)
            u = total * slope_ref[k]
            u_ref[k] = u
            seg = columns_of(segf_ref[k], subs)
            new = sums(seg, u) + sums(seg, u * xhat_ref[k])
            rows = [a + b for a, b in zip(rows, new)]
        spread_rows(sto_ref, slice(0, LANES), rows)

    def back_one_kernel(p_ref, st_ref, u_ref, xhat_ref, inv_ref, params_ref, segf_ref, cnt_ref, low_ref, par_ref):
        count = row_list(cnt_ref[...], subs, subs)
        total = summed(st_ref, slice(0, LANES))
        put_param_grads(par_ref, slice(0, LANES), total, (subs, 0))
        for k in range(4):
            seg = columns_of(segf_ref[k], subs)
            low_ref[k] = norm_back(
                total, subs, own_gain(params_ref, (0, 0)), row_list(inv_ref[...], 0, subs), u_ref[k], xhat_ref[k], seg, count
            )

    st_mid, st_own, st_wide = (
        struct((every, 8, LANES)),
        struct((nb, 8, LANES)),
        struct((nb, 8, wide)),
    )
    matmul = 2 * px * whole_mid * wide

    entry = geo.pack_full(block_input)
    entry = jnp.where(mask_full > 0, entry, jnp.zeros_like(entry)).reshape(4 * px, part_in)
    whole_entry = gather_chan(entry).reshape(4, px, nc * part_in)
    raw_one, st = call(
        reduce_kernel, (struct((4, px, mid), BF16), st_mid), place, whole_entry, r1_w, seg_full, flops=4 * matmul
    )
    raws, st = slots_of(raw_one), to_all(st)
    act_one, xhat_one, slope_one, inv_one, raw_two, st = call(
        spatial_one_kernel,
        (
            struct((4, nc, px, mid), BF16),
            struct((4, px, mid)),
            struct((4, px, mid)),
            struct((8, mid)),
            struct((px, mid), BF16),
            st_mid,
        ),
        place, *raws, st, params, active, seg_full, seg_half, counts, source, s1_w,
        flops=10 * matmul,
    )
    short_in = whole_entry[0]
    pre_short = dot(short_in, sc_w)
    raws, st = slots_of(raw_two), to_all(st)
    act_two, xhat_two, slope_two, inv_two, pre_three, st = call(
        expand_one_kernel,
        (*mid_outs(), struct((px, wide)), struct((nb, 16, wide))),
        place, *mid_inputs(raws, st), e1_w, pre_short,
        flops=2 * matmul,
    )
    xhat_three, xhat_short, section_out, slope_section, inv_wide, section_low, slots = call(
        section_kernel,
        (
            *[struct((px, wide))] * 4,
            struct((8, wide)),
            struct((px, wide), BF16),
            struct((nc, px, mid), BF16),
        ),
        place, to_batch(st), pre_three, pre_short, first_wide_gain, first_wide_bias, seg_half, counts, r2_w,
        flops=2 * matmul,
    )

    raw_four, st = call(
        four_kernel, (struct((px, mid), BF16), st_mid), place, *swap_slots(slots), seg_half
    )
    raws, st = slots_of(raw_four), to_all(st)
    act_four, xhat_four, slope_four, inv_four, raw_five, st = call(
        spatial_two_kernel,
        (*mid_outs(), struct((px, mid), BF16), st_mid),
        place, *mid_inputs(raws, st), source, s2_w,
        flops=8 * matmul,
    )
    raws, st = slots_of(raw_five), to_all(st)
    act_five, xhat_five, slope_five, inv_five, pre_six, st = call(
        expand_two_kernel,
        (*mid_outs(), struct((px, wide)), st_wide),
        place, *mid_inputs(raws, st), e2_w,
        flops=2 * matmul,
    )
    gain_six, bias_six = second_wide_gain[None], second_wide_bias[None]
    out_rows, grad_final, xhat_six, inv_six, st = call(
        final_kernel,
        (*[struct((px, wide))] * 3, struct((8, wide)), st_wide),
        place, to_batch(st), pre_six, section_out, geo.pack_half(cotangent), gain_six, bias_six, seg_half, counts,
    )
    output = geo.unpack_half(out_rows)

    grad_six, par_six, slots = call(
        back_six_kernel,
        (struct((px, wide), BF16), struct((8, wide)), struct((nc, px, mid), BF16)),
        place, to_batch(st), grad_final, xhat_six, inv_six, gain_six, seg_half, counts, e2_w,
        flops=2 * matmul,
    )

    def upstream(slots, slope, xhat):
        return call(
            upstream_kernel, (struct((px, mid)), st_own), place, *swap_slots(slots), slope, xhat, seg_half
        )

    u_five, st = upstream(slots, slope_five, xhat_five)
    cols_five, par_five, slots = call(
        back_spatial_kernel((1, 1), UNIT_TAPS, list(range(9)), False),
        (struct((px, 9 * mid), BF16), struct((8, mid)), struct((nc, 1, px, mid), BF16)),
        place, to_batch(st), u_five, xhat_five, inv_five, params, seg_half, counts, source, s2_w,
        flops=8 * matmul,
    )
    u_four, st = upstream(slots[:, 0], slope_four, xhat_four)
    grad_four, par_four = call(
        back_plain_kernel((1, 0)),
        (struct((px, mid), BF16), struct((8, mid))),
        place, to_batch(st), u_four, xhat_four, inv_four, params, seg_half, counts,
    )
    whole_grad_four, u_wide, st = call(
        back_section_kernel,
        (struct((nc, px, mid), BF16), struct((px, wide)), struct((nb, 16, wide))),
        place, *slots_of(grad_four), r2_w, grad_final, slope_section, xhat_three, xhat_short, seg_half,
        flops=2 * matmul,
    )

    grad_three, grad_short, par_wide, slots = call(
        back_wide_kernel,
        (
            struct((px, wide), BF16),
            struct((px, wide), BF16),
            struct((8, wide)),
            struct((nc, px, mid), BF16),
        ),
        place, to_batch(st), u_wide, xhat_three, xhat_short, inv_wide, first_wide_gain, seg_half, counts, e1_w,
        flops=2 * matmul,
    )
    u_two, st = upstream(slots, slope_two, xhat_two)
    cols_two, par_two, slots = call(
        back_spatial_kernel((0, 1), STRIDED_TAPS, STRIDED_ORDER, True),
        (struct((px, 9 * mid), BF16), struct((8, mid)), struct((nc, 4, px, mid), BF16)),
        place, to_batch(st), u_two, xhat_two, inv_two, params, seg_half, counts, source, s1_w,
        flops=8 * matmul,
    )
    u_one, st = call(
        upstream_one_kernel,
        (struct((4, px, mid)), st_own),
        place, *swap_slots(slots), slope_one, xhat_one, seg_full,
    )
    grad_one, par_one = call(
        back_one_kernel,
        (struct((4, px, mid), BF16), struct((8, mid))),
        place, to_batch(st), u_one, xhat_one, inv_one, params, seg_full, counts,
    )
    grad_one = grad_one.reshape(4 * px, mid)
    from_short = dot_nt(grad_short, sc_w)
    from_reduce = dot_nt(grad_one, r1_w)
    from_reduce = jnp.concatenate([from_reduce[:px] + from_short, from_reduce[px:]], axis=0)
    input_grad = geo.unpack_full(
        scatter_chan(from_reduce.astype(BF16)).reshape(4, px, part_in) * mask_full
    )

    def put_expand(p_ref, out_ref, at, grad_ref, act_ref):
        for k in range(nc):
            got = dot_tn(grad_ref[...], act_ref[p_ref[0] ^ k]).astype(BF16)
            for j in range(spread):
                out_ref[k * spread + j, at : at + e_cols, :] = got[j * e_cols : (j + 1) * e_cols]

    def put_spatial(out_ref, at, k, taps, got):
        for j in range(spread):
            for n, tap in enumerate(taps):
                first = at + tap * s_rows
                out_ref[k * spread + j, first : first + s_rows, :] = got[
                    j * s_rows : (j + 1) * s_rows, n * mid : (n + 1) * mid
                ]

    def grads_two_kernel(p_ref, six_ref, act5_ref, act4_ref, cols_ref, out_ref):
        put_expand(p_ref, out_ref, 0, six_ref, act5_ref)
        for k in range(nc):
            got = dot_tn(act4_ref[p_ref[0] ^ k], cols_ref[...]).astype(BF16)
            put_spatial(out_ref, e_cols, k, range(9), got)

    def grads_mixed_kernel(p_ref, low_ref, four_ref, three_ref, act2_ref, entry_ref, short_ref, out_ref):
        for k in range(nc):
            got = dot_tn(low_ref[...], four_ref[p_ref[0] ^ k]).astype(BF16)
            for j in range(spread):
                out_ref[k * spread + j, 0:r2_rows, :] = got[j * r2_rows : (j + 1) * r2_rows]
        put_expand(p_ref, out_ref, r2_rows, three_ref, act2_ref)
        got = dot_tn(entry_ref[0], short_ref[...]).astype(BF16)
        first = r2_rows + e_cols
        for b in range(nb):
            for k in range(wide_blocks):
                out_ref[b, first + k * in_rows : first + (k + 1) * in_rows, :] = got[
                    b * in_rows : (b + 1) * in_rows, block_lanes(k)
                ]

    def grads_one_kernel(p_ref, act_ref, cols_ref, out_ref):
        for k in range(nc):
            first = 0
            for plane in range(4):
                taps = [t for t in STRIDED_ORDER if STRIDED_TAPS[t][0] == plane]
                lanes = slice(first * mid, (first + len(taps)) * mid)
                got = dot_tn(act_ref[plane, p_ref[0] ^ k], cols_ref[:, lanes]).astype(BF16)
                put_spatial(out_ref, 0, k, taps, got)
                first += len(taps)

    def to_owners(shares, *rows):
        out = lax.psum_scatter(shares, "batch", scatter_dimension=0, tiled=False)
        return jnp.split(out, np.cumsum(rows)[:-1], axis=0)

    in_rows = first_reduce.shape[0]
    (shares,) = call(
        grads_two_kernel, (struct((nb, e_cols + 9 * s_rows, mid), BF16),),
        place, grad_six, act_five, act_four, cols_five, flops=10 * matmul,
    )
    e2_out, s2_out = to_owners(shares, e_cols, 9 * s_rows)
    mixed_rows = (r2_rows, e_cols, wide_blocks * in_rows)
    (shares,) = call(
        grads_mixed_kernel, (struct((nb, sum(mixed_rows), mid), BF16),),
        place, section_low, whole_grad_four, grad_three, act_two, whole_entry, grad_short, flops=8 * matmul,
    )
    r2_out, e1_out, sc_out = to_owners(shares, *mixed_rows)
    (shares,) = call(
        grads_one_kernel, (struct((nb, 9 * s_rows, mid), BF16),), place, act_one, cols_two, flops=8 * matmul
    )
    s1_out = scatter_by_halving(shares).reshape(3, 3, s_rows, mid)
    r1_grad = dot_tn(whole_entry.reshape(4 * px, -1), grad_one).astype(BF16)
    r1_out = jnp.sum(to_batch(r1_grad.reshape(nb, -1, mid)).astype(F32), axis=0)
    back = turn_share(jnp.concatenate([e1_out, r2_out, e2_out], axis=0)).astype(F32)
    e1_own, r2_own, e2_own = jnp.split(back, [e_cols, e_cols + r2_rows], axis=0)
    sc_own = sc_out.astype(F32).reshape(wide_blocks, -1, LANES).transpose(1, 0, 2).reshape(-1, wide)
    return (
        output,
        input_grad,
        r1_out,
        s1_out,
        e1_own.T,
        sc_own,
        r2_own,
        s2_out.astype(F32).reshape(3, 3, s_rows, mid),
        e2_own.T,
        jnp.stack([par_one[0], par_two[0]]),
        jnp.stack([par_one[1], par_two[1]]),
        par_wide[:2],
        jnp.stack([par_wide[2], par_wide[2]]),
        jnp.stack([par_four[0], par_five[0]]),
        jnp.stack([par_four[1], par_five[1]]),
        par_six[0],
        par_six[1],
    )


def solution(mesh):
    placed = (
        P("batch", None, None, "chan"),
        P("batch", "chan"),
        P(None, None, "batch", "chan"),
        P("chan", "batch"),
        P("batch", "chan"),
        P("batch", "chan"),
        P(None, None, "batch", "chan"),
        P("chan", "batch"),
        P(None, "chan"),
        P(None, "chan"),
        P(None, "chan"),
        P(None, "chan"),
        P(None, "chan"),
        P(None, "chan"),
        P("chan"),
        P("chan"),
        P(),
        P(),
        P(),
        P("batch", None, None, "chan"),
    )
    outs = (
        P("batch", None, None, "chan"),
        P("batch", None, None, "chan"),
        P("batch", "chan"),
        P(None, None, "batch", "chan"),
        P("chan", "batch"),
        P("batch", "chan"),
        P("batch", "chan"),
        P(None, None, "batch", "chan"),
        P("chan", "batch"),
        P(None, "chan"),
        P(None, "chan"),
        P(None, "chan"),
        P(None, "chan"),
        P(None, "chan"),
        P(None, "chan"),
        P("chan"),
        P("chan"),
    )
    return jax.shard_map(local, mesh=mesh, in_specs=placed, out_specs=outs, check_vma=False)
```

```python
import jax
import jax.numpy as jnp
import numpy as np
from jax import lax
from jax.experimental import pallas as pl
from jax.experimental.pallas import tpu as pltpu
from jax.sharding import PartitionSpec as P

F32, BF16 = jnp.float32, jnp.bfloat16
EPS = 1e-05
SMALL = 6
LANES = 128
ALL = ("batch", "chan")


class Geometry:
    def __init__(self, crops, side):
        self.crops, self.side = crops, side
        self.half, self.small = side // 2, SMALL // 2
        self.large = [c for c in range(crops) if c % 8 < 2]
        grid = [(i, j) for i in range(self.half) for j in range(self.half)]
        self.common = [at for at in grid if max(at) < self.small]
        self.others = [at for at in grid if max(at) >= self.small]
        rows = [(c, i, j) for i, j in self.common for c in range(crops)]
        rows += [(c, i, j) for i, j in self.others for c in self.large]
        self.cut = len(self.common) * crops
        self.rows = np.array(rows, np.int32)
        self.pixels = len(rows)
        where = {tuple(r): n for n, r in enumerate(rows)}
        source = np.full((self.pixels, 16), -1, np.int32)
        for n, (crop, i, j) in enumerate(rows):
            for shift in range(9):
                source[n, shift] = where.get((crop, i + shift // 3 - 1, j + shift % 3 - 1), -1)
        self.source = source
        self.group = 8
        wanted = len(self.large)
        pick = np.zeros((self.group * wanted, self.group * crops), np.float32)
        for n in range(self.group):
            for m, c in enumerate(self.large):
                pick[n * wanted + m, n * crops + c] = 1.0
        self.pick = pick

    def pack(self, pick, load, store):
        for n, (i, j) in enumerate(self.common):
            store(n * self.crops, load(i, j))
        wanted = len(self.large)
        for n in range(0, len(self.others), self.group):
            rows = jnp.concatenate([load(i, j) for i, j in self.others[n : n + self.group]], axis=0)
            store(self.cut + n * wanted, dot(pick, rows).astype(rows.dtype))

    def unpack(self, load, store):
        for n, (i, j) in enumerate(self.common):
            store(i, j, 0, load(n * self.crops, self.crops))
        wanted = len(self.large)
        for n, (i, j) in enumerate(self.others):
            rows = load(self.cut + n * wanted, wanted)
            store(i, j, 0, jnp.zeros((self.crops, rows.shape[1]), rows.dtype))
            for m in range(0, wanted, 2):
                store(i, j, self.large[m], rows[m : m + 2])


UNIT_TAPS = [(0, tap) for tap in range(9)]
STRIDED_TAPS = [
    (2 * int(r != 1) + int(c != 1), 3 * (0 if r == 0 else 1) + (0 if c == 0 else 1))
    for r in range(3)
    for c in range(3)
]
STRIDED_ORDER = [tap for plane in range(4) for tap in range(9) if STRIDED_TAPS[tap][0] == plane]

SM = pl.BlockSpec(memory_space=pltpu.SMEM)


def struct(shape, dtype=F32):
    return jax.ShapeDtypeStruct(tuple(shape), dtype)


def whole_block(shape, at=None):
    at = at or (0,) * len(shape)
    return pl.BlockSpec(tuple(shape), lambda _: at)


def part(array, shape, at):
    return array, whole_block(shape, at)


def corner(array):
    shape = (1,) * (array.ndim - 2) + (16, LANES) if array.ndim > 1 else array.shape
    return array, whole_block([min(a, b) for a, b in zip(shape, array.shape)], (0,) * array.ndim)


def call(kernel, outs, place, *args, flops=10**8, mib=64, after=()):
    args = [a if isinstance(a, tuple) else (a, whole_block(a.shape)) for a in args]
    moved = sum(int(np.prod([n or 1 for n in b.block_shape])) * a.dtype.itemsize for a, b in args)
    moved += sum(int(np.prod(o.shape)) * o.dtype.itemsize for o in outs)
    used, args = len(args), args + [corner(a) for a in after]

    def body(p_ref, *refs):
        kernel(p_ref, *refs[:used], *refs[len(args) :])

    return pl.pallas_call(
        body,
        grid=(1,),
        out_shape=tuple(outs),
        in_specs=[SM] + [b for _, b in args],
        out_specs=tuple(whole_block(o.shape) for o in outs),
        compiler_params=pltpu.CompilerParams(vmem_limit_bytes=mib * 1024 * 1024),
        cost_estimate=pl.CostEstimate(flops=flops, bytes_accessed=moved, transcendentals=0),
    )(place, *[a for a, _ in args])


def dot(a, b):
    return jnp.dot(a, b, preferred_element_type=F32)


def dot_nt(a, b):
    return lax.dot_general(a, b, (((1,), (1,)), ((), ())), preferred_element_type=F32)


def dot_tn(a, b):
    return lax.dot_general(a, b, (((0,), (0,)), ((), ())), preferred_element_type=F32)


def columns_of(seg, subs):
    return [jnp.broadcast_to(seg[:, s : s + 1], (seg.shape[0], LANES)) for s in range(subs)]


def select(seg, rows):
    total = seg[0] * rows[0]
    for s in range(1, len(rows)):
        total = total + seg[s] * rows[s]
    return total


def mask_of(seg):
    mask = seg[0]
    for other in seg[1:]:
        mask = mask + other
    return mask


def sums(seg, field):
    return [jnp.sum(field * g, axis=0, keepdims=True) for g in seg]


def moments(total, count, subs):
    average = [total[s] / count[s] for s in range(subs)]
    inverse = [
        lax.rsqrt(total[subs + s] / count[s] - average[s] * average[s] + EPS) for s in range(subs)
    ]
    return average, inverse


def silu_and_slope(norm):
    sigmoid = jax.nn.sigmoid(norm)
    return norm * sigmoid, sigmoid * (1.0 + norm * (1.0 - sigmoid))


def shifted(source, shift, value):
    if shift == 4:
        return value
    rows = value.shape[0]
    at = lax.broadcasted_iota(jnp.int32, (rows, rows), 1)
    move = jnp.where(at == source[:, shift : shift + 1], 1.0, 0.0).astype(BF16)
    return dot(move, value).astype(BF16)


def put_sums(ref, rows, first=0):
    for n, row in enumerate(rows):
        ref[0, first + n : first + n + 1, :] = row


def fan_out(ref):
    block = ref[0]
    for b in range(1, ref.shape[0]):
        ref[b] = block


def whole_tiles(rows):
    return -(-rows // 8) * 8


def block_lanes(k):
    return slice(k * LANES, (k + 1) * LANES)


def row_list(block, first, count):
    return [block[n : n + 1] for n in range(first, first + count)]


def local(
    block_input,
    first_reduce,
    first_spatial,
    first_expand,
    first_shortcut,
    second_reduce,
    second_spatial,
    second_expand,
    first_mid_gain,
    first_mid_bias,
    first_wide_gain,
    first_wide_bias,
    second_mid_gain,
    second_mid_bias,
    second_wide_gain,
    second_wide_bias,
    subnet_widths,
    subnet_ids,
    crop_sides,
    cotangent,
):
    nb, nc = lax.axis_size("batch"), lax.axis_size("chan")
    spread = nb // nc
    crops, side = block_input.shape[0], block_input.shape[1]
    geo = Geometry(crops, side)
    px = geo.pixels
    subs = subnet_widths.shape[0]
    me, ber = lax.axis_index("chan"), lax.axis_index("batch")
    mid = first_reduce.shape[1]
    wide = first_shortcut.shape[1]
    part_in = block_input.shape[3]
    whole_mid = nc * mid
    wide_blocks = wide // LANES

    def chan_swap(x, r):
        return lax.ppermute(x, "chan", [(i, i ^ r) for i in range(nc)])

    def slots_of(x):
        return [x] + [chan_swap(x, r) for r in range(1, nc)]

    def swap_slots(x):
        return [x[0]] + [chan_swap(x[r], r) for r in range(1, nc)]

    def to_batch(x):
        return lax.all_to_all(x, "batch", 0, 0, tiled=True)

    def to_all(x):
        return lax.all_to_all(x, ALL, 0, 0, tiled=True)

    turn = []
    for zc in range(nc):
        for j in range(spread):
            for c in range(nc):
                turn.append(((zc * spread + j) * nc + c, (c * spread + j) * nc + zc))

    def turn_share(x):
        return lax.ppermute(x, ALL, turn)

    s_rows, e_cols, r2_rows = first_spatial.shape[2], first_expand.shape[1], second_reduce.shape[0]
    in_rows, part_in = first_reduce.shape[0], block_input.shape[3]

    def prepare_kernel(
        p_ref, x_ref, pick_ref, r1_ref, s1_ref, e1_ref, sc_ref, r2_ref, s2_ref, e2_ref,
        entry_ref, first_out, turn_out, sc_out, s2_out,
    ):
        picked = pick_ref[...]
        for k in range(4):

            def store(first, rows):
                entry_ref[k, first : first + rows.shape[0], :] = rows

            geo.pack(picked, lambda i, j: x_ref[2 * i + k // 2, 2 * j + k % 2], store)
        r1, s1 = r1_ref[...].astype(BF16), s1_ref[...].astype(BF16)
        for b in range(nb):
            first_out[b, 0:in_rows] = r1
            first_out[b, in_rows:] = s1
        s2_out[...] = s2_ref[...].astype(BF16)
        turn_out[0:e_cols] = e1_ref[...].T.astype(BF16)
        turn_out[e_cols : e_cols + r2_rows] = r2_ref[...].astype(BF16)
        turn_out[e_cols + r2_rows :] = e2_ref[...].T.astype(BF16)
        for k in range(wide_blocks):
            sc_out[k * in_rows : (k + 1) * in_rows] = sc_ref[:, block_lanes(k)].astype(BF16)

    def gather_batch(x):
        return lax.all_gather(x, "batch", axis=0, tiled=False)

    place = jnp.stack([me, ber]).astype(jnp.int32)
    pick_large = jnp.asarray(geo.pick, BF16)
    b_rows, turn_rows = e_cols + r2_rows + wide_blocks * in_rows, 2 * e_cols + r2_rows
    entry, first, turned, sc_rows, s2_rows = call(
        prepare_kernel,
        (
            struct((4, px, part_in), BF16),
            struct((nb, in_rows + 9 * s_rows, mid), BF16),
            struct((turn_rows, mid), BF16),
            struct((wide_blocks * in_rows, mid), BF16),
            struct((9 * s_rows, mid), BF16),
        ),
        place, block_input.transpose(1, 2, 0, 3), pick_large, first_reduce, first_spatial.reshape(9 * s_rows, mid),
        first_expand, first_shortcut, second_reduce, second_spatial.reshape(9 * s_rows, mid), second_expand,
    )
    first, turned = to_batch(first), turn_share(turned)
    entry = lax.all_gather(entry, "chan", axis=0, tiled=False)

    def shares_kernel(p_ref, turned_ref, sc_ref, s2_ref, b_out, c_out):
        b_out[0 : e_cols + r2_rows] = turned_ref[0 : e_cols + r2_rows]
        b_out[e_cols + r2_rows :] = sc_ref[...]
        c_out[0:e_cols] = turned_ref[e_cols + r2_rows :]
        c_out[e_cols:] = s2_ref[...]

    b_share, c_share = call(
        shares_kernel,
        (struct((b_rows, mid), BF16), struct((e_cols + 9 * s_rows, mid), BF16)),
        place, turned, sc_rows, s2_rows, after=[first],
    )
    group_b, group_c = gather_batch(b_share), gather_batch(c_share)
    r1_w = first
    e1_w = part(group_b, (nb, e_cols, mid), (0, 0, 0))
    r2_w = part(group_b, (nb, r2_rows, mid), (0, e_cols // r2_rows, 0))
    sc_w = part(group_b, (nb, wide_blocks * in_rows, mid), (0, (e_cols + r2_rows) // (wide_blocks * in_rows), 0))
    e2_w = part(group_c, (nb, e_cols, mid), (0, 0, 0))

    def spatial_weight(x, at):
        if s_rows % 16 == 0:
            return x, at, s_rows, spread
        x = x[:, at:].reshape(nc, spread, 9, s_rows, mid).transpose(0, 2, 1, 3, 4)
        return x.reshape(nc, 9 * mid, mid), 0, mid, 1

    s1_w, s2_w = spatial_weight(first, in_rows), spatial_weight(group_c, e_cols)

    start = ber * crops
    sides = lax.dynamic_slice_in_dim(crop_sides, start, crops)
    ids = lax.dynamic_slice_in_dim(subnet_ids, start, crops)
    labels = jnp.arange(8, dtype=jnp.int32)
    member_all = (subnet_ids[None, :] == labels[:subs, None]).astype(F32)
    halves = crop_sides // 2
    count_full = jnp.sum(member_all * (crop_sides * crop_sides).astype(F32)[None, :], axis=1)
    count_half = jnp.sum(member_all * (halves * halves).astype(F32)[None, :], axis=1)
    counts = jnp.broadcast_to(
        jnp.concatenate([count_half, count_full, jnp.ones((8 - 2 * subs,), F32)])[:, None], (8, LANES)
    )
    pick = jnp.asarray(geo.rows[:, 0:1] == np.arange(crops)[None, :])
    side_row = jnp.sum(jnp.where(pick, sides[None, :], 0), axis=1, keepdims=True)
    id_row = jnp.sum(jnp.where(pick, ids[None, :], 0), axis=1, keepdims=True)
    row_i, row_j = jnp.asarray(geo.rows[:, 1:2]), jnp.asarray(geo.rows[:, 2:3])
    own = id_row == labels[None, :]
    seg_half = (own & (row_i < side_row // 2) & (row_j < side_row // 2)).astype(F32)
    seg_full = jnp.stack(
        [
            (own & (2 * row_i + p < side_row) & (2 * row_j + q < side_row)).astype(F32)
            for p in range(2)
            for q in range(2)
        ]
    )
    channel = jnp.arange(whole_mid, dtype=jnp.int32).reshape(nc, 1, mid)
    limits = jnp.concatenate([subnet_widths, jnp.zeros((8 - subs,), jnp.int32)])
    active = (channel < limits[None, :, None]).astype(F32)
    source = jnp.asarray(geo.source)
    own_params = jnp.concatenate([first_mid_gain, first_mid_bias, second_mid_gain, second_mid_bias], axis=0)
    params = jnp.stack(slots_of(own_params))

    def norm_slots(p_ref, raw, st_ref, par_ref, active_ref, seg, count, which, put, keep_own):
        block, layer = which
        chan = p_ref[0]
        for r in range(nc):
            ch = chan ^ r
            total = st_ref[ch]
            for b in range(1, nb):
                total = total + st_ref[b * nc + ch]
            average, inverse = moments(row_list(total, 0, 2 * subs), count, subs)
            gain = par_ref[r, 4 * block + layer : 4 * block + layer + 1, :]
            bias = par_ref[r, 4 * block + 2 + layer : 4 * block + 3 + layer, :]
            act_rows = row_list(active_ref[ch], 0, subs)
            xhat = (raw(r).astype(F32) - select(seg, average)) * select(seg, inverse)
            keep = select(seg, act_rows)
            value, slope = silu_and_slope(gain * xhat + bias)
            put(r, (value * keep).astype(BF16))
            if r == 0:
                keep_own(xhat, slope * keep, inverse)

    def send_sums(st_ref, seg, raw):
        value = raw.astype(F32)
        put_sums(st_ref, sums(seg, value) + sums(seg, value * value))
        fan_out(st_ref)

    every = nb * nc

    def joined(ref, *at):
        return jnp.concatenate([ref[(*at, r)] for r in range(nc)], axis=1)

    def block_rows(p_ref, ref, r):
        return jnp.concatenate([ref[(p_ref[0] ^ r) * spread + j] for j in range(spread)], axis=0)

    def joined_weight(p_ref, ref):
        return jnp.concatenate([block_rows(p_ref, ref, r) for r in range(nc)], axis=1)

    def tap_weight(p_ref, ref, tap, form):
        _, at, rows, per = form
        first = at + tap * rows
        return jnp.concatenate(
            [ref[(p_ref[0] ^ r) * per + j, first : first + rows, :] for r in range(nc) for j in range(per)], axis=0
        )

    def reduce_rows(ref, first, count):
        return jnp.concatenate([ref[b, 0:in_rows, :] for b in range(first, first + count)], axis=0)

    def shortcut_rows(ref, first, count):
        return jnp.concatenate(
            [
                jnp.concatenate([ref[b, k * in_rows : (k + 1) * in_rows, :] for k in range(wide_blocks)], axis=1)
                for b in range(first, first + count)
            ],
            axis=0,
        )

    def reduce_kernel(p_ref, entry_ref, w_ref, seg_ref, raw_ref, st_ref):
        w = reduce_rows(w_ref, 0, nb)
        rows = [jnp.zeros((1, LANES), F32)] * (2 * subs)
        for k in range(4):
            seg = columns_of(seg_ref[k], subs)
            mask = mask_of(seg)
            raw = (dot(jnp.concatenate([entry_ref[c, k] for c in range(nc)], axis=1), w) * mask).astype(BF16)
            raw_ref[k] = raw
            value = raw.astype(F32)
            new = sums(seg, value) + sums(seg, value * value)
            rows = [a + b for a, b in zip(rows, new)]
        put_sums(st_ref, rows)
        fan_out(st_ref)

    def short_kernel(p_ref, entry_ref, w_ref, segh_ref, out_ref):
        got = dot(jnp.concatenate([entry_ref[c] for c in range(nc)], axis=1), shortcut_rows(w_ref, 0, nb))
        out_ref[...] = got * jnp.sum(segh_ref[...], axis=1, keepdims=True)

    def spatial_one_kernel(
        p_ref, r0, r1_, r2_, r3, st_ref, par_ref, act_ref, segf_ref, segh_ref, cnt_ref, src_ref, w_ref,
        out_ref, xhat_ref, slope_ref, inv_ref, raw_ref, sto_ref,
    ):
        refs = (r0, r1_, r2_, r3)
        count = row_list(cnt_ref[...], subs, subs)
        for k in range(4):
            seg = columns_of(segf_ref[k], subs)

            def put(r, value):
                out_ref[k, r] = value

            def keep_own(xhat, slope, inverse):
                xhat_ref[k] = xhat
                slope_ref[k] = slope
                if k == 0:
                    for n, row in enumerate(inverse):
                        inv_ref[n : n + 1, :] = row

            norm_slots(
                p_ref, lambda r: refs[r][k], st_ref, par_ref, act_ref, seg, count, (0, 0), put, keep_own
            )
        src = src_ref[...]
        total = jnp.zeros((px, mid), F32)
        for tap in range(9):
            plane, shift = STRIDED_TAPS[tap]
            total = total + dot(shifted(src, shift, joined(out_ref, plane)), tap_weight(p_ref, w_ref, tap, s1_w))
        raw = total.astype(BF16)
        raw_ref[...] = raw
        send_sums(sto_ref, columns_of(segh_ref[...], subs), raw)

    def mid_inputs(raws, st):
        return (*raws, st, params, active, seg_half, counts)

    def mid_outs():
        return (
            struct((nc, px, mid), BF16),
            struct((px, mid)),
            struct((px, mid)),
            struct((8, mid)),
        )

    def mid_part(which, p_ref, refs, st_ref, par_ref, act_ref, segh_ref, cnt_ref, out_ref, xhat_ref, slope_ref, inv_ref):
        seg = columns_of(segh_ref[...], subs)

        def put(r, value):
            out_ref[r] = value

        def keep_own(xhat, slope, inverse):
            xhat_ref[...] = xhat
            slope_ref[...] = slope
            for n, row in enumerate(inverse):
                inv_ref[n : n + 1, :] = row

        norm_slots(
            p_ref, lambda r: refs[r][...], st_ref, par_ref, act_ref, seg,
            row_list(cnt_ref[...], 0, subs), which, put, keep_own,
        )
        return seg

    def wide_sums(st_ref, seg, fields):
        for k in range(wide_blocks):
            rows = fields(k)
            put_sums(st_ref, rows, k * len(rows))
        fan_out(st_ref)

    def expand_one_kernel(
        p_ref, r0, r1_, r2_, r3, st_ref, par_ref, act_ref, segh_ref, cnt_ref, w_ref, short_ref,
        out_ref, xhat_ref, slope_ref, inv_ref, pre_ref, sto_ref,
    ):
        seg = mid_part(
            (0, 1), p_ref, (r0, r1_, r2_, r3), st_ref, par_ref, act_ref, segh_ref, cnt_ref,
            out_ref, xhat_ref, slope_ref, inv_ref,
        )
        pre_ref[...] = dot_nt(joined(out_ref), joined_weight(p_ref, w_ref))

        def fields(k):
            a, b = pre_ref[:, block_lanes(k)], short_ref[:, block_lanes(k)]
            return sums(seg, a) + sums(seg, a * a) + sums(seg, b) + sums(seg, b * b)

        wide_sums(sto_ref, seg, fields)

    def summed(st_ref, k=0, rows=2 * subs):
        total = st_ref[0, k * rows : (k + 1) * rows, :]
        for b in range(1, nb):
            total = total + st_ref[b, k * rows : (k + 1) * rows, :]
        return total

    def to_slots(slot_refs, value):
        for r in range(nc):
            slot_refs[r][...] = value[:, r * mid : (r + 1) * mid].astype(BF16)

    def section_kernel(
        p_ref, st_ref, three_ref, short_ref, gain_ref, bias_ref, segh_ref, cnt_ref, w_ref,
        xh3_ref, xhs_ref, out_ref, slope_ref, inv_ref, low_ref, *slot_refs,
    ):
        seg = columns_of(segh_ref[...], subs)
        mask = mask_of(seg)
        count = row_list(cnt_ref[...], 0, subs)
        for k in range(wide_blocks):
            ln = block_lanes(k)
            total = summed(st_ref, k, 4 * subs)
            both = None
            for n, (pre, keep) in enumerate(((three_ref, xh3_ref), (short_ref, xhs_ref))):
                average, inverse = moments(row_list(total, 2 * subs * n, 2 * subs), count, subs)
                xhat = (pre[:, ln] - select(seg, average)) * select(seg, inverse)
                keep[:, ln] = xhat
                for s in range(subs):
                    inv_ref[n * subs + s : n * subs + s + 1, ln] = inverse[s]
                norm = gain_ref[n : n + 1, ln] * xhat + bias_ref[n : n + 1, ln]
                both = norm if both is None else both + norm
            value, slope = silu_and_slope(both)
            value = value * mask
            out_ref[:, ln] = value
            slope_ref[:, ln] = slope * mask
            low_ref[:, ln] = value.astype(BF16)
        to_slots(slot_refs, dot(low_ref[...], joined_weight(p_ref, w_ref)))

    def four_kernel(p_ref, s0, s1_, s2_, s3, segh_ref, raw_ref, sto_ref):
        total = s0[...].astype(F32)
        for ref in (s1_, s2_, s3):
            total = total + ref[...].astype(F32)
        raw = total.astype(BF16)
        raw_ref[...] = raw
        send_sums(sto_ref, columns_of(segh_ref[...], subs), raw)

    def spatial_two_kernel(
        p_ref, r0, r1_, r2_, r3, st_ref, par_ref, act_ref, segh_ref, cnt_ref, src_ref, w_ref,
        out_ref, xhat_ref, slope_ref, inv_ref, raw_ref, sto_ref,
    ):
        seg = mid_part(
            (1, 0), p_ref, (r0, r1_, r2_, r3), st_ref, par_ref, act_ref, segh_ref, cnt_ref,
            out_ref, xhat_ref, slope_ref, inv_ref,
        )
        src = src_ref[...]
        total = jnp.zeros((px, mid), F32)
        whole = joined(out_ref)
        for tap in range(9):
            total = total + dot(shifted(src, tap, whole), tap_weight(p_ref, w_ref, tap, s2_w))
        raw = total.astype(BF16)
        raw_ref[...] = raw
        send_sums(sto_ref, seg, raw)

    def expand_two_kernel(
        p_ref, r0, r1_, r2_, r3, st_ref, par_ref, act_ref, segh_ref, cnt_ref, w_ref,
        out_ref, xhat_ref, slope_ref, inv_ref, pre_ref, sto_ref,
    ):
        seg = mid_part(
            (1, 1), p_ref, (r0, r1_, r2_, r3), st_ref, par_ref, act_ref, segh_ref, cnt_ref,
            out_ref, xhat_ref, slope_ref, inv_ref,
        )
        pre_ref[...] = dot_nt(joined(out_ref), joined_weight(p_ref, w_ref))

        def fields(k):
            a = pre_ref[:, block_lanes(k)]
            return sums(seg, a) + sums(seg, a * a)

        wide_sums(sto_ref, seg, fields)

    def final_kernel(
        p_ref, st_ref, pre_ref, section_ref, cot_ref, gain_ref, bias_ref, segh_ref, cnt_ref, pick_ref,
        out_ref, grad_ref, xhat_ref, inv_ref, sto_ref,
    ):
        seg = columns_of(segh_ref[...], subs)
        mask = mask_of(seg)
        count = row_list(cnt_ref[...], 0, subs)
        picked = pick_ref[...]
        for k in range(wide_blocks):
            ln = block_lanes(k)
            average, inverse = moments(row_list(summed(st_ref, k), 0, 2 * subs), count, subs)
            xhat = (pre_ref[:, ln] - select(seg, average)) * select(seg, inverse)
            xhat_ref[:, ln] = xhat
            for s in range(subs):
                inv_ref[s : s + 1, ln] = inverse[s]
            both = gain_ref[:, ln] * xhat + bias_ref[:, ln] + section_ref[:, ln]
            value, slope = silu_and_slope(both)
            value = value * mask

            def place_out(i, j, first, rows):
                out_ref[i, j, first : first + rows.shape[0], ln] = rows

            geo.unpack(lambda first, count: value[first : first + count], place_out)
            parts = []
            geo.pack(picked, lambda i, j: cot_ref[i, j, :, ln], lambda first, rows: parts.append(rows))
            grad = jnp.concatenate(parts, axis=0).astype(F32) * mask * slope
            grad_ref[:, ln] = grad
            put_sums(sto_ref, sums(seg, grad) + sums(seg, grad * xhat), k * 2 * subs)
        fan_out(sto_ref)

    def norm_back(total, at, gain, inverse, u, xhat, seg, count):
        g = [total[s : s + 1] / count[s] for s in range(subs)]
        x = [total[at + s : at + s + 1] / count[s] for s in range(subs)]
        scale = select(seg, [gain * row for row in inverse])
        return (scale * (u - (select(seg, g) + xhat * select(seg, x)))).astype(BF16)

    def put_param_grads(ref, ln, total, pairs):
        for n, first in enumerate(pairs):
            row = total[first : first + 1]
            for s in range(1, subs):
                row = row + total[first + s : first + s + 1]
            ref[n : n + 1, ln] = row

    def back_six_kernel(
        p_ref, st_ref, u_ref, xhat_ref, inv_ref, gain_ref, segh_ref, cnt_ref, w_ref, low_ref, par_ref, *slot_refs
    ):
        seg = columns_of(segh_ref[...], subs)
        count = row_list(cnt_ref[...], 0, subs)
        for k in range(wide_blocks):
            ln = block_lanes(k)
            total = summed(st_ref, k)
            put_param_grads(par_ref, ln, total, (subs, 0))
            low_ref[:, ln] = norm_back(
                total, subs, gain_ref[:, ln], row_list(inv_ref[:, ln], 0, subs), u_ref[:, ln], xhat_ref[:, ln], seg, count
            )
        to_slots(slot_refs, dot(low_ref[...], joined_weight(p_ref, w_ref)))

    def upstream_kernel(p_ref, s0, s1_, s2_, s3, slope_ref, xhat_ref, segh_ref, u_ref, sto_ref):
        total = s0[...].astype(F32)
        for ref in (s1_, s2_, s3):
            total = total + ref[...].astype(F32)
        u = total * slope_ref[...]
        u_ref[...] = u
        seg = columns_of(segh_ref[...], subs)
        put_sums(sto_ref, sums(seg, u) + sums(seg, u * xhat_ref[...]))
        fan_out(sto_ref)

    def own_gain(ref, which):
        block, layer = which
        return ref[0, 4 * block + layer : 4 * block + layer + 1, :]

    def back_spatial_kernel(which, taps, order, form):
        def kernel(
            p_ref, st_ref, u_ref, xhat_ref, inv_ref, params_ref, segh_ref, cnt_ref, src_ref, w_ref,
            cols_ref, par_ref, *slot_refs,
        ):
            seg = columns_of(segh_ref[...], subs)
            count = row_list(cnt_ref[...], 0, subs)
            total = summed(st_ref)
            put_param_grads(par_ref, slice(0, LANES), total, (subs, 0))
            low = norm_back(
                total, subs, own_gain(params_ref, which), row_list(inv_ref[...], 0, subs), u_ref[...], xhat_ref[...], seg, count
            )
            src = src_ref[...]
            back, at = None, None
            for n, tap in enumerate(order):
                plane, shift = taps[tap]
                g = shifted(src, 8 - shift, low)
                cols_ref[:, n * mid : (n + 1) * mid] = g
                new = dot_nt(g, tap_weight(p_ref, w_ref, tap, form))
                back = new if plane != at else back + new
                at = plane
                if n == 8 or taps[order[n + 1]][0] != plane:
                    for r in range(nc):
                        slot_refs[r][plane] = back[:, r * mid : (r + 1) * mid].astype(BF16)

        return kernel

    def back_plain_kernel(which):
        def kernel(p_ref, st_ref, u_ref, xhat_ref, inv_ref, params_ref, segh_ref, cnt_ref, low_ref, par_ref):
            seg = columns_of(segh_ref[...], subs)
            count = row_list(cnt_ref[...], 0, subs)
            total = summed(st_ref)
            put_param_grads(par_ref, slice(0, LANES), total, (subs, 0))
            low_ref[...] = norm_back(
                total, subs, own_gain(params_ref, which), row_list(inv_ref[...], 0, subs), u_ref[...], xhat_ref[...], seg, count
            )

        return kernel

    def back_section_kernel(
        p_ref, g0, g1, g2, g3, w_ref, grad_ref, slope_ref, xh3_ref, xhs_ref, segh_ref,
        whole_ref, u_ref, sto_ref,
    ):
        for r, ref in enumerate((g0, g1, g2, g3)):
            whole_ref[r] = ref[...]
        u_ref[...] = dot_nt(joined(whole_ref), joined_weight(p_ref, w_ref))
        seg = columns_of(segh_ref[...], subs)
        for k in range(wide_blocks):
            ln = block_lanes(k)
            u = (u_ref[:, ln] + grad_ref[:, ln]) * slope_ref[:, ln]
            u_ref[:, ln] = u
            rows = sums(seg, u) + sums(seg, u * xh3_ref[:, ln]) + sums(seg, u * xhs_ref[:, ln])
            put_sums(sto_ref, rows, k * 3 * subs)
        fan_out(sto_ref)

    def back_wide_kernel(
        p_ref, st_ref, u_ref, xh3_ref, xhs_ref, inv_ref, gain_ref, segh_ref, cnt_ref, w_ref,
        three_ref, short_ref, par_ref, *slot_refs,
    ):
        seg = columns_of(segh_ref[...], subs)
        count = row_list(cnt_ref[...], 0, subs)
        for k in range(wide_blocks):
            ln = block_lanes(k)
            total = summed(st_ref, k, 3 * subs)
            put_param_grads(par_ref, ln, total, (subs, 2 * subs, 0))
            u = u_ref[:, ln]
            inverse = inv_ref[:, ln]
            three_ref[:, ln] = norm_back(
                total, subs, gain_ref[0:1, ln], row_list(inverse, 0, subs), u, xh3_ref[:, ln], seg, count
            )
            short_ref[:, ln] = norm_back(
                total, 2 * subs, gain_ref[1:2, ln], row_list(inverse, subs, subs), u, xhs_ref[:, ln], seg, count
            )
        to_slots(slot_refs, dot(three_ref[...], joined_weight(p_ref, w_ref)))

    def upstream_one_kernel(p_ref, s0, s1_, s2_, s3, slope_ref, xhat_ref, segf_ref, u_ref, sto_ref):
        rows = [jnp.zeros((1, LANES), F32)] * (2 * subs)
        for k in range(4):
            total = s0[k].astype(F32)
            for ref in (s1_, s2_, s3):
                total = total + ref[k].astype(F32)
            u = total * slope_ref[k]
            u_ref[k] = u
            seg = columns_of(segf_ref[k], subs)
            new = sums(seg, u) + sums(seg, u * xhat_ref[k])
            rows = [a + b for a, b in zip(rows, new)]
        put_sums(sto_ref, rows)
        fan_out(sto_ref)

    def back_one_kernel(
        p_ref, st_ref, u_ref, xhat_ref, inv_ref, params_ref, segf_ref, cnt_ref, w_ref, short_ref, sc_ref,
        low_ref, par_ref, *slot_refs,
    ):
        count = row_list(cnt_ref[...], subs, subs)
        total = summed(st_ref)
        put_param_grads(par_ref, slice(0, LANES), total, (subs, 0))
        for k in range(4):
            seg = columns_of(segf_ref[k], subs)
            low_ref[k] = norm_back(
                total, subs, own_gain(params_ref, (0, 0)), row_list(inv_ref[...], 0, subs), u_ref[k], xhat_ref[k], seg, count
            )
        for r in range(nc):
            first = (p_ref[0] ^ r) * spread
            w = jnp.concatenate([w_ref[first + j, 0:in_rows, :] for j in range(spread)], axis=0)
            for k in range(4):
                got = dot_nt(low_ref[k], w)
                if k == 0:
                    got = got + dot_nt(
                        short_ref[...],
                        jnp.concatenate(
                            [
                                jnp.concatenate(
                                    [sc_ref[first + j, n * in_rows : (n + 1) * in_rows, :] for n in range(wide_blocks)],
                                    axis=1,
                                )
                                for j in range(spread)
                            ],
                            axis=0,
                        ),
                    )
                slot_refs[r][k] = got.astype(BF16)

    def input_kernel(p_ref, a_ref, b_ref, c_ref, segf_ref, out_ref):
        for k in range(4):
            mask = jnp.sum(segf_ref[k], axis=1, keepdims=True)
            total = a_ref[k].astype(F32) + b_ref[k].astype(F32) + c_ref[k].astype(F32)
            total = total * mask

            def place_out(i, j, first, rows):
                out_ref[2 * i + k // 2, 2 * j + k % 2, first : first + rows.shape[0], :] = rows

            geo.unpack(lambda first, count: total[first : first + count], place_out)

    def put_expand(p_ref, out_ref, at, grad_ref, act_ref):
        for k in range(nc):
            got = dot_tn(grad_ref[...], act_ref[p_ref[0] ^ k]).astype(BF16)
            for j in range(spread):
                out_ref[k * spread + j, at : at + e_cols, :] = got[j * e_cols : (j + 1) * e_cols]

    def put_spatial(out_ref, at, k, taps, got):
        for j in range(spread):
            for n, tap in enumerate(taps):
                first = at + tap * s_rows
                out_ref[k * spread + j, first : first + s_rows, :] = got[
                    j * s_rows : (j + 1) * s_rows, n * mid : (n + 1) * mid
                ]

    def grads_two_kernel(p_ref, six_ref, act5_ref, act4_ref, cols_ref, out_ref):
        put_expand(p_ref, out_ref, 0, six_ref, act5_ref)
        for k in range(nc):
            got = dot_tn(act4_ref[p_ref[0] ^ k], cols_ref[...]).astype(BF16)
            put_spatial(out_ref, e_cols, k, range(9), got)

    def grads_mixed_kernel(p_ref, low_ref, four_ref, three_ref, act2_ref, entry_ref, short_ref, out_ref):
        for k in range(nc):
            got = dot_tn(low_ref[...], four_ref[p_ref[0] ^ k]).astype(BF16)
            for j in range(spread):
                out_ref[k * spread + j, 0:r2_rows, :] = got[j * r2_rows : (j + 1) * r2_rows]
        put_expand(p_ref, out_ref, r2_rows, three_ref, act2_ref)
        first = r2_rows + e_cols
        for c in range(nc):
            got = dot_tn(entry_ref[c], short_ref[...]).astype(BF16)
            for j in range(spread):
                for k in range(wide_blocks):
                    out_ref[c * spread + j, first + k * in_rows : first + (k + 1) * in_rows, :] = got[
                        j * in_rows : (j + 1) * in_rows, block_lanes(k)
                    ]

    def grads_reduce_kernel(p_ref, entry_ref, grad_ref, out_ref):
        for c in range(nc):
            got = dot_tn(entry_ref[c, 0], grad_ref[0])
            for k in range(1, 4):
                got = got + dot_tn(entry_ref[c, k], grad_ref[k])
            for j in range(spread):
                out_ref[c * spread + j] = got[j * in_rows : (j + 1) * in_rows].astype(BF16)

    def grads_one_kernel(p_ref, act_ref, cols_ref, keep_ref, send_ref):
        odd = lax.rem(p_ref[1], 2) == 1
        for k in range(nc):
            first = 0
            for plane in range(4):
                taps = [t for t in STRIDED_ORDER if STRIDED_TAPS[t][0] == plane]
                lanes = slice(first * mid, (first + len(taps)) * mid)
                first += len(taps)
                got = dot_tn(act_ref[plane, p_ref[0] ^ k], cols_ref[:, lanes])
                for j in range(0, spread, 2):
                    one, two = got[j * s_rows : (j + 1) * s_rows], got[(j + 1) * s_rows : (j + 2) * s_rows]
                    keep, send = jnp.where(odd, two, one).astype(BF16), jnp.where(odd, one, two).astype(BF16)
                    for n, tap in enumerate(taps):
                        rows = slice(tap * s_rows, (tap + 1) * s_rows)
                        keep_ref[(k * spread + j) // 2, rows, :] = keep[:, n * mid : (n + 1) * mid]
                        send_ref[(k * spread + j) // 2, rows, :] = send[:, n * mid : (n + 1) * mid]

    def halves_kernel(p_ref, keep_ref, got_ref, *slot_refs):
        pair = lax.div(p_ref[1], 2)
        for r, ref in enumerate(slot_refs):
            ref[...] = (keep_ref[pair ^ r].astype(F32) + got_ref[pair ^ r].astype(F32)).astype(BF16)

    def total_kernel(p_ref, *refs):
        total = refs[0][...].astype(F32)
        for ref in refs[1:-1]:
            total = total + ref[...].astype(F32)
        refs[-1][...] = total

    def turn_kernel(p_ref, two_ref, mixed_ref, turn_out, s2_out, sc_out):
        turn_out[0:e_cols] = mixed_ref[r2_rows : r2_rows + e_cols]
        turn_out[e_cols : e_cols + r2_rows] = mixed_ref[0:r2_rows]
        turn_out[e_cols + r2_rows :] = two_ref[0:e_cols]
        s2_out[...] = two_ref[e_cols:].astype(F32)
        first = r2_rows + e_cols
        for k in range(wide_blocks):
            sc_out[:, block_lanes(k)] = mixed_ref[first + k * in_rows : first + (k + 1) * in_rows].astype(F32)

    def own_kernel(p_ref, turned_ref, e1_out, r2_out, e2_out):
        e1_out[...] = turned_ref[0:e_cols].astype(F32).T
        r2_out[...] = turned_ref[e_cols : e_cols + r2_rows].astype(F32)
        e2_out[...] = turned_ref[e_cols + r2_rows :].astype(F32).T

    def to_owners(shares):
        return lax.psum_scatter(shares, "batch", scatter_dimension=0, tiled=False)

    st_mid, st_own, st_wide = (
        struct((every, 8, LANES)),
        struct((nb, 8, LANES)),
        struct((nb, whole_tiles(2 * subs * wide_blocks), LANES)),
    )
    matmul = 2 * px * whole_mid * wide
    mid_slots = [struct((px, mid), BF16)] * nc
    half = side // 2

    raw_one, st = call(
        reduce_kernel, (struct((4, px, mid), BF16), st_mid), place, entry, r1_w, seg_full, flops=4 * matmul
    )
    raws, st = slots_of(raw_one), to_all(st)
    act_one, xhat_one, slope_one, inv_one, raw_two, st = call(
        spatial_one_kernel,
        (
            struct((4, nc, px, mid), BF16),
            struct((4, px, mid)),
            struct((4, px, mid)),
            struct((8, mid)),
            struct((px, mid), BF16),
            st_mid,
        ),
        place, *raws, st, params, active, seg_full, seg_half, counts, source, s1_w[0],
        flops=10 * matmul,
    )
    short_in = part(entry, (nc, None, px, part_in), (0, 0, 0, 0))
    (pre_short,) = call(short_kernel, (struct((px, wide)),), place, short_in, sc_w, seg_half, flops=4 * matmul)
    raws, st = slots_of(raw_two), to_all(st)
    act_two, xhat_two, slope_two, inv_two, pre_three, st = call(
        expand_one_kernel,
        (*mid_outs(), struct((px, wide)), struct((nb, whole_tiles(4 * subs * wide_blocks), LANES))),
        place, *mid_inputs(raws, st), e1_w, pre_short,
        flops=2 * matmul,
    )
    xhat_three, xhat_short, section_out, slope_section, inv_wide, section_low, *slots = call(
        section_kernel,
        (
            *[struct((px, wide))] * 4,
            struct((8, wide)),
            struct((px, wide), BF16),
            *mid_slots,
        ),
        place, to_batch(st), pre_three, pre_short, first_wide_gain, first_wide_bias, seg_half, counts, r2_w,
        flops=2 * matmul,
    )

    raw_four, st = call(
        four_kernel, (struct((px, mid), BF16), st_mid), place, *swap_slots(slots), seg_half
    )
    raws, st = slots_of(raw_four), to_all(st)
    act_four, xhat_four, slope_four, inv_four, raw_five, st = call(
        spatial_two_kernel,
        (*mid_outs(), struct((px, mid), BF16), st_mid),
        place, *mid_inputs(raws, st), source, s2_w[0],
        flops=8 * matmul,
    )
    raws, st = slots_of(raw_five), to_all(st)
    act_five, xhat_five, slope_five, inv_five, pre_six, st = call(
        expand_two_kernel,
        (*mid_outs(), struct((px, wide)), st_wide),
        place, *mid_inputs(raws, st), e2_w,
        flops=2 * matmul,
    )
    gain_six, bias_six = second_wide_gain[None], second_wide_bias[None]
    out_rows, grad_final, xhat_six, inv_six, st = call(
        final_kernel,
        (struct((half, half, crops, wide)), *[struct((px, wide))] * 2, struct((8, wide)), st_wide),
        place, to_batch(st), pre_six, section_out, cotangent.transpose(1, 2, 0, 3), gain_six, bias_six, seg_half, counts,
        pick_large,
    )
    output = out_rows.transpose(2, 0, 1, 3)

    grad_six, par_six, *slots = call(
        back_six_kernel,
        (struct((px, wide), BF16), struct((8, wide)), *mid_slots),
        place, to_batch(st), grad_final, xhat_six, inv_six, gain_six, seg_half, counts, e2_w,
        flops=2 * matmul,
    )

    def upstream(got, slope, xhat):
        return call(upstream_kernel, (struct((px, mid)), st_own), place, *got, slope, xhat, seg_half)

    u_five, st = upstream(swap_slots(slots), slope_five, xhat_five)
    cols_five, par_five, *slots = call(
        back_spatial_kernel((1, 1), UNIT_TAPS, list(range(9)), s2_w),
        (struct((px, 9 * mid), BF16), struct((8, mid)), *[struct((1, px, mid), BF16)] * nc),
        place, to_batch(st), u_five, xhat_five, inv_five, params, seg_half, counts, source, s2_w[0],
        flops=8 * matmul,
    )
    got_four = swap_slots([x.reshape(px, mid) for x in slots])
    u_four, st = upstream(got_four, slope_four, xhat_four)
    (shares_two,) = call(
        grads_two_kernel, (struct((nb, e_cols + 9 * s_rows, mid), BF16),),
        place, grad_six, act_five, act_four, cols_five, flops=10 * matmul,
    )
    grad_four, par_four = call(
        back_plain_kernel((1, 0)),
        (struct((px, mid), BF16), struct((8, mid))),
        place, to_batch(st), u_four, xhat_four, inv_four, params, seg_half, counts,
    )
    whole_grad_four, u_wide, st = call(
        back_section_kernel,
        (struct((nc, px, mid), BF16), struct((px, wide)), struct((nb, whole_tiles(3 * subs * wide_blocks), LANES))),
        place, *slots_of(grad_four), r2_w, grad_final, slope_section, xhat_three, xhat_short, seg_half,
        flops=2 * matmul,
    )

    grad_three, grad_short, par_wide, *slots = call(
        back_wide_kernel,
        (
            struct((px, wide), BF16),
            struct((px, wide), BF16),
            struct((8, wide)),
            *mid_slots,
        ),
        place, to_batch(st), u_wide, xhat_three, xhat_short, inv_wide, first_wide_gain, seg_half, counts, e1_w,
        flops=2 * matmul,
    )
    got_two = swap_slots(slots)
    u_two, st = upstream(got_two, slope_two, xhat_two)
    (shares_mixed,) = call(
        grads_mixed_kernel, (struct((nb, b_rows, mid), BF16),),
        place, section_low, whole_grad_four, grad_three, act_two, short_in, grad_short, flops=8 * matmul, after=[u_two],
    )
    cols_two, par_two, *slots = call(
        back_spatial_kernel((0, 1), STRIDED_TAPS, STRIDED_ORDER, s1_w),
        (struct((px, 9 * mid), BF16), struct((8, mid)), *[struct((4, px, mid), BF16)] * nc),
        place, to_batch(st), u_two, xhat_two, inv_two, params, seg_half, counts, source, s1_w[0],
        flops=8 * matmul, after=[shares_mixed],
    )
    got_one = swap_slots(slots)
    half_grad = struct((nb // 2, 9 * s_rows, mid), BF16)
    keep, send = call(
        grads_one_kernel, (half_grad, half_grad), place, act_one, cols_two, flops=8 * matmul
    )
    received = lax.ppermute(send, "batch", [(i, i ^ 1) for i in range(nb)])
    u_one, st = call(
        upstream_one_kernel,
        (struct((4, px, mid)), st_own),
        place, *got_one, slope_one, xhat_one, seg_full, after=[keep],
    )
    s1_slots = call(
        halves_kernel, [struct((9 * s_rows, mid), BF16)] * (nb // 2), place, keep, received, after=[u_one]
    )
    grad_one, par_one, *slots = call(
        back_one_kernel,
        (struct((4, px, mid), BF16), struct((8, mid)), *[struct((4, px, part_in), BF16)] * nc),
        place, to_batch(st), u_one, xhat_one, inv_one, params, seg_full, counts, r1_w, grad_short, sc_w,
        flops=8 * matmul, after=[s1_slots[0]],
    )
    far_first, own_back = chan_swap(slots[3], 1), chan_swap(slots[1], 1)
    far_sum = (slots[2].astype(F32) + far_first.astype(F32)).astype(BF16)
    far_back = chan_swap(far_sum, 2)

    (s1_total,) = call(
        total_kernel, (struct((9 * s_rows, mid)),), place,
        *[
            x if r == 0 else lax.ppermute(x, "batch", [(i, i ^ (2 * r)) for i in range(nb)])
            for r, x in enumerate(s1_slots)
        ],
    )
    (shares,) = call(
        grads_reduce_kernel, (struct((nb, in_rows, mid), BF16),),
        place, entry, grad_one, flops=4 * matmul, after=[far_sum],
    )
    r1_out = jnp.sum(to_batch(shares).astype(F32), axis=0)
    turned, s2_own, sc_own = call(
        turn_kernel,
        (struct((turn_rows, mid), BF16), struct((9 * s_rows, mid)), struct((in_rows, wide))),
        place, to_owners(shares_two), to_owners(shares_mixed),
    )
    e1_own, r2_own, e2_own = call(
        own_kernel,
        (struct((mid, e_cols)), struct((r2_rows, mid)), struct((mid, e_cols))),
        place, turn_share(turned),
    )
    outs = (
        output,
        s1_total.reshape(3, 3, s_rows, mid),
        e1_own,
        sc_own,
        r2_own,
        s2_own.reshape(3, 3, s_rows, mid),
        e2_own,
        jnp.stack([par_one[0], par_two[0]]),
        jnp.stack([par_one[1], par_two[1]]),
        par_wide[:2],
        jnp.stack([par_wide[2], par_wide[2]]),
        jnp.stack([par_four[0], par_five[0]]),
        jnp.stack([par_four[1], par_five[1]]),
        par_six[0],
        par_six[1],
    )
    (input_grad,) = call(
        input_kernel, (struct((side, side, crops, part_in)),), place, slots[0], own_back, far_back, seg_full,
        after=[s1_total, *outs[2:5], s2_own, *outs[6:]],
    )
    return outs[:1] + (input_grad.transpose(2, 0, 1, 3), r1_out) + outs[1:]


def solution(mesh):
    placed = (
        P("batch", None, None, "chan"),
        P("batch", "chan"),
        P(None, None, "batch", "chan"),
        P("chan", "batch"),
        P("batch", "chan"),
        P("batch", "chan"),
        P(None, None, "batch", "chan"),
        P("chan", "batch"),
        P(None, "chan"),
        P(None, "chan"),
        P(None, "chan"),
        P(None, "chan"),
        P(None, "chan"),
        P(None, "chan"),
        P("chan"),
        P("chan"),
        P(),
        P(),
        P(),
        P("batch", None, None, "chan"),
    )
    outs = (
        P("batch", None, None, "chan"),
        P("batch", None, None, "chan"),
        P("batch", "chan"),
        P(None, None, "batch", "chan"),
        P("chan", "batch"),
        P("batch", "chan"),
        P("batch", "chan"),
        P(None, None, "batch", "chan"),
        P("chan", "batch"),
        P(None, "chan"),
        P(None, "chan"),
        P(None, "chan"),
        P(None, "chan"),
        P(None, "chan"),
        P(None, "chan"),
        P("chan"),
        P("chan"),
    )
    return jax.shard_map(local, mesh=mesh, in_specs=placed, out_specs=outs, check_vma=False)
```

```python
import jax
import jax.numpy as jnp
import numpy as np
from jax import lax
from jax.experimental import pallas as pl
from jax.experimental.pallas import tpu as pltpu
from jax.sharding import PartitionSpec as P

F32, BF16 = jnp.float32, jnp.bfloat16
EPS = 1e-05
SMALL = 6
LANES = 128
ALL = ("batch", "chan")


class Geometry:
    def __init__(self, crops, side):
        self.crops, self.side = crops, side
        self.half, self.small = side // 2, SMALL // 2
        self.large = [c for c in range(crops) if c % 8 < 2]
        grid = [(i, j) for i in range(self.half) for j in range(self.half)]
        self.common = [at for at in grid if max(at) < self.small]
        self.others = [at for at in grid if max(at) >= self.small]
        rows = [(c, i, j) for i, j in self.common for c in range(crops)]
        rows += [(c, i, j) for i, j in self.others for c in self.large]
        self.cut = len(self.common) * crops
        self.rows = np.array(rows, np.int32)
        self.pixels = len(rows)
        where = {tuple(r): n for n, r in enumerate(rows)}
        source = np.full((self.pixels, 16), -1, np.int32)
        for n, (crop, i, j) in enumerate(rows):
            for shift in range(9):
                source[n, shift] = where.get((crop, i + shift // 3 - 1, j + shift % 3 - 1), -1)
        self.source = source
        self.group = 8
        wanted = len(self.large)
        pick = np.zeros((self.group * wanted, self.group * crops), np.float32)
        for n in range(self.group):
            for m, c in enumerate(self.large):
                pick[n * wanted + m, n * crops + c] = 1.0
        self.pick = pick

    def pack(self, pick, load, store):
        for n, (i, j) in enumerate(self.common):
            store(n * self.crops, load(i, j))
        wanted = len(self.large)
        for n in range(0, len(self.others), self.group):
            rows = jnp.concatenate([load(i, j) for i, j in self.others[n : n + self.group]], axis=0)
            store(self.cut + n * wanted, dot(pick, rows).astype(rows.dtype))

    def unpack(self, load, store):
        for n, (i, j) in enumerate(self.common):
            store(i, j, 0, load(n * self.crops, self.crops))
        wanted = len(self.large)
        for n, (i, j) in enumerate(self.others):
            rows = load(self.cut + n * wanted, wanted)
            store(i, j, 0, jnp.zeros((self.crops, rows.shape[1]), rows.dtype))
            for m in range(0, wanted, 2):
                store(i, j, self.large[m], rows[m : m + 2])


UNIT_TAPS = [(0, tap) for tap in range(9)]
STRIDED_TAPS = [
    (2 * int(r != 1) + int(c != 1), 3 * (0 if r == 0 else 1) + (0 if c == 0 else 1))
    for r in range(3)
    for c in range(3)
]
STRIDED_ORDER = [tap for plane in range(4) for tap in range(9) if STRIDED_TAPS[tap][0] == plane]

SM = pl.BlockSpec(memory_space=pltpu.SMEM)


def struct(shape, dtype=F32):
    return jax.ShapeDtypeStruct(tuple(shape), dtype)


def whole_block(shape, at=None):
    at = at or (0,) * len(shape)
    return pl.BlockSpec(tuple(shape), lambda _: at)


def part(array, shape, at):
    return array, whole_block(shape, at)


def corner(array):
    shape = (1,) * (array.ndim - 2) + (16, LANES) if array.ndim > 1 else array.shape
    return array, whole_block([min(a, b) for a, b in zip(shape, array.shape)], (0,) * array.ndim)


def call(kernel, outs, place, *args, flops=10**8, mib=64, after=()):
    args = [a if isinstance(a, tuple) else (a, whole_block(a.shape)) for a in args]
    moved = sum(int(np.prod([n or 1 for n in b.block_shape])) * a.dtype.itemsize for a, b in args)
    moved += sum(int(np.prod(o.shape)) * o.dtype.itemsize for o in outs)
    used, args = len(args), args + [corner(a) for a in after]

    def body(p_ref, *refs):
        kernel(p_ref, *refs[:used], *refs[len(args) :])

    return pl.pallas_call(
        body,
        grid=(1,),
        out_shape=tuple(outs),
        in_specs=[SM] + [b for _, b in args],
        out_specs=tuple(whole_block(o.shape) for o in outs),
        compiler_params=pltpu.CompilerParams(vmem_limit_bytes=mib * 1024 * 1024),
        cost_estimate=pl.CostEstimate(flops=flops, bytes_accessed=moved, transcendentals=0),
    )(place, *[a for a, _ in args])


def dot(a, b):
    return jnp.dot(a, b, preferred_element_type=F32)


def dot_nt(a, b):
    return lax.dot_general(a, b, (((1,), (1,)), ((), ())), preferred_element_type=F32)


def dot_tn(a, b):
    return lax.dot_general(a, b, (((0,), (0,)), ((), ())), preferred_element_type=F32)


def columns_of(seg, subs):
    return [jnp.broadcast_to(seg[:, s : s + 1], (seg.shape[0], LANES)) for s in range(subs)]


def select(seg, rows):
    total = seg[0] * rows[0]
    for s in range(1, len(rows)):
        total = total + seg[s] * rows[s]
    return total


def mask_of(seg):
    mask = seg[0]
    for other in seg[1:]:
        mask = mask + other
    return mask


def sums(seg, field):
    return [jnp.sum(field * g, axis=0, keepdims=True) for g in seg]


def moments(total, count, subs):
    average = [total[s] / count[s] for s in range(subs)]
    inverse = [
        lax.rsqrt(total[subs + s] / count[s] - average[s] * average[s] + EPS) for s in range(subs)
    ]
    return average, inverse


def silu_and_slope(norm):
    sigmoid = jax.nn.sigmoid(norm)
    return norm * sigmoid, sigmoid * (1.0 + norm * (1.0 - sigmoid))


def shifted(source, shift, value):
    if shift == 4:
        return value
    rows = value.shape[0]
    at = lax.broadcasted_iota(jnp.int32, (rows, rows), 1)
    move = jnp.where(at == source[:, shift : shift + 1], 1.0, 0.0).astype(BF16)
    return dot(move, value).astype(BF16)


def put_rows(ref, rows):
    for n, row in enumerate(rows):
        ref[n : n + 1, :] = row


def put_sums(ref, rows, first=0):
    for n, row in enumerate(rows):
        ref[0, first + n : first + n + 1, :] = row


def fan_out(ref):
    block = ref[0]
    for b in range(1, ref.shape[0]):
        ref[b] = block


def whole_tiles(rows):
    return -(-rows // 8) * 8


def block_lanes(k):
    return slice(k * LANES, (k + 1) * LANES)


def row_list(block, first, count):
    return [block[n : n + 1] for n in range(first, first + count)]


def local(
    block_input,
    first_reduce,
    first_spatial,
    first_expand,
    first_shortcut,
    second_reduce,
    second_spatial,
    second_expand,
    first_mid_gain,
    first_mid_bias,
    first_wide_gain,
    first_wide_bias,
    second_mid_gain,
    second_mid_bias,
    second_wide_gain,
    second_wide_bias,
    subnet_widths,
    subnet_ids,
    crop_sides,
    cotangent,
):
    nb, nc = lax.axis_size("batch"), lax.axis_size("chan")
    spread = nb // nc
    crops, side = block_input.shape[0], block_input.shape[1]
    geo = Geometry(crops, side)
    px = geo.pixels
    subs = subnet_widths.shape[0]
    me, ber = lax.axis_index("chan"), lax.axis_index("batch")
    mid = first_reduce.shape[1]
    wide = first_shortcut.shape[1]
    part_in = block_input.shape[3]
    whole_mid = nc * mid
    wide_blocks = wide // LANES

    def chan_swap(x, r):
        return lax.ppermute(x, "chan", [(i, i ^ r) for i in range(nc)])

    def slots_of(x):
        return [x] + [chan_swap(x, r) for r in range(1, nc)]

    def swap_slots(x):
        return [x[0]] + [chan_swap(x[r], r) for r in range(1, nc)]

    def to_batch(x):
        return lax.all_to_all(x, "batch", 0, 0, tiled=True)

    def to_all(x):
        return lax.all_to_all(x, ALL, 0, 0, tiled=True)

    turn = []
    for zc in range(nc):
        for j in range(spread):
            for c in range(nc):
                turn.append(((zc * spread + j) * nc + c, (c * spread + j) * nc + zc))

    def turn_share(x):
        return lax.ppermute(x, ALL, turn)

    s_rows, e_cols, r2_rows = first_spatial.shape[2], first_expand.shape[1], second_reduce.shape[0]
    in_rows, part_in = first_reduce.shape[0], block_input.shape[3]
    early = 2

    def prepare_kernel(
        p_ref, x_ref, pick_ref, r1_ref, s1_ref, e1_ref, sc_ref, r2_ref, s2_ref, e2_ref,
        entry_ref, first_out, later_out, turn_out, mine_out, s2_out,
    ):
        picked = pick_ref[...]
        for k in range(4):

            def store(first, rows):
                entry_ref[k, first : first + rows.shape[0], :] = rows

            geo.pack(picked, lambda i, j: x_ref[2 * i + k // 2, 2 * j + k % 2], store)
        r1, s1 = r1_ref[...].astype(BF16), s1_ref[...].astype(BF16)
        for b in range(nb):
            first_out[b, 0:in_rows] = r1
            first_out[b, in_rows:] = s1[: early * s_rows]
            later_out[b] = s1[early * s_rows :]
        s2_out[...] = s2_ref[...].astype(BF16)
        turn_out[0:e_cols] = e1_ref[...].T.astype(BF16)
        turn_out[e_cols : e_cols + r2_rows] = r2_ref[...].astype(BF16)
        turn_out[e_cols + r2_rows :] = e2_ref[...].T.astype(BF16)
        for k in range(wide_blocks):
            mine_out[k * in_rows : (k + 1) * in_rows] = sc_ref[:, block_lanes(k)].astype(BF16)

    def gather_batch(x):
        return lax.all_gather(x, "batch", axis=0, tiled=False)

    place = jnp.stack([me, ber]).astype(jnp.int32)
    pick_large = jnp.asarray(geo.pick, BF16)
    b_rows, turn_rows = e_cols + r2_rows + wide_blocks * in_rows, 2 * e_cols + r2_rows
    entry, first, later, turned, mine, s2_rows = call(
        prepare_kernel,
        (
            struct((4, px, part_in), BF16),
            struct((nb, in_rows + early * s_rows, mid), BF16),
            struct((nb, (9 - early) * s_rows, mid), BF16),
            struct((turn_rows, mid), BF16),
            struct((wide_blocks * in_rows, mid), BF16),
            struct((9 * s_rows, mid), BF16),
        ),
        place, block_input.transpose(1, 2, 0, 3), pick_large, first_reduce, first_spatial.reshape(9 * s_rows, mid),
        first_expand, first_shortcut, second_reduce, second_spatial.reshape(9 * s_rows, mid), second_expand,
    )
    entry = lax.all_gather(entry, "chan", axis=0, tiled=False)
    entries = [part(entry, (None, 4, px, part_in), (c, 0, 0, 0)) for c in range(nc)]
    first, later, turned = to_batch(first), to_batch(later), turn_share(turned)
    r1_w = part(first, (nb, in_rows, mid), (0, 0, 0))

    def shares_kernel(p_ref, turned_ref, mine_ref, s2_ref, b_out, c_out):
        b_out[0 : e_cols + r2_rows] = turned_ref[0 : e_cols + r2_rows]
        b_out[e_cols + r2_rows :] = mine_ref[...]
        c_out[0:e_cols] = turned_ref[e_cols + r2_rows :]
        c_out[e_cols:] = s2_ref[...]

    b_share, c_share = call(
        shares_kernel,
        (struct((b_rows, mid), BF16), struct((e_cols + 9 * s_rows, mid), BF16)),
        place, turned, mine, s2_rows, after=[first],
    )
    group_b, group_c = gather_batch(b_share), gather_batch(c_share)
    e1_w = part(group_b, (nb, e_cols, mid), (0, 0, 0))
    r2_w = part(group_b, (nb, r2_rows, mid), (0, e_cols // r2_rows, 0))
    sc_w = part(group_b, (nb, wide_blocks * in_rows, mid), (0, (e_cols + r2_rows) // (wide_blocks * in_rows), 0))
    e2_w = part(group_c, (nb, e_cols, mid), (0, 0, 0))

    def spatial_weight(x, at):
        rows, per = s_rows, spread
        if s_rows % 16:
            x = x[:, at:].reshape(nc, spread, 9, s_rows, mid).transpose(0, 2, 1, 3, 4)
            x, at, rows, per = x.reshape(nc, 9 * mid, mid), 0, mid, 1
        return [part(x, (x.shape[0], rows, mid), (0, at // rows + tap, 0)) for tap in range(9)], per

    if s_rows % 16:
        s1_w = spatial_weight(jnp.concatenate([first[:, in_rows:], later], axis=1), 0)
    else:
        one, two = spatial_weight(first, in_rows), spatial_weight(later, -early * s_rows)
        s1_w = one[0][:early] + two[0][early:], spread
    s2_w = spatial_weight(group_c, e_cols)

    start = ber * crops
    sides = lax.dynamic_slice_in_dim(crop_sides, start, crops)
    ids = lax.dynamic_slice_in_dim(subnet_ids, start, crops)
    labels = jnp.arange(8, dtype=jnp.int32)
    member_all = (subnet_ids[None, :] == labels[:subs, None]).astype(F32)
    halves = crop_sides // 2
    count_full = jnp.sum(member_all * (crop_sides * crop_sides).astype(F32)[None, :], axis=1)
    count_half = jnp.sum(member_all * (halves * halves).astype(F32)[None, :], axis=1)
    counts = jnp.broadcast_to(
        jnp.concatenate([count_half, count_full, jnp.ones((8 - 2 * subs,), F32)])[:, None], (8, LANES)
    )
    pick = jnp.asarray(geo.rows[:, 0:1] == np.arange(crops)[None, :])
    side_row = jnp.sum(jnp.where(pick, sides[None, :], 0), axis=1, keepdims=True)
    id_row = jnp.sum(jnp.where(pick, ids[None, :], 0), axis=1, keepdims=True)
    row_i, row_j = jnp.asarray(geo.rows[:, 1:2]), jnp.asarray(geo.rows[:, 2:3])
    own = id_row == labels[None, :]
    seg_half = (own & (row_i < side_row // 2) & (row_j < side_row // 2)).astype(F32)
    seg_full = jnp.stack(
        [
            (own & (2 * row_i + p < side_row) & (2 * row_j + q < side_row)).astype(F32)
            for p in range(2)
            for q in range(2)
        ]
    )
    channel = jnp.arange(whole_mid, dtype=jnp.int32).reshape(nc, 1, mid)
    limits = jnp.concatenate([subnet_widths, jnp.zeros((8 - subs,), jnp.int32)])
    active = (channel < limits[None, :, None]).astype(F32)
    source = jnp.asarray(geo.source)
    own_params = jnp.concatenate([first_mid_gain, first_mid_bias, second_mid_gain, second_mid_bias], axis=0)
    params = jnp.stack(slots_of(own_params))

    def norm_slots(p_ref, raw, st_ref, par_ref, active_ref, seg, count, which, put, keep_slot):
        block, layer = which
        chan = p_ref[0]
        for r in range(nc):
            ch = chan ^ r
            total = st_ref[ch]
            for b in range(1, nb):
                total = total + st_ref[b * nc + ch]
            average, inverse = moments(row_list(total, 0, 2 * subs), count, subs)
            gain = par_ref[r, 4 * block + layer : 4 * block + layer + 1, :]
            bias = par_ref[r, 4 * block + 2 + layer : 4 * block + 3 + layer, :]
            act_rows = row_list(active_ref[ch], 0, subs)
            xhat = (raw(r).astype(F32) - select(seg, average)) * select(seg, inverse)
            keep = select(seg, act_rows)
            value, slope = silu_and_slope(gain * xhat + bias)
            put(r, (value * keep).astype(BF16))
            keep_slot(r, xhat, slope * keep, inverse)

    def send_sums(st_ref, seg, raw):
        value = raw.astype(F32)
        put_sums(st_ref, sums(seg, value) + sums(seg, value * value))
        fan_out(st_ref)

    every = nb * nc

    def joined(ref, *at):
        return jnp.concatenate([ref[(*at, r)] for r in range(nc)], axis=1)

    def block_rows(p_ref, ref, r):
        return jnp.concatenate([ref[(p_ref[0] ^ r) * spread + j] for j in range(spread)], axis=0)

    def joined_weight(p_ref, ref):
        return jnp.concatenate([block_rows(p_ref, ref, r) for r in range(nc)], axis=1)

    def tap_weight(p_ref, ref, per):
        return jnp.concatenate([ref[(p_ref[0] ^ r) * per + j] for r in range(nc) for j in range(per)], axis=0)

    def reduce_rows(ref, c):
        return jnp.concatenate([ref[c * spread + j] for j in range(spread)], axis=0)

    def shortcut_rows(ref, c):
        return jnp.concatenate(
            [
                jnp.concatenate(
                    [ref[c * spread + j, k * in_rows : (k + 1) * in_rows, :] for k in range(wide_blocks)], axis=1
                )
                for j in range(spread)
            ],
            axis=0,
        )

    def reduce_kernel(p_ref, e0, e1_, e2_, e3, w_ref, seg_ref, raw_ref, st_ref):
        w = jnp.concatenate([reduce_rows(w_ref, c) for c in range(nc)], axis=0)
        rows = [jnp.zeros((1, LANES), F32)] * (2 * subs)
        for k in range(4):
            seg = columns_of(seg_ref[k], subs)
            mask = mask_of(seg)
            raw = (dot(jnp.concatenate([e[k] for e in (e0, e1_, e2_, e3)], axis=1), w) * mask).astype(BF16)
            raw_ref[k] = raw
            value = raw.astype(F32)
            new = sums(seg, value) + sums(seg, value * value)
            rows = [a + b for a, b in zip(rows, new)]
        put_sums(st_ref, rows)
        fan_out(st_ref)

    def short_kernel(p_ref, e0, e1_, e2_, e3, w_ref, segh_ref, out_ref):
        w = jnp.concatenate([shortcut_rows(w_ref, c) for c in range(nc)], axis=0)
        got = dot(jnp.concatenate([e[...] for e in (e0, e1_, e2_, e3)], axis=1), w)
        out_ref[...] = got * jnp.sum(segh_ref[...], axis=1, keepdims=True)

    def spatial_one_kernel(
        p_ref, r0, r1_, r2_, r3, st_ref, par_ref, act_ref, segf_ref, segh_ref, cnt_ref, src_ref, *rest
    ):
        w_refs, (out_ref, xhat_ref, slope_ref, inv_ref, raw_ref, sto_ref) = rest[:9], rest[9:]
        refs = (r0, r1_, r2_, r3)
        count = row_list(cnt_ref[...], subs, subs)
        for k in range(4):
            seg = columns_of(segf_ref[k], subs)

            def put(r, value):
                out_ref[k, r] = value

            def keep_slot(r, xhat, slope, inverse):
                xhat_ref[r, k] = xhat.astype(BF16)
                slope_ref[r, k] = slope.astype(BF16)
                if k == 0 and r == 0:
                    put_rows(inv_ref, inverse)

            norm_slots(
                p_ref, lambda r: refs[r][k], st_ref, par_ref, act_ref, seg, count, (0, 0), put, keep_slot
            )
        src = src_ref[...]
        total = jnp.zeros((px, mid), F32)
        for tap in range(9):
            plane, shift = STRIDED_TAPS[tap]
            total = total + dot(shifted(src, shift, joined(out_ref, plane)), tap_weight(p_ref, w_refs[tap], s1_w[1]))
        raw = total.astype(BF16)
        raw_ref[...] = raw
        send_sums(sto_ref, columns_of(segh_ref[...], subs), raw)

    def mid_inputs(raws, st):
        return (*raws, st, params, active, seg_half, counts)

    def mid_outs():
        return (
            struct((nc, px, mid), BF16),
            struct((nc, px, mid)),
            struct((nc, px, mid)),
            struct((8, mid)),
        )

    def mid_part(which, p_ref, refs, st_ref, par_ref, act_ref, segh_ref, cnt_ref, out_ref, xhat_ref, slope_ref, inv_ref):
        seg = columns_of(segh_ref[...], subs)

        def put(r, value):
            out_ref[r] = value

        def keep_slot(r, xhat, slope, inverse):
            xhat_ref[r] = xhat
            slope_ref[r] = slope
            if r == 0:
                put_rows(inv_ref, inverse)

        norm_slots(
            p_ref, lambda r: refs[r][...], st_ref, par_ref, act_ref, seg,
            row_list(cnt_ref[...], 0, subs), which, put, keep_slot,
        )
        return seg

    def wide_sums(st_ref, seg, fields):
        for k in range(wide_blocks):
            rows = fields(k)
            put_sums(st_ref, rows, k * len(rows))
        fan_out(st_ref)

    def expand_one_kernel(
        p_ref, r0, r1_, r2_, r3, st_ref, par_ref, act_ref, segh_ref, cnt_ref, w_ref, short_ref,
        out_ref, xhat_ref, slope_ref, inv_ref, pre_ref, sto_ref,
    ):
        seg = mid_part(
            (0, 1), p_ref, (r0, r1_, r2_, r3), st_ref, par_ref, act_ref, segh_ref, cnt_ref,
            out_ref, xhat_ref, slope_ref, inv_ref,
        )
        pre_ref[...] = dot_nt(joined(out_ref), joined_weight(p_ref, w_ref))

        def fields(k):
            a, b = pre_ref[:, block_lanes(k)], short_ref[:, block_lanes(k)]
            return sums(seg, a) + sums(seg, a * a) + sums(seg, b) + sums(seg, b * b)

        wide_sums(sto_ref, seg, fields)

    def summed(st_ref, k=0, rows=2 * subs):
        total = st_ref[0, k * rows : (k + 1) * rows, :]
        for b in range(1, nb):
            total = total + st_ref[b, k * rows : (k + 1) * rows, :]
        return total

    def to_slots(slot_refs, value):
        for r in range(nc):
            slot_refs[r][...] = value[:, r * mid : (r + 1) * mid].astype(BF16)

    def send_upstream(p_ref, slot_refs, st_ref, seg, back, slope_ref, xhat_ref):
        for r in range(nc):
            u = (back[:, r * mid : (r + 1) * mid] * slope_ref[r]).astype(BF16)
            slot_refs[r][...] = u
            u = u.astype(F32)
            send_block(p_ref, st_ref, r, sums(seg, u) + sums(seg, u * xhat_ref[r]))

    def send_block(p_ref, st_ref, r, rows):
        block = jnp.concatenate(rows + [jnp.zeros((8 - len(rows), LANES), F32)], axis=0)
        for b in range(nb):
            st_ref[b * nc + (p_ref[0] ^ r)] = block

    def received(refs, *at):
        total = refs[0][at or ...].astype(F32)
        for ref in refs[1:]:
            total = total + ref[at or ...].astype(F32)
        return total

    def all_summed(st_ref):
        total = st_ref[0]
        for b in range(1, every):
            total = total + st_ref[b]
        return total

    def section_kernel(
        p_ref, st_ref, three_ref, short_ref, gain_ref, bias_ref, segh_ref, cnt_ref, w_ref,
        xh3_ref, xhs_ref, out_ref, slope_ref, inv_ref, low_ref, *slot_refs,
    ):
        seg = columns_of(segh_ref[...], subs)
        mask = mask_of(seg)
        count = row_list(cnt_ref[...], 0, subs)
        for k in range(wide_blocks):
            ln = block_lanes(k)
            total = summed(st_ref, k, 4 * subs)
            both = None
            for n, (pre, keep) in enumerate(((three_ref, xh3_ref), (short_ref, xhs_ref))):
                average, inverse = moments(row_list(total, 2 * subs * n, 2 * subs), count, subs)
                xhat = (pre[:, ln] - select(seg, average)) * select(seg, inverse)
                keep[:, ln] = xhat
                for s in range(subs):
                    inv_ref[n * subs + s : n * subs + s + 1, ln] = inverse[s]
                norm = gain_ref[n : n + 1, ln] * xhat + bias_ref[n : n + 1, ln]
                both = norm if both is None else both + norm
            value, slope = silu_and_slope(both)
            value = value * mask
            out_ref[:, ln] = value
            slope_ref[:, ln] = slope * mask
            low_ref[:, ln] = value.astype(BF16)
        to_slots(slot_refs, dot(low_ref[...], joined_weight(p_ref, w_ref)))

    def four_kernel(p_ref, s0, s1_, s2_, s3, segh_ref, raw_ref, sto_ref):
        total = s0[...].astype(F32)
        for ref in (s1_, s2_, s3):
            total = total + ref[...].astype(F32)
        raw = total.astype(BF16)
        raw_ref[...] = raw
        send_sums(sto_ref, columns_of(segh_ref[...], subs), raw)

    def spatial_two_kernel(
        p_ref, r0, r1_, r2_, r3, st_ref, par_ref, act_ref, segh_ref, cnt_ref, src_ref, *rest
    ):
        w_refs, (out_ref, xhat_ref, slope_ref, inv_ref, raw_ref, sto_ref) = rest[:9], rest[9:]
        seg = mid_part(
            (1, 0), p_ref, (r0, r1_, r2_, r3), st_ref, par_ref, act_ref, segh_ref, cnt_ref,
            out_ref, xhat_ref, slope_ref, inv_ref,
        )
        src = src_ref[...]
        total = jnp.zeros((px, mid), F32)
        whole = joined(out_ref)
        for tap in range(9):
            total = total + dot(shifted(src, tap, whole), tap_weight(p_ref, w_refs[tap], s2_w[1]))
        raw = total.astype(BF16)
        raw_ref[...] = raw
        send_sums(sto_ref, seg, raw)

    def expand_two_kernel(
        p_ref, r0, r1_, r2_, r3, st_ref, par_ref, act_ref, segh_ref, cnt_ref, w_ref,
        out_ref, xhat_ref, slope_ref, inv_ref, pre_ref, sto_ref,
    ):
        seg = mid_part(
            (1, 1), p_ref, (r0, r1_, r2_, r3), st_ref, par_ref, act_ref, segh_ref, cnt_ref,
            out_ref, xhat_ref, slope_ref, inv_ref,
        )
        pre_ref[...] = dot_nt(joined(out_ref), joined_weight(p_ref, w_ref))

        def fields(k):
            a = pre_ref[:, block_lanes(k)]
            return sums(seg, a) + sums(seg, a * a)

        wide_sums(sto_ref, seg, fields)

    def final_kernel(
        p_ref, st_ref, pre_ref, section_ref, cot_ref, gain_ref, bias_ref, segh_ref, cnt_ref, pick_ref,
        out_ref, grad_ref, xhat_ref, inv_ref, sto_ref,
    ):
        seg = columns_of(segh_ref[...], subs)
        mask = mask_of(seg)
        count = row_list(cnt_ref[...], 0, subs)
        picked = pick_ref[...]
        for k in range(wide_blocks):
            ln = block_lanes(k)
            average, inverse = moments(row_list(summed(st_ref, k), 0, 2 * subs), count, subs)
            xhat = (pre_ref[:, ln] - select(seg, average)) * select(seg, inverse)
            xhat_ref[:, ln] = xhat
            for s in range(subs):
                inv_ref[s : s + 1, ln] = inverse[s]
            both = gain_ref[:, ln] * xhat + bias_ref[:, ln] + section_ref[:, ln]
            value, slope = silu_and_slope(both)
            value = value * mask

            def place_out(i, j, first, rows):
                out_ref[i, j, first : first + rows.shape[0], ln] = rows

            geo.unpack(lambda first, count: value[first : first + count], place_out)
            parts = []
            geo.pack(picked, lambda i, j: cot_ref[i, j, :, ln], lambda first, rows: parts.append(rows))
            grad = jnp.concatenate(parts, axis=0).astype(F32) * mask * slope
            grad_ref[:, ln] = grad
            put_sums(sto_ref, sums(seg, grad) + sums(seg, grad * xhat), k * 2 * subs)
        fan_out(sto_ref)

    def norm_back(total, at, gain, inverse, u, xhat, seg, count):
        g = [total[s : s + 1] / count[s] for s in range(subs)]
        x = [total[at + s : at + s + 1] / count[s] for s in range(subs)]
        scale = select(seg, [gain * row for row in inverse])
        return (scale * (u - (select(seg, g) + xhat * select(seg, x)))).astype(BF16)

    def put_param_grads(ref, ln, total, pairs):
        for n, first in enumerate(pairs):
            row = total[first : first + 1]
            for s in range(1, subs):
                row = row + total[first + s : first + s + 1]
            ref[n : n + 1, ln] = row

    def back_six_kernel(
        p_ref, st_ref, u_ref, xhat_ref, inv_ref, gain_ref, segh_ref, cnt_ref, w_ref, slope_ref, xh5_ref, low_ref, par_ref, sto_ref, *slot_refs
    ):
        seg = columns_of(segh_ref[...], subs)
        count = row_list(cnt_ref[...], 0, subs)
        for k in range(wide_blocks):
            ln = block_lanes(k)
            total = summed(st_ref, k)
            put_param_grads(par_ref, ln, total, (subs, 0))
            low_ref[:, ln] = norm_back(
                total, subs, gain_ref[:, ln], row_list(inv_ref[:, ln], 0, subs), u_ref[:, ln], xhat_ref[:, ln], seg, count
            )
        send_upstream(p_ref, slot_refs, sto_ref, seg, dot(low_ref[...], joined_weight(p_ref, w_ref)), slope_ref, xh5_ref)

    def own_gain(ref, which):
        block, layer = which
        return ref[0, 4 * block + layer : 4 * block + layer + 1, :]

    def back_own(st_ref, u_refs, xhat_ref, inv_ref, params_ref, which, segh_ref, cnt_ref, par_ref):
        seg = columns_of(segh_ref[...], subs)
        total = all_summed(st_ref)
        put_param_grads(par_ref, slice(0, LANES), total, (subs, 0))
        return seg, norm_back(
            total, subs, own_gain(params_ref, which), row_list(inv_ref[...], 0, subs), received(u_refs), xhat_ref[...],
            seg, row_list(cnt_ref[...], 0, subs),
        )

    def back_spatial_kernel(which, taps, order, per, planes):
        def kernel(
            p_ref, st_ref, u0, u1, u2, u3, xhat_ref, inv_ref, params_ref, segh_ref, cnt_ref, src_ref,
            slope_ref, xhats_ref, segs_ref, *rest
        ):
            w_refs, (cols_ref, par_ref, sto_ref, *slot_refs) = rest[:9], rest[9:]
            _, low = back_own(
                st_ref, (u0, u1, u2, u3), xhat_ref, inv_ref, params_ref, which, segh_ref, cnt_ref, par_ref
            )
            src = src_ref[...]
            rows = [None] * nc
            back = None
            for n, tap in enumerate(order):
                plane, shift = taps[tap]
                g = shifted(src, 8 - shift, low)
                cols_ref[:, n * mid : (n + 1) * mid] = g
                new = dot_nt(g, tap_weight(p_ref, w_refs[tap], per))
                back = new if back is None else back + new
                if n < 8 and taps[order[n + 1]][0] == plane:
                    continue
                seg = columns_of(segs_ref[plane], subs)
                for r in range(nc):
                    u = (back[:, r * mid : (r + 1) * mid] * slope_ref[r, plane].astype(F32)).astype(BF16)
                    slot_refs[r][plane] = u
                    u = u.astype(F32)
                    got = sums(seg, u) + sums(seg, u * xhats_ref[r, plane].astype(F32))
                    rows[r] = got if rows[r] is None else [a + b for a, b in zip(rows[r], got)]
                back = None
            for r in range(nc):
                send_block(p_ref, sto_ref, r, rows[r])

        return kernel

    def back_plain_kernel(which):
        def kernel(p_ref, st_ref, u0, u1, u2, u3, xhat_ref, inv_ref, params_ref, segh_ref, cnt_ref, low_ref, par_ref):
            _, low_ref[...] = back_own(
                st_ref, (u0, u1, u2, u3), xhat_ref, inv_ref, params_ref, which, segh_ref, cnt_ref, par_ref
            )

        return kernel

    def back_section_kernel(
        p_ref, g0, g1, g2, g3, w_ref, grad_ref, slope_ref, xh3_ref, xhs_ref, segh_ref,
        whole_ref, u_ref, sto_ref,
    ):
        for r, ref in enumerate((g0, g1, g2, g3)):
            whole_ref[r] = ref[...]
        u_ref[...] = dot_nt(joined(whole_ref), joined_weight(p_ref, w_ref))
        seg = columns_of(segh_ref[...], subs)
        for k in range(wide_blocks):
            ln = block_lanes(k)
            u = (u_ref[:, ln] + grad_ref[:, ln]) * slope_ref[:, ln]
            u_ref[:, ln] = u
            rows = sums(seg, u) + sums(seg, u * xh3_ref[:, ln]) + sums(seg, u * xhs_ref[:, ln])
            put_sums(sto_ref, rows, k * 3 * subs)
        fan_out(sto_ref)

    def back_wide_kernel(
        p_ref, st_ref, u_ref, xh3_ref, xhs_ref, inv_ref, gain_ref, segh_ref, cnt_ref, w_ref, slope_ref, xh2_ref,
        three_ref, short_ref, par_ref, sto_ref, *slot_refs,
    ):
        seg = columns_of(segh_ref[...], subs)
        count = row_list(cnt_ref[...], 0, subs)
        for k in range(wide_blocks):
            ln = block_lanes(k)
            total = summed(st_ref, k, 3 * subs)
            put_param_grads(par_ref, ln, total, (subs, 2 * subs, 0))
            u = u_ref[:, ln]
            inverse = inv_ref[:, ln]
            three_ref[:, ln] = norm_back(
                total, subs, gain_ref[0:1, ln], row_list(inverse, 0, subs), u, xh3_ref[:, ln], seg, count
            )
            short_ref[:, ln] = norm_back(
                total, 2 * subs, gain_ref[1:2, ln], row_list(inverse, subs, subs), u, xhs_ref[:, ln], seg, count
            )
        send_upstream(p_ref, slot_refs, sto_ref, seg, dot(three_ref[...], joined_weight(p_ref, w_ref)), slope_ref, xh2_ref)

    def back_one_kernel(
        p_ref, st_ref, u0, u1, u2, u3, xhat_ref, inv_ref, params_ref, segf_ref, cnt_ref, w_ref, short_ref, sc_ref,
        low_ref, par_ref, *slot_refs,
    ):
        count = row_list(cnt_ref[...], subs, subs)
        total = all_summed(st_ref)
        put_param_grads(par_ref, slice(0, LANES), total, (subs, 0))
        for k in range(4):
            seg = columns_of(segf_ref[k], subs)
            low_ref[k] = norm_back(
                total, subs, own_gain(params_ref, (0, 0)), row_list(inv_ref[...], 0, subs),
                received((u0, u1, u2, u3), k), xhat_ref[k].astype(F32), seg, count,
            )
        for r in range(nc):
            w = reduce_rows(w_ref, p_ref[0] ^ r)
            for k in range(4):
                got = dot_nt(low_ref[k], w)
                if k == 0:
                    got = got + dot_nt(short_ref[...], shortcut_rows(sc_ref, p_ref[0] ^ r))
                slot_refs[r][k] = got.astype(BF16)

    def input_kernel(p_ref, a_ref, b_ref, c_ref, segf_ref, out_ref):
        for k in range(4):
            mask = jnp.sum(segf_ref[k], axis=1, keepdims=True)
            total = a_ref[k].astype(F32) + b_ref[k].astype(F32) + c_ref[k].astype(F32)
            total = total * mask

            def place_out(i, j, first, rows):
                out_ref[2 * i + k // 2, 2 * j + k % 2, first : first + rows.shape[0], :] = rows

            geo.unpack(lambda first, count: total[first : first + count], place_out)

    def put_expand(p_ref, out_ref, at, grad_ref, act_ref):
        for k in range(nc):
            got = dot_tn(grad_ref[...], act_ref[p_ref[0] ^ k]).astype(BF16)
            for j in range(spread):
                out_ref[k * spread + j, at : at + e_cols, :] = got[j * e_cols : (j + 1) * e_cols]

    def put_spatial(out_ref, at, k, taps, got):
        for j in range(spread):
            for n, tap in enumerate(taps):
                first = at + tap * s_rows
                out_ref[k * spread + j, first : first + s_rows, :] = got[
                    j * s_rows : (j + 1) * s_rows, n * mid : (n + 1) * mid
                ]

    def grads_two_kernel(p_ref, six_ref, act5_ref, act4_ref, cols_ref, out_ref):
        put_expand(p_ref, out_ref, 0, six_ref, act5_ref)
        for k in range(nc):
            got = dot_tn(act4_ref[p_ref[0] ^ k], cols_ref[...]).astype(BF16)
            put_spatial(out_ref, e_cols, k, range(9), got)

    def grads_mixed_kernel(p_ref, low_ref, four_ref, three_ref, act2_ref, e0, e1_, e2_, e3, short_ref, out_ref):
        for k in range(nc):
            got = dot_tn(low_ref[...], four_ref[p_ref[0] ^ k]).astype(BF16)
            for j in range(spread):
                out_ref[k * spread + j, 0:r2_rows, :] = got[j * r2_rows : (j + 1) * r2_rows]
        put_expand(p_ref, out_ref, r2_rows, three_ref, act2_ref)
        first = r2_rows + e_cols
        for c, entry_ref in enumerate((e0, e1_, e2_, e3)):
            got = dot_tn(entry_ref[...], short_ref[...]).astype(BF16)
            for j in range(spread):
                for k in range(wide_blocks):
                    out_ref[c * spread + j, first + k * in_rows : first + (k + 1) * in_rows, :] = got[
                        j * in_rows : (j + 1) * in_rows, block_lanes(k)
                    ]

    def grads_reduce_kernel(p_ref, e0, e1_, e2_, e3, grad_ref, out_ref):
        for c, entry_ref in enumerate((e0, e1_, e2_, e3)):
            got = dot_tn(entry_ref[0], grad_ref[0])
            for k in range(1, 4):
                got = got + dot_tn(entry_ref[k], grad_ref[k])
            for j in range(spread):
                out_ref[c * spread + j] = got[j * in_rows : (j + 1) * in_rows].astype(BF16)

    def grads_one_kernel(p_ref, act_ref, cols_ref, out_ref):
        for k in range(nc):
            first = 0
            for plane in range(4):
                taps = [t for t in STRIDED_ORDER if STRIDED_TAPS[t][0] == plane]
                lanes = slice(first * mid, (first + len(taps)) * mid)
                got = dot_tn(act_ref[plane, p_ref[0] ^ k], cols_ref[:, lanes]).astype(BF16)
                put_spatial(out_ref, 0, k, taps, got)
                first += len(taps)

    def mine(p_ref, pair_ref, got_ref):
        return pair_ref[lax.rem(p_ref[1], 2)].astype(F32) + got_ref[...].astype(F32)

    def mine_kernel(p_ref, pair_ref, got_ref, out_ref):
        out_ref[...] = mine(p_ref, pair_ref, got_ref)

    def total_kernel(p_ref, *refs):
        total = refs[0][...].astype(F32)
        for ref in refs[1:-1]:
            total = total + ref[...].astype(F32)
        refs[-1][...] = total

    def turn_kernel(p_ref, two_ref, two_got, mixed_ref, mixed_got, turn_out, s2_out, sc_out):
        two, mixed = mine(p_ref, two_ref, two_got), mine(p_ref, mixed_ref, mixed_got)
        turn_out[0:e_cols] = mixed[r2_rows : r2_rows + e_cols].astype(BF16)
        turn_out[e_cols : e_cols + r2_rows] = mixed[0:r2_rows].astype(BF16)
        turn_out[e_cols + r2_rows :] = two[0:e_cols].astype(BF16)
        s2_out[...] = two[e_cols:]
        first = r2_rows + e_cols
        for k in range(wide_blocks):
            sc_out[:, block_lanes(k)] = mixed[first + k * in_rows : first + (k + 1) * in_rows]

    def param_kernel(p_ref, one, two, wide_one, four, five, six, g1, b1, gw1, bw1, g2, b2, gw2, bw2):
        for first, second, gain, bias in ((one, two, g1, b1), (four, five, g2, b2)):
            for n, ref in enumerate((first, second)):
                gain[n : n + 1, :] = ref[0:1, :]
                bias[n : n + 1, :] = ref[1:2, :]
        gw1[...] = wide_one[0:2, :]
        bw1[0:1, :] = wide_one[2:3, :]
        bw1[1:2, :] = wide_one[2:3, :]
        gw2[...] = six[0:1, :]
        bw2[...] = six[1:2, :]

    def own_kernel(p_ref, turned_ref, e1_out, r2_out, e2_out):
        e1_out[...] = turned_ref[0:e_cols].astype(F32).T
        r2_out[...] = turned_ref[e_cols : e_cols + r2_rows].astype(F32)
        e2_out[...] = turned_ref[e_cols + r2_rows :].astype(F32).T

    def to_owners(shares):
        rows = shares.shape[1]
        groups = [list(range(first, nb, 2)) for first in range(2)]
        pair = lax.psum_scatter(
            shares.reshape(nb // 2, 2 * rows, mid), "batch", scatter_dimension=0, axis_index_groups=groups, tiled=False
        ).reshape(2, rows, mid)
        send = lax.dynamic_index_in_dim(pair, 1 - ber % 2, 0, False)
        return pair, lax.ppermute(send, "batch", [(i, i ^ 1) for i in range(nb)])

    st_mid, st_own, st_wide = (
        struct((every, 8, LANES)),
        struct((nb, 8, LANES)),
        struct((nb, whole_tiles(2 * subs * wide_blocks), LANES)),
    )
    matmul = 2 * px * whole_mid * wide
    mid_slots = [struct((px, mid), BF16)] * nc
    half = side // 2

    raw_one, st = call(
        reduce_kernel, (struct((4, px, mid), BF16), st_mid), place, *entries, r1_w, seg_full, flops=4 * matmul
    )
    (st,) = call(total_kernel, (st_mid,), place, st, after=[later])
    raws, st = slots_of(raw_one), to_all(st)
    act_one, xhat_one, slope_one, inv_one, raw_two, st = call(
        spatial_one_kernel,
        (
            struct((4, nc, px, mid), BF16),
            struct((nc, 4, px, mid), BF16),
            struct((nc, 4, px, mid), BF16),
            struct((8, mid)),
            struct((px, mid), BF16),
            st_mid,
        ),
        place, *raws, st, params, active, seg_full, seg_half, counts, source, *s1_w[0],
        flops=10 * matmul,
    )
    shorts = [part(entry, (None, None, px, part_in), (c, 0, 0, 0)) for c in range(nc)]
    (pre_short,) = call(short_kernel, (struct((px, wide)),), place, *shorts, sc_w, seg_half, flops=4 * matmul)
    raws, st = slots_of(raw_two), to_all(st)
    act_two, xhat_two, slope_two, inv_two, pre_three, st = call(
        expand_one_kernel,
        (*mid_outs(), struct((px, wide)), struct((nb, whole_tiles(4 * subs * wide_blocks), LANES))),
        place, *mid_inputs(raws, st), e1_w, pre_short,
        flops=2 * matmul,
    )
    xhat_three, xhat_short, section_out, slope_section, inv_wide, section_low, *slots = call(
        section_kernel,
        (
            *[struct((px, wide))] * 4,
            struct((8, wide)),
            struct((px, wide), BF16),
            *mid_slots,
        ),
        place, to_batch(st), pre_three, pre_short, first_wide_gain, first_wide_bias, seg_half, counts, r2_w,
        flops=2 * matmul,
    )

    raw_four, st = call(
        four_kernel, (struct((px, mid), BF16), st_mid), place, *swap_slots(slots), seg_half
    )
    raws, st = slots_of(raw_four), to_all(st)
    act_four, xhat_four, slope_four, inv_four, raw_five, st = call(
        spatial_two_kernel,
        (*mid_outs(), struct((px, mid), BF16), st_mid),
        place, *mid_inputs(raws, st), source, *s2_w[0],
        flops=8 * matmul,
    )
    raws, st = slots_of(raw_five), to_all(st)
    act_five, xhat_five, slope_five, inv_five, pre_six, st = call(
        expand_two_kernel,
        (*mid_outs(), struct((px, wide)), st_wide),
        place, *mid_inputs(raws, st), e2_w,
        flops=2 * matmul,
    )
    gain_six, bias_six = second_wide_gain[None], second_wide_bias[None]
    out_rows, grad_final, xhat_six, inv_six, st = call(
        final_kernel,
        (struct((half, half, crops, wide)), *[struct((px, wide))] * 2, struct((8, wide)), st_wide),
        place, to_batch(st), pre_six, section_out, cotangent.transpose(1, 2, 0, 3), gain_six, bias_six, seg_half, counts,
        pick_large,
    )
    output = out_rows.transpose(2, 0, 1, 3)

    grad_six, par_six, st, *slots = call(
        back_six_kernel,
        (struct((px, wide), BF16), struct((8, wide)), st_mid, *mid_slots),
        place, to_batch(st), grad_final, xhat_six, inv_six, gain_six, seg_half, counts, e2_w, slope_five, xhat_five,
        flops=2 * matmul,
    )

    def own(xhat):
        return part(xhat, (None, *xhat.shape[1:]), (0,) * xhat.ndim)

    raws, st = swap_slots(slots), to_all(st)
    cols_five, par_five, st, *slots = call(
        back_spatial_kernel((1, 1), UNIT_TAPS, list(range(9)), s2_w[1], 1),
        (struct((px, 9 * mid), BF16), struct((8, mid)), st_mid, *[struct((1, px, mid), BF16)] * nc),
        place, st, *raws, own(xhat_five), inv_five, params, seg_half, counts, source, slope_four[:, None],
        xhat_four[:, None], seg_half[None], *s2_w[0],
        flops=8 * matmul,
    )
    raws, st = swap_slots([x.reshape(px, mid) for x in slots]), to_all(st)
    (shares_two,) = call(
        grads_two_kernel, (struct((nb, e_cols + 9 * s_rows, mid), BF16),),
        place, grad_six, act_five, act_four, cols_five, flops=10 * matmul,
    )
    grad_four, par_four = call(
        back_plain_kernel((1, 0)),
        (struct((px, mid), BF16), struct((8, mid))),
        place, st, *raws, own(xhat_four), inv_four, params, seg_half, counts, after=[shares_two],
    )
    whole_grad_four, u_wide, st = call(
        back_section_kernel,
        (struct((nc, px, mid), BF16), struct((px, wide)), struct((nb, whole_tiles(3 * subs * wide_blocks), LANES))),
        place, *slots_of(grad_four), r2_w, grad_final, slope_section, xhat_three, xhat_short, seg_half,
        flops=2 * matmul,
    )

    grad_three, grad_short, par_wide, st, *slots = call(
        back_wide_kernel,
        (
            struct((px, wide), BF16),
            struct((px, wide), BF16),
            struct((8, wide)),
            st_mid,
            *mid_slots,
        ),
        place, to_batch(st), u_wide, xhat_three, xhat_short, inv_wide, first_wide_gain, seg_half, counts, e1_w,
        slope_two, xhat_two,
        flops=2 * matmul,
    )
    raws, st = swap_slots(slots), to_all(st)
    (shares_mixed,) = call(
        grads_mixed_kernel, (struct((nb, b_rows, mid), BF16),),
        place, section_low, whole_grad_four, grad_three, act_two, *shorts, grad_short, flops=8 * matmul,
    )
    owned_two, owned_mixed = to_owners(shares_two), to_owners(shares_mixed)
    cols_two, par_two, st, *slots = call(
        back_spatial_kernel((0, 1), STRIDED_TAPS, STRIDED_ORDER, s1_w[1], 4),
        (struct((px, 9 * mid), BF16), struct((8, mid)), st_mid, *[struct((4, px, mid), BF16)] * nc),
        place, st, *raws, own(xhat_two), inv_two, params, seg_half, counts, source, slope_one, xhat_one, seg_full,
        *s1_w[0],
        flops=8 * matmul, after=[shares_mixed, owned_two[0]],
    )
    raws, st = swap_slots(slots), to_all(st)
    (shares_one,) = call(
        grads_one_kernel, (struct((nb, 9 * s_rows, mid), BF16),), place, act_one, cols_two, flops=8 * matmul
    )
    grad_one, par_one, *slots = call(
        back_one_kernel,
        (struct((4, px, mid), BF16), struct((8, mid)), *[struct((4, px, part_in), BF16)] * nc),
        place, st, *raws, own(xhat_one), inv_one, params, seg_full, counts, r1_w, grad_short, sc_w,
        flops=8 * matmul, after=[shares_one],
    )
    far_first, own_back = chan_swap(slots[3], 1), chan_swap(slots[1], 1)
    far_sum = (slots[2].astype(F32) + far_first.astype(F32)).astype(BF16)
    far_back = chan_swap(far_sum, 2)

    (shares,) = call(
        grads_reduce_kernel, (struct((nb, in_rows, mid), BF16),),
        place, *entries, grad_one, flops=4 * matmul, after=[far_sum, owned_mixed[0]],
    )
    r1_out = jnp.sum(to_batch(shares).astype(F32), axis=0)
    turned, s2_own, sc_own = call(
        turn_kernel,
        (struct((turn_rows, mid), BF16), struct((9 * s_rows, mid)), struct((in_rows, wide))),
        place, *owned_two, *owned_mixed,
    )
    (s1_total,) = call(mine_kernel, (struct((9 * s_rows, mid)),), place, *to_owners(shares_one))
    e1_own, r2_own, e2_own = call(
        own_kernel,
        (struct((mid, e_cols)), struct((r2_rows, mid)), struct((mid, e_cols))),
        place, turn_share(turned),
    )
    mid_pair, wide_pair, wide_row = struct((2, mid)), struct((2, wide)), struct((1, wide))
    own_params_grad = call(
        param_kernel,
        (mid_pair, mid_pair, wide_pair, wide_pair, mid_pair, mid_pair, wide_row, wide_row),
        place, par_one, par_two, par_wide, par_four, par_five, par_six, after=[far_sum],
    )
    outs = (
        output,
        s1_total.reshape(3, 3, s_rows, mid),
        e1_own,
        sc_own,
        r2_own,
        s2_own.reshape(3, 3, s_rows, mid),
        e2_own,
        *own_params_grad[:-2],
        own_params_grad[-2][0],
        own_params_grad[-1][0],
    )
    (input_grad,) = call(
        input_kernel, (struct((side, side, crops, part_in)),), place, slots[0], own_back, far_back, seg_full,
        after=[own_params_grad[0]],
    )
    return outs[:1] + (input_grad.transpose(2, 0, 1, 3), r1_out) + outs[1:]


def solution(mesh):
    placed = (
        P("batch", None, None, "chan"),
        P("batch", "chan"),
        P(None, None, "batch", "chan"),
        P("chan", "batch"),
        P("batch", "chan"),
        P("batch", "chan"),
        P(None, None, "batch", "chan"),
        P("chan", "batch"),
        P(None, "chan"),
        P(None, "chan"),
        P(None, "chan"),
        P(None, "chan"),
        P(None, "chan"),
        P(None, "chan"),
        P("chan"),
        P("chan"),
        P(),
        P(),
        P(),
        P("batch", None, None, "chan"),
    )
    outs = (
        P("batch", None, None, "chan"),
        P("batch", None, None, "chan"),
        P("batch", "chan"),
        P(None, None, "batch", "chan"),
        P("chan", "batch"),
        P("batch", "chan"),
        P("batch", "chan"),
        P(None, None, "batch", "chan"),
        P("chan", "batch"),
        P(None, "chan"),
        P(None, "chan"),
        P(None, "chan"),
        P(None, "chan"),
        P(None, "chan"),
        P(None, "chan"),
        P("chan"),
        P("chan"),
    )
    return jax.shard_map(local, mesh=mesh, in_specs=placed, out_specs=outs, check_vma=False)
```

```python
import jax
import jax.numpy as jnp
import numpy as np
from jax import lax
from jax.experimental import pallas as pl
from jax.experimental.pallas import tpu as pltpu
from jax.sharding import PartitionSpec as P

F32, BF16 = jnp.float32, jnp.bfloat16
EPS = 1e-05
SMALL = 6
LANES = 128
ALL = ("batch", "chan")


class Geometry:
    def __init__(self, crops, side):
        self.crops, self.side = crops, side
        self.half, self.small = side // 2, SMALL // 2
        self.large = [c for c in range(crops) if c % 8 < 2]
        grid = [(i, j) for i in range(self.half) for j in range(self.half)]
        self.common = [at for at in grid if max(at) < self.small]
        self.others = [at for at in grid if max(at) >= self.small]
        rows = [(c, i, j) for i, j in self.common for c in range(crops)]
        rows += [(c, i, j) for i, j in self.others for c in self.large]
        self.cut = len(self.common) * crops
        self.rows = np.array(rows, np.int32)
        self.pixels = len(rows)
        where = {tuple(r): n for n, r in enumerate(rows)}
        source = np.full((self.pixels, 16), -1, np.int32)
        for n, (crop, i, j) in enumerate(rows):
            for shift in range(9):
                source[n, shift] = where.get((crop, i + shift // 3 - 1, j + shift % 3 - 1), -1)
        self.source = source
        self.group = 8
        wanted = len(self.large)
        pick = np.zeros((self.group * wanted, self.group * crops), np.float32)
        for n in range(self.group):
            for m, c in enumerate(self.large):
                pick[n * wanted + m, n * crops + c] = 1.0
        self.pick = pick

    def pack(self, pick, load, store):
        for n, (i, j) in enumerate(self.common):
            store(n * self.crops, load(i, j))
        wanted = len(self.large)
        for n in range(0, len(self.others), self.group):
            rows = jnp.concatenate([load(i, j) for i, j in self.others[n : n + self.group]], axis=0)
            store(self.cut + n * wanted, dot(pick, rows).astype(rows.dtype))

    def unpack(self, load, store):
        for n, (i, j) in enumerate(self.common):
            store(i, j, 0, load(n * self.crops, self.crops))
        wanted = len(self.large)
        for n, (i, j) in enumerate(self.others):
            rows = load(self.cut + n * wanted, wanted)
            store(i, j, 0, jnp.zeros((self.crops, rows.shape[1]), rows.dtype))
            for m in range(0, wanted, 2):
                store(i, j, self.large[m], rows[m : m + 2])


UNIT_TAPS = [(0, tap) for tap in range(9)]
STRIDED_TAPS = [
    (2 * int(r != 1) + int(c != 1), 3 * (0 if r == 0 else 1) + (0 if c == 0 else 1))
    for r in range(3)
    for c in range(3)
]
STRIDED_ORDER = [tap for plane in range(4) for tap in range(9) if STRIDED_TAPS[tap][0] == plane]

SM = pl.BlockSpec(memory_space=pltpu.SMEM)


def struct(shape, dtype=F32):
    return jax.ShapeDtypeStruct(tuple(shape), dtype)


def whole_block(shape, at=None):
    at = at or (0,) * len(shape)
    return pl.BlockSpec(tuple(shape), lambda _: at)


def part(array, shape, at):
    return array, whole_block(shape, at)


def corner(array):
    shape = (1,) * (array.ndim - 2) + (16, LANES) if array.ndim > 1 else array.shape
    return array, whole_block([min(a, b) for a, b in zip(shape, array.shape)], (0,) * array.ndim)


def call(kernel, outs, place, *args, flops=10**8, mib=64, after=()):
    args = [a if isinstance(a, tuple) else (a, whole_block(a.shape)) for a in args]
    moved = sum(int(np.prod([n or 1 for n in b.block_shape])) * a.dtype.itemsize for a, b in args)
    moved += sum(int(np.prod(o.shape)) * o.dtype.itemsize for o in outs)
    used, args = len(args), args + [corner(a) for a in after]

    def body(p_ref, *refs):
        kernel(p_ref, *refs[:used], *refs[len(args) :])

    return pl.pallas_call(
        body,
        grid=(1,),
        out_shape=tuple(outs),
        in_specs=[SM] + [b for _, b in args],
        out_specs=tuple(whole_block(o.shape) for o in outs),
        compiler_params=pltpu.CompilerParams(vmem_limit_bytes=mib * 1024 * 1024),
        cost_estimate=pl.CostEstimate(flops=flops, bytes_accessed=moved, transcendentals=0),
    )(place, *[a for a, _ in args])


def dot(a, b):
    return jnp.dot(a, b, preferred_element_type=F32)


def dot_nt(a, b):
    return lax.dot_general(a, b, (((1,), (1,)), ((), ())), preferred_element_type=F32)


def dot_tn(a, b):
    return lax.dot_general(a, b, (((0,), (0,)), ((), ())), preferred_element_type=F32)


def columns_of(seg, subs):
    return [jnp.broadcast_to(seg[:, s : s + 1], (seg.shape[0], LANES)) for s in range(subs)]


def select(seg, rows):
    total = seg[0] * rows[0]
    for s in range(1, len(rows)):
        total = total + seg[s] * rows[s]
    return total


def mask_of(seg):
    mask = seg[0]
    for other in seg[1:]:
        mask = mask + other
    return mask


def sums(seg, field):
    return [jnp.sum(field * g, axis=0, keepdims=True) for g in seg]


def moments(total, count, subs):
    average = [total[s] / count[s] for s in range(subs)]
    inverse = [
        lax.rsqrt(total[subs + s] / count[s] - average[s] * average[s] + EPS) for s in range(subs)
    ]
    return average, inverse


def silu_and_slope(norm):
    sigmoid = jax.nn.sigmoid(norm)
    return norm * sigmoid, sigmoid * (1.0 + norm * (1.0 - sigmoid))


def shifted(source, shift, value):
    if shift == 4:
        return value
    rows = value.shape[0]
    at = lax.broadcasted_iota(jnp.int32, (rows, rows), 1)
    move = jnp.where(at == source[:, shift : shift + 1], 1.0, 0.0).astype(BF16)
    return dot(move, value).astype(BF16)


def put_rows(ref, rows):
    for n, row in enumerate(rows):
        ref[n : n + 1, :] = row


def put_sums(ref, rows, first=0):
    for n, row in enumerate(rows):
        ref[0, first + n : first + n + 1, :] = row


def fan_out(ref):
    block = ref[0]
    for b in range(1, ref.shape[0]):
        ref[b] = block


def whole_tiles(rows):
    return -(-rows // 8) * 8


def block_lanes(k):
    return slice(k * LANES, (k + 1) * LANES)


def row_list(block, first, count):
    return [block[n : n + 1] for n in range(first, first + count)]


def local(
    block_input,
    first_reduce,
    first_spatial,
    first_expand,
    first_shortcut,
    second_reduce,
    second_spatial,
    second_expand,
    first_mid_gain,
    first_mid_bias,
    first_wide_gain,
    first_wide_bias,
    second_mid_gain,
    second_mid_bias,
    second_wide_gain,
    second_wide_bias,
    subnet_widths,
    subnet_ids,
    crop_sides,
    cotangent,
):
    nb, nc = lax.axis_size("batch"), lax.axis_size("chan")
    spread = nb // nc
    crops, side = block_input.shape[0], block_input.shape[1]
    geo = Geometry(crops, side)
    px = geo.pixels
    subs = subnet_widths.shape[0]
    me, ber = lax.axis_index("chan"), lax.axis_index("batch")
    mid = first_reduce.shape[1]
    wide = first_shortcut.shape[1]
    part_in = block_input.shape[3]
    whole_mid = nc * mid
    wide_blocks = wide // LANES

    def chan_swap(x, r):
        return lax.ppermute(x, "chan", [(i, i ^ r) for i in range(nc)])

    def slots_of(x):
        return [x] + [chan_swap(x, r) for r in range(1, nc)]

    def swap_slots(x):
        return [x[0]] + [chan_swap(x[r], r) for r in range(1, nc)]

    def to_batch(x):
        return lax.all_to_all(x, "batch", 0, 0, tiled=True)

    def to_all(x):
        return lax.all_to_all(x, ALL, 0, 0, tiled=True)

    turn = []
    for zc in range(nc):
        for j in range(spread):
            for c in range(nc):
                turn.append(((zc * spread + j) * nc + c, (c * spread + j) * nc + zc))

    def turn_share(x):
        return lax.ppermute(x, ALL, turn)

    s_rows, e_cols, r2_rows = first_spatial.shape[2], first_expand.shape[1], second_reduce.shape[0]
    in_rows, part_in = first_reduce.shape[0], block_input.shape[3]
    early = 2

    def prepare_kernel(
        p_ref, x_ref, pick_ref, r1_ref, s1_ref, e1_ref, sc_ref, r2_ref, s2_ref, e2_ref,
        entry_ref, first_out, later_out, turn_out, mine_out, s2_out,
    ):
        picked = pick_ref[...]
        for k in range(4):

            def store(first, rows):
                entry_ref[k, first : first + rows.shape[0], :] = rows

            geo.pack(picked, lambda i, j: x_ref[2 * i + k // 2, 2 * j + k % 2], store)
        r1, s1 = r1_ref[...].astype(BF16), s1_ref[...].astype(BF16)
        for b in range(nb):
            first_out[b, 0:in_rows] = r1
            first_out[b, in_rows:] = s1[: early * s_rows]
            later_out[b] = s1[early * s_rows :]
        s2_out[...] = s2_ref[...].astype(BF16)
        turn_out[0:e_cols] = e1_ref[...].T.astype(BF16)
        turn_out[e_cols : e_cols + r2_rows] = r2_ref[...].astype(BF16)
        turn_out[e_cols + r2_rows :] = e2_ref[...].T.astype(BF16)
        for k in range(wide_blocks):
            mine_out[k * in_rows : (k + 1) * in_rows] = sc_ref[:, block_lanes(k)].astype(BF16)

    def gather_batch(x):
        return lax.all_gather(x, "batch", axis=0, tiled=False)

    place = jnp.stack([me, ber]).astype(jnp.int32)
    pick_large = jnp.asarray(geo.pick, BF16)
    b_rows, turn_rows = e_cols + r2_rows + wide_blocks * in_rows, 2 * e_cols + r2_rows
    entry, first, later, turned, mine, s2_rows = call(
        prepare_kernel,
        (
            struct((4, px, part_in), BF16),
            struct((nb, in_rows + early * s_rows, mid), BF16),
            struct((nb, (9 - early) * s_rows, mid), BF16),
            struct((turn_rows, mid), BF16),
            struct((wide_blocks * in_rows, mid), BF16),
            struct((9 * s_rows, mid), BF16),
        ),
        place, block_input.transpose(1, 2, 0, 3), pick_large, first_reduce, first_spatial.reshape(9 * s_rows, mid),
        first_expand, first_shortcut, second_reduce, second_spatial.reshape(9 * s_rows, mid), second_expand,
    )
    entry = lax.all_gather(entry, "chan", axis=0, tiled=False)
    entries = [part(entry, (None, 4, px, part_in), (c, 0, 0, 0)) for c in range(nc)]
    first, later, turned = to_batch(first), to_batch(later), turn_share(turned)
    r1_w = part(first, (nb, in_rows, mid), (0, 0, 0))

    def shares_kernel(p_ref, turned_ref, mine_ref, s2_ref, b_out, c_out):
        b_out[0 : e_cols + r2_rows] = turned_ref[0 : e_cols + r2_rows]
        b_out[e_cols + r2_rows :] = mine_ref[...]
        c_out[0:e_cols] = turned_ref[e_cols + r2_rows :]
        c_out[e_cols:] = s2_ref[...]

    b_share, c_share = call(
        shares_kernel,
        (struct((b_rows, mid), BF16), struct((e_cols + 9 * s_rows, mid), BF16)),
        place, turned, mine, s2_rows, after=[first],
    )
    group_b, group_c = gather_batch(b_share), gather_batch(c_share)
    e1_w = part(group_b, (nb, e_cols, mid), (0, 0, 0))
    r2_w = part(group_b, (nb, r2_rows, mid), (0, e_cols // r2_rows, 0))
    sc_w = part(group_b, (nb, wide_blocks * in_rows, mid), (0, (e_cols + r2_rows) // (wide_blocks * in_rows), 0))
    e2_w = part(group_c, (nb, e_cols, mid), (0, 0, 0))

    def spatial_weight(x, at):
        rows, per = s_rows, spread
        if s_rows % 16:
            x = x[:, at:].reshape(nc, spread, 9, s_rows, mid).transpose(0, 2, 1, 3, 4)
            x, at, rows, per = x.reshape(nc, 9 * mid, mid), 0, mid, 1
        return [part(x, (x.shape[0], rows, mid), (0, at // rows + tap, 0)) for tap in range(9)], per

    if s_rows % 16:
        s1_w = spatial_weight(jnp.concatenate([first[:, in_rows:], later], axis=1), 0)
    else:
        one, two = spatial_weight(first, in_rows), spatial_weight(later, -early * s_rows)
        s1_w = one[0][:early] + two[0][early:], spread
    s2_w = spatial_weight(group_c, e_cols)

    start = ber * crops
    sides = lax.dynamic_slice_in_dim(crop_sides, start, crops)
    ids = lax.dynamic_slice_in_dim(subnet_ids, start, crops)
    labels = jnp.arange(8, dtype=jnp.int32)
    member_all = (subnet_ids[None, :] == labels[:subs, None]).astype(F32)
    halves = crop_sides // 2
    count_full = jnp.sum(member_all * (crop_sides * crop_sides).astype(F32)[None, :], axis=1)
    count_half = jnp.sum(member_all * (halves * halves).astype(F32)[None, :], axis=1)
    counts = jnp.broadcast_to(
        jnp.concatenate([count_half, count_full, jnp.ones((8 - 2 * subs,), F32)])[:, None], (8, LANES)
    )
    pick = jnp.asarray(geo.rows[:, 0:1] == np.arange(crops)[None, :])
    side_row = jnp.sum(jnp.where(pick, sides[None, :], 0), axis=1, keepdims=True)
    id_row = jnp.sum(jnp.where(pick, ids[None, :], 0), axis=1, keepdims=True)
    row_i, row_j = jnp.asarray(geo.rows[:, 1:2]), jnp.asarray(geo.rows[:, 2:3])
    own = id_row == labels[None, :]
    seg_half = (own & (row_i < side_row // 2) & (row_j < side_row // 2)).astype(F32)
    seg_full = jnp.stack(
        [
            (own & (2 * row_i + p < side_row) & (2 * row_j + q < side_row)).astype(F32)
            for p in range(2)
            for q in range(2)
        ]
    )
    channel = jnp.arange(whole_mid, dtype=jnp.int32).reshape(nc, 1, mid)
    limits = jnp.concatenate([subnet_widths, jnp.zeros((8 - subs,), jnp.int32)])
    active = (channel < limits[None, :, None]).astype(F32)
    source = jnp.asarray(geo.source)
    own_params = jnp.concatenate([first_mid_gain, first_mid_bias, second_mid_gain, second_mid_bias], axis=0)
    params = jnp.stack(slots_of(own_params))

    def norm_slots(p_ref, raw, st_ref, par_ref, active_ref, seg, count, which, put, keep_slot):
        block, layer = which
        chan = p_ref[0]
        for r in range(nc):
            ch = chan ^ r
            total = st_ref[ch]
            for b in range(1, nb):
                total = total + st_ref[b * nc + ch]
            average, inverse = moments(row_list(total, 0, 2 * subs), count, subs)
            gain = par_ref[r, 4 * block + layer : 4 * block + layer + 1, :]
            bias = par_ref[r, 4 * block + 2 + layer : 4 * block + 3 + layer, :]
            act_rows = row_list(active_ref[ch], 0, subs)
            xhat = (raw(r).astype(F32) - select(seg, average)) * select(seg, inverse)
            keep = select(seg, act_rows)
            value, slope = silu_and_slope(gain * xhat + bias)
            put(r, (value * keep).astype(BF16))
            keep_slot(r, xhat, slope * keep, inverse)

    def send_sums(st_ref, seg, raw):
        value = raw.astype(F32)
        put_sums(st_ref, sums(seg, value) + sums(seg, value * value))
        fan_out(st_ref)

    every = nb * nc

    def joined(ref, *at):
        return jnp.concatenate([ref[(*at, r)] for r in range(nc)], axis=1)

    def block_rows(p_ref, ref, r):
        return jnp.concatenate([ref[(p_ref[0] ^ r) * spread + j] for j in range(spread)], axis=0)

    def joined_weight(p_ref, ref):
        return jnp.concatenate([block_rows(p_ref, ref, r) for r in range(nc)], axis=1)

    def tap_weight(p_ref, ref, per):
        return jnp.concatenate([ref[(p_ref[0] ^ r) * per + j] for r in range(nc) for j in range(per)], axis=0)

    def reduce_rows(ref, c):
        return jnp.concatenate([ref[c * spread + j] for j in range(spread)], axis=0)

    def shortcut_rows(ref, c):
        return jnp.concatenate(
            [
                jnp.concatenate(
                    [ref[c * spread + j, k * in_rows : (k + 1) * in_rows, :] for k in range(wide_blocks)], axis=1
                )
                for j in range(spread)
            ],
            axis=0,
        )

    def reduce_kernel(p_ref, e0, e1_, e2_, e3, w_ref, seg_ref, raw_ref, st_ref):
        w = jnp.concatenate([reduce_rows(w_ref, c) for c in range(nc)], axis=0)
        rows = [jnp.zeros((1, LANES), F32)] * (2 * subs)
        for k in range(4):
            seg = columns_of(seg_ref[k], subs)
            mask = mask_of(seg)
            raw = (dot(jnp.concatenate([e[k] for e in (e0, e1_, e2_, e3)], axis=1), w) * mask).astype(BF16)
            raw_ref[k] = raw
            value = raw.astype(F32)
            new = sums(seg, value) + sums(seg, value * value)
            rows = [a + b for a, b in zip(rows, new)]
        put_sums(st_ref, rows)
        fan_out(st_ref)

    def short_kernel(p_ref, e0, e1_, e2_, e3, w_ref, segh_ref, out_ref):
        w = jnp.concatenate([shortcut_rows(w_ref, c) for c in range(nc)], axis=0)
        got = dot(jnp.concatenate([e[...] for e in (e0, e1_, e2_, e3)], axis=1), w)
        out_ref[...] = got * jnp.sum(segh_ref[...], axis=1, keepdims=True)

    def spatial_one_kernel(
        p_ref, r0, r1_, r2_, r3, st_ref, par_ref, act_ref, segf_ref, segh_ref, cnt_ref, src_ref, *rest
    ):
        w_refs, (out_ref, xhat_ref, slope_ref, inv_ref, raw_ref, sto_ref) = rest[:9], rest[9:]
        refs = (r0, r1_, r2_, r3)
        count = row_list(cnt_ref[...], subs, subs)
        for k in range(4):
            seg = columns_of(segf_ref[k], subs)

            def put(r, value):
                out_ref[k, r] = value

            def keep_slot(r, xhat, slope, inverse):
                xhat_ref[r, k] = xhat.astype(BF16)
                slope_ref[r, k] = slope.astype(BF16)
                if k == 0 and r == 0:
                    put_rows(inv_ref, inverse)

            norm_slots(
                p_ref, lambda r: refs[r][k], st_ref, par_ref, act_ref, seg, count, (0, 0), put, keep_slot
            )
        src = src_ref[...]
        total = jnp.zeros((px, mid), F32)
        for tap in range(9):
            plane, shift = STRIDED_TAPS[tap]
            total = total + dot(shifted(src, shift, joined(out_ref, plane)), tap_weight(p_ref, w_refs[tap], s1_w[1]))
        raw = total.astype(BF16)
        raw_ref[...] = raw
        send_sums(sto_ref, columns_of(segh_ref[...], subs), raw)

    def mid_inputs(raws, st):
        return (*raws, st, params, active, seg_half, counts)

    def mid_outs():
        return (
            struct((nc, px, mid), BF16),
            struct((nc, px, mid)),
            struct((nc, px, mid)),
            struct((8, mid)),
        )

    def mid_part(which, p_ref, refs, st_ref, par_ref, act_ref, segh_ref, cnt_ref, out_ref, xhat_ref, slope_ref, inv_ref):
        seg = columns_of(segh_ref[...], subs)

        def put(r, value):
            out_ref[r] = value

        def keep_slot(r, xhat, slope, inverse):
            xhat_ref[r] = xhat
            slope_ref[r] = slope
            if r == 0:
                put_rows(inv_ref, inverse)

        norm_slots(
            p_ref, lambda r: refs[r][...], st_ref, par_ref, act_ref, seg,
            row_list(cnt_ref[...], 0, subs), which, put, keep_slot,
        )
        return seg

    def wide_sums(st_ref, seg, fields):
        for k in range(wide_blocks):
            rows = fields(k)
            put_sums(st_ref, rows, k * len(rows))
        fan_out(st_ref)

    def expand_one_kernel(
        p_ref, r0, r1_, r2_, r3, st_ref, par_ref, act_ref, segh_ref, cnt_ref, w_ref, short_ref,
        out_ref, xhat_ref, slope_ref, inv_ref, pre_ref, sto_ref,
    ):
        seg = mid_part(
            (0, 1), p_ref, (r0, r1_, r2_, r3), st_ref, par_ref, act_ref, segh_ref, cnt_ref,
            out_ref, xhat_ref, slope_ref, inv_ref,
        )
        pre_ref[...] = dot_nt(joined(out_ref), joined_weight(p_ref, w_ref))

        def fields(k):
            a, b = pre_ref[:, block_lanes(k)], short_ref[:, block_lanes(k)]
            return sums(seg, a) + sums(seg, a * a) + sums(seg, b) + sums(seg, b * b)

        wide_sums(sto_ref, seg, fields)

    def summed(st_ref, k=0, rows=2 * subs):
        total = st_ref[0, k * rows : (k + 1) * rows, :]
        for b in range(1, nb):
            total = total + st_ref[b, k * rows : (k + 1) * rows, :]
        return total

    def to_slots(slot_refs, value):
        for r in range(nc):
            slot_refs[r][...] = value[:, r * mid : (r + 1) * mid].astype(BF16)

    def send_upstream(p_ref, slot_refs, st_ref, seg, back, slope_ref, xhat_ref):
        for r in range(nc):
            u = (back[:, r * mid : (r + 1) * mid] * slope_ref[r]).astype(BF16)
            slot_refs[r][...] = u
            u = u.astype(F32)
            send_block(p_ref, st_ref, r, sums(seg, u) + sums(seg, u * xhat_ref[r]))

    def send_block(p_ref, st_ref, r, rows):
        block = jnp.concatenate(rows + [jnp.zeros((8 - len(rows), LANES), F32)], axis=0)
        for b in range(nb):
            st_ref[b * nc + (p_ref[0] ^ r)] = block

    def received(refs, *at):
        total = refs[0][at or ...].astype(F32)
        for ref in refs[1:]:
            total = total + ref[at or ...].astype(F32)
        return total

    def all_summed(st_ref):
        total = st_ref[0]
        for b in range(1, every):
            total = total + st_ref[b]
        return total

    def section_kernel(
        p_ref, st_ref, three_ref, short_ref, gain_ref, bias_ref, segh_ref, cnt_ref, w_ref,
        xh3_ref, xhs_ref, out_ref, slope_ref, inv_ref, low_ref, *slot_refs,
    ):
        seg = columns_of(segh_ref[...], subs)
        mask = mask_of(seg)
        count = row_list(cnt_ref[...], 0, subs)
        for k in range(wide_blocks):
            ln = block_lanes(k)
            total = summed(st_ref, k, 4 * subs)
            both = None
            for n, (pre, keep) in enumerate(((three_ref, xh3_ref), (short_ref, xhs_ref))):
                average, inverse = moments(row_list(total, 2 * subs * n, 2 * subs), count, subs)
                xhat = (pre[:, ln] - select(seg, average)) * select(seg, inverse)
                keep[:, ln] = xhat
                for s in range(subs):
                    inv_ref[n * subs + s : n * subs + s + 1, ln] = inverse[s]
                norm = gain_ref[n : n + 1, ln] * xhat + bias_ref[n : n + 1, ln]
                both = norm if both is None else both + norm
            value, slope = silu_and_slope(both)
            value = value * mask
            out_ref[:, ln] = value
            slope_ref[:, ln] = slope * mask
            low_ref[:, ln] = value.astype(BF16)
        to_slots(slot_refs, dot(low_ref[...], joined_weight(p_ref, w_ref)))

    def four_kernel(p_ref, s0, s1_, s2_, s3, segh_ref, raw_ref, sto_ref):
        total = s0[...].astype(F32)
        for ref in (s1_, s2_, s3):
            total = total + ref[...].astype(F32)
        raw = total.astype(BF16)
        raw_ref[...] = raw
        send_sums(sto_ref, columns_of(segh_ref[...], subs), raw)

    def spatial_two_kernel(
        p_ref, r0, r1_, r2_, r3, st_ref, par_ref, act_ref, segh_ref, cnt_ref, src_ref, *rest
    ):
        w_refs, (out_ref, xhat_ref, slope_ref, inv_ref, raw_ref, sto_ref) = rest[:9], rest[9:]
        seg = mid_part(
            (1, 0), p_ref, (r0, r1_, r2_, r3), st_ref, par_ref, act_ref, segh_ref, cnt_ref,
            out_ref, xhat_ref, slope_ref, inv_ref,
        )
        src = src_ref[...]
        total = jnp.zeros((px, mid), F32)
        whole = joined(out_ref)
        for tap in range(9):
            total = total + dot(shifted(src, tap, whole), tap_weight(p_ref, w_refs[tap], s2_w[1]))
        raw = total.astype(BF16)
        raw_ref[...] = raw
        send_sums(sto_ref, seg, raw)

    def expand_two_kernel(
        p_ref, r0, r1_, r2_, r3, st_ref, par_ref, act_ref, segh_ref, cnt_ref, w_ref,
        out_ref, xhat_ref, slope_ref, inv_ref, pre_ref, sto_ref,
    ):
        seg = mid_part(
            (1, 1), p_ref, (r0, r1_, r2_, r3), st_ref, par_ref, act_ref, segh_ref, cnt_ref,
            out_ref, xhat_ref, slope_ref, inv_ref,
        )
        pre_ref[...] = dot_nt(joined(out_ref), joined_weight(p_ref, w_ref))

        def fields(k):
            a = pre_ref[:, block_lanes(k)]
            return sums(seg, a) + sums(seg, a * a)

        wide_sums(sto_ref, seg, fields)

    def final_kernel(
        p_ref, st_ref, pre_ref, section_ref, cot_ref, gain_ref, bias_ref, segh_ref, cnt_ref, pick_ref,
        out_ref, grad_ref, xhat_ref, inv_ref, sto_ref,
    ):
        seg = columns_of(segh_ref[...], subs)
        mask = mask_of(seg)
        count = row_list(cnt_ref[...], 0, subs)
        picked = pick_ref[...]
        for k in range(wide_blocks):
            ln = block_lanes(k)
            average, inverse = moments(row_list(summed(st_ref, k), 0, 2 * subs), count, subs)
            xhat = (pre_ref[:, ln] - select(seg, average)) * select(seg, inverse)
            xhat_ref[:, ln] = xhat
            for s in range(subs):
                inv_ref[s : s + 1, ln] = inverse[s]
            both = gain_ref[:, ln] * xhat + bias_ref[:, ln] + section_ref[:, ln]
            value, slope = silu_and_slope(both)
            value = value * mask

            def place_out(i, j, first, rows):
                out_ref[i, j, first : first + rows.shape[0], ln] = rows

            geo.unpack(lambda first, count: value[first : first + count], place_out)
            parts = []
            geo.pack(picked, lambda i, j: cot_ref[i, j, :, ln], lambda first, rows: parts.append(rows))
            grad = jnp.concatenate(parts, axis=0).astype(F32) * mask * slope
            grad_ref[:, ln] = grad
            put_sums(sto_ref, sums(seg, grad) + sums(seg, grad * xhat), k * 2 * subs)
        fan_out(sto_ref)

    def norm_back(total, at, gain, inverse, u, xhat, seg, count):
        g = [total[s : s + 1] / count[s] for s in range(subs)]
        x = [total[at + s : at + s + 1] / count[s] for s in range(subs)]
        scale = select(seg, [gain * row for row in inverse])
        return (scale * (u - (select(seg, g) + xhat * select(seg, x)))).astype(BF16)

    def put_param_grads(ref, ln, total, pairs):
        for n, first in enumerate(pairs):
            row = total[first : first + 1]
            for s in range(1, subs):
                row = row + total[first + s : first + s + 1]
            ref[n : n + 1, ln] = row

    def back_six_kernel(
        p_ref, st_ref, u_ref, xhat_ref, inv_ref, gain_ref, segh_ref, cnt_ref, w_ref, slope_ref, xh5_ref, low_ref, par_ref, sto_ref, *slot_refs
    ):
        seg = columns_of(segh_ref[...], subs)
        count = row_list(cnt_ref[...], 0, subs)
        for k in range(wide_blocks):
            ln = block_lanes(k)
            total = summed(st_ref, k)
            put_param_grads(par_ref, ln, total, (subs, 0))
            low_ref[:, ln] = norm_back(
                total, subs, gain_ref[:, ln], row_list(inv_ref[:, ln], 0, subs), u_ref[:, ln], xhat_ref[:, ln], seg, count
            )
        send_upstream(p_ref, slot_refs, sto_ref, seg, dot(low_ref[...], joined_weight(p_ref, w_ref)), slope_ref, xh5_ref)

    def own_gain(ref, which):
        block, layer = which
        return ref[0, 4 * block + layer : 4 * block + layer + 1, :]

    def back_own(st_ref, u_refs, xhat_ref, inv_ref, params_ref, which, segh_ref, cnt_ref, par_ref):
        seg = columns_of(segh_ref[...], subs)
        total = all_summed(st_ref)
        put_param_grads(par_ref, slice(0, LANES), total, (subs, 0))
        return seg, norm_back(
            total, subs, own_gain(params_ref, which), row_list(inv_ref[...], 0, subs), received(u_refs), xhat_ref[...],
            seg, row_list(cnt_ref[...], 0, subs),
        )

    def back_spatial_kernel(which, taps, order, per, planes):
        def kernel(
            p_ref, st_ref, u0, u1, u2, u3, xhat_ref, inv_ref, params_ref, segh_ref, cnt_ref, src_ref,
            slope_ref, xhats_ref, segs_ref, *rest
        ):
            w_refs, (cols_ref, par_ref, sto_ref, *slot_refs) = rest[:9], rest[9:]
            _, low = back_own(
                st_ref, (u0, u1, u2, u3), xhat_ref, inv_ref, params_ref, which, segh_ref, cnt_ref, par_ref
            )
            src = src_ref[...]
            rows = [None] * nc
            back = None
            for n, tap in enumerate(order):
                plane, shift = taps[tap]
                g = shifted(src, 8 - shift, low)
                cols_ref[:, n * mid : (n + 1) * mid] = g
                new = dot_nt(g, tap_weight(p_ref, w_refs[tap], per))
                back = new if back is None else back + new
                if n < 8 and taps[order[n + 1]][0] == plane:
                    continue
                seg = columns_of(segs_ref[plane], subs)
                for r in range(nc):
                    u = (back[:, r * mid : (r + 1) * mid] * slope_ref[r, plane].astype(F32)).astype(BF16)
                    slot_refs[r][plane] = u
                    u = u.astype(F32)
                    got = sums(seg, u) + sums(seg, u * xhats_ref[r, plane].astype(F32))
                    rows[r] = got if rows[r] is None else [a + b for a, b in zip(rows[r], got)]
                back = None
            for r in range(nc):
                send_block(p_ref, sto_ref, r, rows[r])

        return kernel

    def back_plain_kernel(which):
        def kernel(p_ref, st_ref, u0, u1, u2, u3, xhat_ref, inv_ref, params_ref, segh_ref, cnt_ref, low_ref, par_ref):
            _, low_ref[...] = back_own(
                st_ref, (u0, u1, u2, u3), xhat_ref, inv_ref, params_ref, which, segh_ref, cnt_ref, par_ref
            )

        return kernel

    def back_section_kernel(
        p_ref, g0, g1, g2, g3, w_ref, grad_ref, slope_ref, xh3_ref, xhs_ref, segh_ref,
        whole_ref, u_ref, sto_ref,
    ):
        for r, ref in enumerate((g0, g1, g2, g3)):
            whole_ref[r] = ref[...]
        u_ref[...] = dot_nt(joined(whole_ref), joined_weight(p_ref, w_ref))
        seg = columns_of(segh_ref[...], subs)
        for k in range(wide_blocks):
            ln = block_lanes(k)
            u = (u_ref[:, ln] + grad_ref[:, ln]) * slope_ref[:, ln]
            u_ref[:, ln] = u
            rows = sums(seg, u) + sums(seg, u * xh3_ref[:, ln]) + sums(seg, u * xhs_ref[:, ln])
            put_sums(sto_ref, rows, k * 3 * subs)
        fan_out(sto_ref)

    def back_wide_kernel(
        p_ref, st_ref, u_ref, xh3_ref, xhs_ref, inv_ref, gain_ref, segh_ref, cnt_ref, w_ref, slope_ref, xh2_ref,
        three_ref, short_ref, par_ref, sto_ref, *slot_refs,
    ):
        seg = columns_of(segh_ref[...], subs)
        count = row_list(cnt_ref[...], 0, subs)
        for k in range(wide_blocks):
            ln = block_lanes(k)
            total = summed(st_ref, k, 3 * subs)
            put_param_grads(par_ref, ln, total, (subs, 2 * subs, 0))
            u = u_ref[:, ln]
            inverse = inv_ref[:, ln]
            three_ref[:, ln] = norm_back(
                total, subs, gain_ref[0:1, ln], row_list(inverse, 0, subs), u, xh3_ref[:, ln], seg, count
            )
            short_ref[:, ln] = norm_back(
                total, 2 * subs, gain_ref[1:2, ln], row_list(inverse, subs, subs), u, xhs_ref[:, ln], seg, count
            )
        send_upstream(p_ref, slot_refs, sto_ref, seg, dot(three_ref[...], joined_weight(p_ref, w_ref)), slope_ref, xh2_ref)

    def back_one_kernel(
        p_ref, st_ref, u0, u1, u2, u3, xhat_ref, inv_ref, params_ref, segf_ref, cnt_ref, w_ref, short_ref, sc_ref,
        low_ref, par_ref, *slot_refs,
    ):
        count = row_list(cnt_ref[...], subs, subs)
        total = all_summed(st_ref)
        put_param_grads(par_ref, slice(0, LANES), total, (subs, 0))
        for k in range(4):
            seg = columns_of(segf_ref[k], subs)
            low_ref[k] = norm_back(
                total, subs, own_gain(params_ref, (0, 0)), row_list(inv_ref[...], 0, subs),
                received((u0, u1, u2, u3), k), xhat_ref[k].astype(F32), seg, count,
            )
        for r in range(nc):
            w = reduce_rows(w_ref, p_ref[0] ^ r)
            for k in range(4):
                got = dot_nt(low_ref[k], w)
                if k == 0:
                    got = got + dot_nt(short_ref[...], shortcut_rows(sc_ref, p_ref[0] ^ r))
                slot_refs[r][k] = got.astype(BF16)

    def input_kernel(p_ref, a_ref, b_ref, c_ref, segf_ref, out_ref):
        for k in range(4):
            mask = jnp.sum(segf_ref[k], axis=1, keepdims=True)
            total = a_ref[k].astype(F32) + b_ref[k].astype(F32) + c_ref[k].astype(F32)
            total = total * mask

            def place_out(i, j, first, rows):
                out_ref[2 * i + k // 2, 2 * j + k % 2, first : first + rows.shape[0], :] = rows

            geo.unpack(lambda first, count: total[first : first + count], place_out)

    def put_expand(p_ref, out_ref, at, grad_ref, act_ref):
        for k in range(nc):
            got = dot_tn(grad_ref[...], act_ref[p_ref[0] ^ k]).astype(BF16)
            for j in range(spread):
                out_ref[k * spread + j, at : at + e_cols, :] = got[j * e_cols : (j + 1) * e_cols]

    def put_spatial(out_ref, at, k, taps, got):
        for j in range(spread):
            for n, tap in enumerate(taps):
                first = at + tap * s_rows
                out_ref[k * spread + j, first : first + s_rows, :] = got[
                    j * s_rows : (j + 1) * s_rows, n * mid : (n + 1) * mid
                ]

    def grads_two_kernel(p_ref, six_ref, act5_ref, act4_ref, cols_ref, out_ref):
        put_expand(p_ref, out_ref, 0, six_ref, act5_ref)
        for k in range(nc):
            got = dot_tn(act4_ref[p_ref[0] ^ k], cols_ref[...]).astype(BF16)
            put_spatial(out_ref, e_cols, k, range(9), got)

    def grads_mixed_kernel(p_ref, low_ref, four_ref, three_ref, act2_ref, e0, e1_, e2_, e3, short_ref, out_ref):
        for k in range(nc):
            got = dot_tn(low_ref[...], four_ref[p_ref[0] ^ k]).astype(BF16)
            for j in range(spread):
                out_ref[k * spread + j, 0:r2_rows, :] = got[j * r2_rows : (j + 1) * r2_rows]
        put_expand(p_ref, out_ref, r2_rows, three_ref, act2_ref)
        first = r2_rows + e_cols
        for c, entry_ref in enumerate((e0, e1_, e2_, e3)):
            got = dot_tn(entry_ref[...], short_ref[...]).astype(BF16)
            for j in range(spread):
                for k in range(wide_blocks):
                    out_ref[c * spread + j, first + k * in_rows : first + (k + 1) * in_rows, :] = got[
                        j * in_rows : (j + 1) * in_rows, block_lanes(k)
                    ]

    def grads_reduce_kernel(p_ref, e0, e1_, e2_, e3, grad_ref, out_ref):
        for c, entry_ref in enumerate((e0, e1_, e2_, e3)):
            got = dot_tn(entry_ref[0], grad_ref[0])
            for k in range(1, 4):
                got = got + dot_tn(entry_ref[k], grad_ref[k])
            for j in range(spread):
                out_ref[c * spread + j] = got[j * in_rows : (j + 1) * in_rows].astype(BF16)

    def grads_one_kernel(p_ref, act_ref, cols_ref, keep_ref, send_ref):
        odd = lax.rem(p_ref[1], 2) == 1
        for k in range(nc):
            first = 0
            for plane in range(4):
                taps = [t for t in STRIDED_ORDER if STRIDED_TAPS[t][0] == plane]
                lanes = slice(first * mid, (first + len(taps)) * mid)
                first += len(taps)
                got = dot_tn(act_ref[plane, p_ref[0] ^ k], cols_ref[:, lanes])
                for j in range(0, spread, 2):
                    one, two = got[j * s_rows : (j + 1) * s_rows], got[(j + 1) * s_rows : (j + 2) * s_rows]
                    keep, send = jnp.where(odd, two, one).astype(BF16), jnp.where(odd, one, two).astype(BF16)
                    for n, tap in enumerate(taps):
                        rows = slice(tap * s_rows, (tap + 1) * s_rows)
                        keep_ref[(k * spread + j) // 2, rows, :] = keep[:, block_lanes(n)]
                        send_ref[(k * spread + j) // 2, rows, :] = send[:, block_lanes(n)]

    def mine(p_ref, pair_ref, got_ref):
        return pair_ref[lax.rem(p_ref[1], 2)].astype(F32) + got_ref[...].astype(F32)

    def total_kernel(p_ref, *refs):
        total = refs[0][...].astype(F32)
        for ref in refs[1:-1]:
            total = total + ref[...].astype(F32)
        refs[-1][...] = total.astype(refs[-1].dtype)

    def turn_kernel(p_ref, two_ref, two_got, mixed_ref, mixed_got, turn_out, s2_out, sc_out):
        two, mixed = mine(p_ref, two_ref, two_got), mine(p_ref, mixed_ref, mixed_got)
        turn_out[0:e_cols] = mixed[r2_rows : r2_rows + e_cols].astype(BF16)
        turn_out[e_cols : e_cols + r2_rows] = mixed[0:r2_rows].astype(BF16)
        turn_out[e_cols + r2_rows :] = two[0:e_cols].astype(BF16)
        s2_out[...] = two[e_cols:]
        first = r2_rows + e_cols
        for k in range(wide_blocks):
            sc_out[:, block_lanes(k)] = mixed[first + k * in_rows : first + (k + 1) * in_rows]

    def param_kernel(p_ref, one, two, wide_one, four, five, six, g1, b1, gw1, bw1, g2, b2, gw2, bw2):
        for first, second, gain, bias in ((one, two, g1, b1), (four, five, g2, b2)):
            for n, ref in enumerate((first, second)):
                gain[n : n + 1, :] = ref[0:1, :]
                bias[n : n + 1, :] = ref[1:2, :]
        gw1[...] = wide_one[0:2, :]
        bw1[0:1, :] = wide_one[2:3, :]
        bw1[1:2, :] = wide_one[2:3, :]
        gw2[...] = six[0:1, :]
        bw2[...] = six[1:2, :]

    def own_kernel(p_ref, turned_ref, e1_out, r2_out, e2_out):
        e1_out[...] = turned_ref[0:e_cols].astype(F32).T
        r2_out[...] = turned_ref[e_cols : e_cols + r2_rows].astype(F32)
        e2_out[...] = turned_ref[e_cols + r2_rows :].astype(F32).T

    def to_owners(shares):
        rows = shares.shape[1]
        groups = [list(range(first, nb, 2)) for first in range(2)]
        pair = lax.psum_scatter(
            shares.reshape(nb // 2, 2 * rows, mid), "batch", scatter_dimension=0, axis_index_groups=groups, tiled=False
        ).reshape(2, rows, mid)
        send = lax.dynamic_index_in_dim(pair, 1 - ber % 2, 0, False)
        return pair, lax.ppermute(send, "batch", [(i, i ^ 1) for i in range(nb)])

    st_mid, st_own, st_wide = (
        struct((every, 8, LANES)),
        struct((nb, 8, LANES)),
        struct((nb, whole_tiles(2 * subs * wide_blocks), LANES)),
    )
    matmul = 2 * px * whole_mid * wide
    mid_slots = [struct((px, mid), BF16)] * nc
    half = side // 2

    raw_one, st = call(
        reduce_kernel, (struct((4, px, mid), BF16), st_mid), place, *entries, r1_w, seg_full, flops=4 * matmul
    )
    (st,) = call(total_kernel, (st_mid,), place, st, after=[later])
    raws, st = slots_of(raw_one), to_all(st)
    act_one, xhat_one, slope_one, inv_one, raw_two, st = call(
        spatial_one_kernel,
        (
            struct((4, nc, px, mid), BF16),
            struct((nc, 4, px, mid), BF16),
            struct((nc, 4, px, mid), BF16),
            struct((8, mid)),
            struct((px, mid), BF16),
            st_mid,
        ),
        place, *raws, st, params, active, seg_full, seg_half, counts, source, *s1_w[0],
        flops=10 * matmul,
    )
    shorts = [part(entry, (None, None, px, part_in), (c, 0, 0, 0)) for c in range(nc)]
    (pre_short,) = call(short_kernel, (struct((px, wide)),), place, *shorts, sc_w, seg_half, flops=4 * matmul)
    raws, st = slots_of(raw_two), to_all(st)
    act_two, xhat_two, slope_two, inv_two, pre_three, st = call(
        expand_one_kernel,
        (*mid_outs(), struct((px, wide)), struct((nb, whole_tiles(4 * subs * wide_blocks), LANES))),
        place, *mid_inputs(raws, st), e1_w, pre_short,
        flops=2 * matmul,
    )
    xhat_three, xhat_short, section_out, slope_section, inv_wide, section_low, *slots = call(
        section_kernel,
        (
            *[struct((px, wide))] * 4,
            struct((8, wide)),
            struct((px, wide), BF16),
            *mid_slots,
        ),
        place, to_batch(st), pre_three, pre_short, first_wide_gain, first_wide_bias, seg_half, counts, r2_w,
        flops=2 * matmul,
    )

    raw_four, st = call(
        four_kernel, (struct((px, mid), BF16), st_mid), place, *swap_slots(slots), seg_half
    )
    raws, st = slots_of(raw_four), to_all(st)
    act_four, xhat_four, slope_four, inv_four, raw_five, st = call(
        spatial_two_kernel,
        (*mid_outs(), struct((px, mid), BF16), st_mid),
        place, *mid_inputs(raws, st), source, *s2_w[0],
        flops=8 * matmul,
    )
    raws, st = slots_of(raw_five), to_all(st)
    act_five, xhat_five, slope_five, inv_five, pre_six, st = call(
        expand_two_kernel,
        (*mid_outs(), struct((px, wide)), st_wide),
        place, *mid_inputs(raws, st), e2_w,
        flops=2 * matmul,
    )
    gain_six, bias_six = second_wide_gain[None], second_wide_bias[None]
    out_rows, grad_final, xhat_six, inv_six, st = call(
        final_kernel,
        (struct((half, half, crops, wide)), *[struct((px, wide))] * 2, struct((8, wide)), st_wide),
        place, to_batch(st), pre_six, section_out, cotangent.transpose(1, 2, 0, 3), gain_six, bias_six, seg_half, counts,
        pick_large,
    )
    output = out_rows.transpose(2, 0, 1, 3)

    grad_six, par_six, st, *slots = call(
        back_six_kernel,
        (struct((px, wide), BF16), struct((8, wide)), st_mid, *mid_slots),
        place, to_batch(st), grad_final, xhat_six, inv_six, gain_six, seg_half, counts, e2_w, slope_five, xhat_five,
        flops=2 * matmul,
    )

    def own(xhat):
        return part(xhat, (None, *xhat.shape[1:]), (0,) * xhat.ndim)

    raws, st = swap_slots(slots), to_all(st)
    cols_five, par_five, st, *slots = call(
        back_spatial_kernel((1, 1), UNIT_TAPS, list(range(9)), s2_w[1], 1),
        (struct((px, 9 * mid), BF16), struct((8, mid)), st_mid, *[struct((1, px, mid), BF16)] * nc),
        place, st, *raws, own(xhat_five), inv_five, params, seg_half, counts, source, slope_four[:, None],
        xhat_four[:, None], seg_half[None], *s2_w[0],
        flops=8 * matmul,
    )
    raws, st = swap_slots([x.reshape(px, mid) for x in slots]), to_all(st)
    (shares_two,) = call(
        grads_two_kernel, (struct((nb, e_cols + 9 * s_rows, mid), BF16),),
        place, grad_six, act_five, act_four, cols_five, flops=10 * matmul,
    )
    grad_four, par_four = call(
        back_plain_kernel((1, 0)),
        (struct((px, mid), BF16), struct((8, mid))),
        place, st, *raws, own(xhat_four), inv_four, params, seg_half, counts, after=[shares_two],
    )
    whole_grad_four, u_wide, st = call(
        back_section_kernel,
        (struct((nc, px, mid), BF16), struct((px, wide)), struct((nb, whole_tiles(3 * subs * wide_blocks), LANES))),
        place, *slots_of(grad_four), r2_w, grad_final, slope_section, xhat_three, xhat_short, seg_half,
        flops=2 * matmul,
    )

    grad_three, grad_short, par_wide, st, *slots = call(
        back_wide_kernel,
        (
            struct((px, wide), BF16),
            struct((px, wide), BF16),
            struct((8, wide)),
            st_mid,
            *mid_slots,
        ),
        place, to_batch(st), u_wide, xhat_three, xhat_short, inv_wide, first_wide_gain, seg_half, counts, e1_w,
        slope_two, xhat_two,
        flops=2 * matmul,
    )
    raws, st = swap_slots(slots), to_all(st)
    (shares_mixed,) = call(
        grads_mixed_kernel, (struct((nb, b_rows, mid), BF16),),
        place, section_low, whole_grad_four, grad_three, act_two, *shorts, grad_short, flops=8 * matmul,
    )
    owned_two, owned_mixed = to_owners(shares_two), to_owners(shares_mixed)
    cols_two, par_two, st, *slots = call(
        back_spatial_kernel((0, 1), STRIDED_TAPS, STRIDED_ORDER, s1_w[1], 4),
        (struct((px, 9 * mid), BF16), struct((8, mid)), st_mid, *[struct((4, px, mid), BF16)] * nc),
        place, st, *raws, own(xhat_two), inv_two, params, seg_half, counts, source, slope_one, xhat_one, seg_full,
        *s1_w[0],
        flops=8 * matmul, after=[shares_mixed, owned_two[0]],
    )
    raws, st = swap_slots(slots), to_all(st)
    half_one = struct((nb // 2, 9 * s_rows, mid), BF16)
    keep, send = call(grads_one_kernel, (half_one, half_one), place, act_one, cols_two, flops=8 * matmul)
    send = lax.ppermute(send, "batch", [(i, i ^ 1) for i in range(nb)])
    (sum_one,) = call(total_kernel, (half_one,), place, keep, send)
    grad_one, par_one, *slots = call(
        back_one_kernel,
        (struct((4, px, mid), BF16), struct((8, mid)), *[struct((4, px, part_in), BF16)] * nc),
        place, st, *raws, own(xhat_one), inv_one, params, seg_full, counts, r1_w, grad_short, sc_w,
        flops=8 * matmul, after=[sum_one],
    )
    far_first, own_back = chan_swap(slots[3], 1), chan_swap(slots[1], 1)
    far_sum = (slots[2].astype(F32) + far_first.astype(F32)).astype(BF16)
    far_back = chan_swap(far_sum, 2)

    (shares,) = call(
        grads_reduce_kernel, (struct((nb, in_rows, mid), BF16),),
        place, *entries, grad_one, flops=4 * matmul, after=[far_sum, owned_mixed[0]],
    )
    r1_out = jnp.sum(to_batch(shares).astype(F32), axis=0)
    turned, s2_own, sc_own = call(
        turn_kernel,
        (struct((turn_rows, mid), BF16), struct((9 * s_rows, mid)), struct((in_rows, wide))),
        place, *owned_two, *owned_mixed,
    )
    s1_total = lax.psum_scatter(
        sum_one, "batch", scatter_dimension=0, tiled=False,
        axis_index_groups=[list(range(first, nb, 2)) for first in range(2)],
    ).astype(F32)
    e1_own, r2_own, e2_own = call(
        own_kernel,
        (struct((mid, e_cols)), struct((r2_rows, mid)), struct((mid, e_cols))),
        place, turn_share(turned),
    )
    mid_pair, wide_pair, wide_row = struct((2, mid)), struct((2, wide)), struct((1, wide))
    own_params_grad = call(
        param_kernel,
        (mid_pair, mid_pair, wide_pair, wide_pair, mid_pair, mid_pair, wide_row, wide_row),
        place, par_one, par_two, par_wide, par_four, par_five, par_six, after=[far_sum],
    )
    outs = (
        output,
        s1_total.reshape(3, 3, s_rows, mid),
        e1_own,
        sc_own,
        r2_own,
        s2_own.reshape(3, 3, s_rows, mid),
        e2_own,
        *own_params_grad[:-2],
        own_params_grad[-2][0],
        own_params_grad[-1][0],
    )
    (input_grad,) = call(
        input_kernel, (struct((side, side, crops, part_in)),), place, slots[0], own_back, far_back, seg_full,
        after=[own_params_grad[0]],
    )
    return outs[:1] + (input_grad.transpose(2, 0, 1, 3), r1_out) + outs[1:]


def solution(mesh):
    placed = (
        P("batch", None, None, "chan"),
        P("batch", "chan"),
        P(None, None, "batch", "chan"),
        P("chan", "batch"),
        P("batch", "chan"),
        P("batch", "chan"),
        P(None, None, "batch", "chan"),
        P("chan", "batch"),
        P(None, "chan"),
        P(None, "chan"),
        P(None, "chan"),
        P(None, "chan"),
        P(None, "chan"),
        P(None, "chan"),
        P("chan"),
        P("chan"),
        P(),
        P(),
        P(),
        P("batch", None, None, "chan"),
    )
    outs = (
        P("batch", None, None, "chan"),
        P("batch", None, None, "chan"),
        P("batch", "chan"),
        P(None, None, "batch", "chan"),
        P("chan", "batch"),
        P("batch", "chan"),
        P("batch", "chan"),
        P(None, None, "batch", "chan"),
        P("chan", "batch"),
        P(None, "chan"),
        P(None, "chan"),
        P(None, "chan"),
        P(None, "chan"),
        P(None, "chan"),
        P(None, "chan"),
        P("chan"),
        P("chan"),
    )
    return jax.shard_map(local, mesh=mesh, in_specs=placed, out_specs=outs, check_vma=False)
```

```python
import jax
import jax.numpy as jnp
import numpy as np
from jax import lax
from jax.experimental import pallas as pl
from jax.experimental.pallas import tpu as pltpu
from jax.sharding import PartitionSpec as P

F32, BF16 = jnp.float32, jnp.bfloat16
EPS = 1e-05
SMALL = 6
LANES = 128
ALL = ("batch", "chan")


class Geometry:
    def __init__(self, crops, side):
        self.crops, self.side = crops, side
        self.half, self.small = side // 2, SMALL // 2
        self.large = [c for c in range(crops) if c % 8 < 2]
        grid = [(i, j) for i in range(self.half) for j in range(self.half)]
        self.common = [at for at in grid if max(at) < self.small]
        self.others = [at for at in grid if max(at) >= self.small]
        rows = [(c, i, j) for i, j in self.common for c in range(crops)]
        rows += [(c, i, j) for i, j in self.others for c in self.large]
        self.cut = len(self.common) * crops
        self.rows = np.array(rows, np.int32)
        self.pixels = len(rows)
        where = {tuple(r): n for n, r in enumerate(rows)}
        source = np.full((self.pixels, 16), -1, np.int32)
        for n, (crop, i, j) in enumerate(rows):
            for shift in range(9):
                source[n, shift] = where.get((crop, i + shift // 3 - 1, j + shift % 3 - 1), -1)
        self.source = source
        self.group = 8
        wanted = len(self.large)
        pick = np.zeros((self.group * wanted, self.group * crops), np.float32)
        for n in range(self.group):
            for m, c in enumerate(self.large):
                pick[n * wanted + m, n * crops + c] = 1.0
        self.pick = pick

    def pack(self, pick, load, store):
        for n, (i, j) in enumerate(self.common):
            store(n * self.crops, load(i, j))
        wanted = len(self.large)
        for n in range(0, len(self.others), self.group):
            rows = jnp.concatenate([load(i, j) for i, j in self.others[n : n + self.group]], axis=0)
            store(self.cut + n * wanted, dot(pick, rows).astype(rows.dtype))

    def unpack(self, load, store):
        for n, (i, j) in enumerate(self.common):
            store(i, j, 0, load(n * self.crops, self.crops))
        wanted = len(self.large)
        for n, (i, j) in enumerate(self.others):
            rows = load(self.cut + n * wanted, wanted)
            store(i, j, 0, jnp.zeros((self.crops, rows.shape[1]), rows.dtype))
            for m in range(0, wanted, 2):
                store(i, j, self.large[m], rows[m : m + 2])


UNIT_TAPS = [(0, tap) for tap in range(9)]
STRIDED_TAPS = [
    (2 * int(r != 1) + int(c != 1), 3 * (0 if r == 0 else 1) + (0 if c == 0 else 1))
    for r in range(3)
    for c in range(3)
]
STRIDED_ORDER = [tap for plane in range(4) for tap in range(9) if STRIDED_TAPS[tap][0] == plane]

SM = pl.BlockSpec(memory_space=pltpu.SMEM)


def struct(shape, dtype=F32):
    return jax.ShapeDtypeStruct(tuple(shape), dtype)


def whole_block(shape, at=None):
    at = at or (0,) * len(shape)
    return pl.BlockSpec(tuple(shape), lambda _: at)


def part(array, shape, at):
    return array, whole_block(shape, at)


def corner(array):
    shape = (1,) * (array.ndim - 2) + (16, LANES) if array.ndim > 1 else array.shape
    return array, whole_block([min(a, b) for a, b in zip(shape, array.shape)], (0,) * array.ndim)


def call(kernel, outs, place, *args, flops=10**8, mib=64, after=()):
    args = [a if isinstance(a, tuple) else (a, whole_block(a.shape)) for a in args]
    moved = sum(int(np.prod([n or 1 for n in b.block_shape])) * a.dtype.itemsize for a, b in args)
    moved += sum(int(np.prod(o.shape)) * o.dtype.itemsize for o in outs)
    used, args = len(args), args + [corner(a) for a in after]

    def body(p_ref, *refs):
        kernel(p_ref, *refs[:used], *refs[len(args) :])

    return pl.pallas_call(
        body,
        grid=(1,),
        out_shape=tuple(outs),
        in_specs=[SM] + [b for _, b in args],
        out_specs=tuple(whole_block(o.shape) for o in outs),
        compiler_params=pltpu.CompilerParams(vmem_limit_bytes=mib * 1024 * 1024),
        cost_estimate=pl.CostEstimate(flops=flops, bytes_accessed=moved, transcendentals=0),
    )(place, *[a for a, _ in args])


def dot(a, b):
    return jnp.dot(a, b, preferred_element_type=F32)


def dot_nt(a, b):
    return lax.dot_general(a, b, (((1,), (1,)), ((), ())), preferred_element_type=F32)


def dot_tn(a, b):
    return lax.dot_general(a, b, (((0,), (0,)), ((), ())), preferred_element_type=F32)


def columns_of(seg, subs):
    return [jnp.broadcast_to(seg[:, s : s + 1], (seg.shape[0], LANES)) for s in range(subs)]


def select(seg, rows):
    total = seg[0] * rows[0]
    for s in range(1, len(rows)):
        total = total + seg[s] * rows[s]
    return total


def mask_of(seg):
    mask = seg[0]
    for other in seg[1:]:
        mask = mask + other
    return mask


def sums(seg, field):
    return [jnp.sum(field * g, axis=0, keepdims=True) for g in seg]


def moments(total, count, subs):
    average = [total[s] / count[s] for s in range(subs)]
    inverse = [
        lax.rsqrt(total[subs + s] / count[s] - average[s] * average[s] + EPS) for s in range(subs)
    ]
    return average, inverse


def silu_and_slope(norm):
    sigmoid = jax.nn.sigmoid(norm)
    return norm * sigmoid, sigmoid * (1.0 + norm * (1.0 - sigmoid))


def shifted(source, shift, value):
    if shift == 4:
        return value
    rows = value.shape[0]
    at = lax.broadcasted_iota(jnp.int32, (rows, rows), 1)
    move = jnp.where(at == source[:, shift : shift + 1], 1.0, 0.0).astype(BF16)
    return dot(move, value).astype(BF16)


def put_rows(ref, rows):
    for n, row in enumerate(rows):
        ref[n : n + 1, :] = row


def put_sums(ref, rows, first=0):
    for n, row in enumerate(rows):
        ref[0, first + n : first + n + 1, :] = row


def fan_out(ref):
    block = ref[0]
    for b in range(1, ref.shape[0]):
        ref[b] = block


def whole_tiles(rows):
    return -(-rows // 8) * 8


def block_lanes(k):
    return slice(k * LANES, (k + 1) * LANES)


def row_list(block, first, count):
    return [block[n : n + 1] for n in range(first, first + count)]


def local(
    block_input,
    first_reduce,
    first_spatial,
    first_expand,
    first_shortcut,
    second_reduce,
    second_spatial,
    second_expand,
    first_mid_gain,
    first_mid_bias,
    first_wide_gain,
    first_wide_bias,
    second_mid_gain,
    second_mid_bias,
    second_wide_gain,
    second_wide_bias,
    subnet_widths,
    subnet_ids,
    crop_sides,
    cotangent,
):
    nb, nc = lax.axis_size("batch"), lax.axis_size("chan")
    spread = nb // nc
    crops, side = block_input.shape[0], block_input.shape[1]
    geo = Geometry(crops, side)
    px = geo.pixels
    subs = subnet_widths.shape[0]
    me, ber = lax.axis_index("chan"), lax.axis_index("batch")
    mid = first_reduce.shape[1]
    wide = first_shortcut.shape[1]
    part_in = block_input.shape[3]
    whole_mid = nc * mid
    wide_blocks = wide // LANES

    def chan_swap(x, r):
        return lax.ppermute(x, "chan", [(i, i ^ r) for i in range(nc)])

    def slots_of(x):
        return [x] + [chan_swap(x, r) for r in range(1, nc)]

    def swap_slots(x):
        return [x[0]] + [chan_swap(x[r], r) for r in range(1, nc)]

    def to_batch(x):
        return lax.all_to_all(x, "batch", 0, 0, tiled=True)

    def to_all(x):
        return lax.all_to_all(x, ALL, 0, 0, tiled=True)

    turn = []
    for zc in range(nc):
        for j in range(spread):
            for c in range(nc):
                turn.append(((zc * spread + j) * nc + c, (c * spread + j) * nc + zc))

    def turn_share(x):
        return lax.ppermute(x, ALL, turn)

    s_rows, e_cols, r2_rows = first_spatial.shape[2], first_expand.shape[1], second_reduce.shape[0]
    in_rows, part_in = first_reduce.shape[0], block_input.shape[3]
    early = 2

    def prepare_kernel(
        p_ref, x_ref, pick_ref, r1_ref, s1_ref, e1_ref, sc_ref, r2_ref, s2_ref, e2_ref,
        entry_ref, first_out, later_out, turn_out, mine_out, s2_out,
    ):
        picked = pick_ref[...]
        for k in range(4):

            def store(first, rows):
                entry_ref[k, first : first + rows.shape[0], :] = rows

            geo.pack(picked, lambda i, j: x_ref[2 * i + k // 2, 2 * j + k % 2], store)
        r1, s1 = r1_ref[...].astype(BF16), s1_ref[...].astype(BF16)
        for b in range(nb):
            first_out[b, 0:in_rows] = r1
            first_out[b, in_rows:] = s1[: early * s_rows]
            later_out[b] = s1[early * s_rows :]
        s2_out[...] = s2_ref[...].astype(BF16)
        turn_out[0:e_cols] = e1_ref[...].T.astype(BF16)
        turn_out[e_cols : e_cols + r2_rows] = r2_ref[...].astype(BF16)
        turn_out[e_cols + r2_rows :] = e2_ref[...].T.astype(BF16)
        for k in range(wide_blocks):
            mine_out[k * in_rows : (k + 1) * in_rows] = sc_ref[:, block_lanes(k)].astype(BF16)

    def gather_batch(x):
        return lax.all_gather(x, "batch", axis=0, tiled=False)

    place = jnp.stack([me, ber]).astype(jnp.int32)
    pick_large = jnp.asarray(geo.pick, BF16)
    b_rows, turn_rows = e_cols + r2_rows + wide_blocks * in_rows, 2 * e_cols + r2_rows
    entry, first, later, turned, mine, s2_rows = call(
        prepare_kernel,
        (
            struct((4, px, part_in), BF16),
            struct((nb, in_rows + early * s_rows, mid), BF16),
            struct((nb, (9 - early) * s_rows, mid), BF16),
            struct((turn_rows, mid), BF16),
            struct((wide_blocks * in_rows, mid), BF16),
            struct((9 * s_rows, mid), BF16),
        ),
        place, block_input.transpose(1, 2, 0, 3), pick_large, first_reduce, first_spatial.reshape(9 * s_rows, mid),
        first_expand, first_shortcut, second_reduce, second_spatial.reshape(9 * s_rows, mid), second_expand,
    )
    entry = lax.all_gather(entry, "chan", axis=0, tiled=False)
    entries = [part(entry, (None, 4, px, part_in), (c, 0, 0, 0)) for c in range(nc)]
    first, later, turned = to_batch(first), to_batch(later), turn_share(turned)
    r1_w = part(first, (nb, in_rows, mid), (0, 0, 0))

    def shares_kernel(p_ref, turned_ref, mine_ref, s2_ref, b_out, c_out):
        b_out[0 : e_cols + r2_rows] = turned_ref[0 : e_cols + r2_rows]
        b_out[e_cols + r2_rows :] = mine_ref[...]
        c_out[0:e_cols] = turned_ref[e_cols + r2_rows :]
        c_out[e_cols:] = s2_ref[...]

    b_share, c_share = call(
        shares_kernel,
        (struct((b_rows, mid), BF16), struct((e_cols + 9 * s_rows, mid), BF16)),
        place, turned, mine, s2_rows, after=[first],
    )
    group_b, group_c = gather_batch(b_share), gather_batch(c_share)
    e1_w = part(group_b, (nb, e_cols, mid), (0, 0, 0))
    r2_w = part(group_b, (nb, r2_rows, mid), (0, e_cols // r2_rows, 0))
    sc_w = part(group_b, (nb, wide_blocks * in_rows, mid), (0, (e_cols + r2_rows) // (wide_blocks * in_rows), 0))
    e2_w = part(group_c, (nb, e_cols, mid), (0, 0, 0))

    def spatial_weight(x, at):
        rows, per = s_rows, spread
        if s_rows % 16:
            x = x[:, at:].reshape(nc, spread, 9, s_rows, mid).transpose(0, 2, 1, 3, 4)
            x, at, rows, per = x.reshape(nc, 9 * mid, mid), 0, mid, 1
        return [part(x, (x.shape[0], rows, mid), (0, at // rows + tap, 0)) for tap in range(9)], per

    if s_rows % 16:
        s1_w = spatial_weight(jnp.concatenate([first[:, in_rows:], later], axis=1), 0)
    else:
        one, two = spatial_weight(first, in_rows), spatial_weight(later, -early * s_rows)
        s1_w = one[0][:early] + two[0][early:], spread
    s2_w = spatial_weight(group_c, e_cols)

    start = ber * crops
    sides = lax.dynamic_slice_in_dim(crop_sides, start, crops)
    ids = lax.dynamic_slice_in_dim(subnet_ids, start, crops)
    labels = jnp.arange(8, dtype=jnp.int32)
    member_all = (subnet_ids[None, :] == labels[:subs, None]).astype(F32)
    halves = crop_sides // 2
    count_full = jnp.sum(member_all * (crop_sides * crop_sides).astype(F32)[None, :], axis=1)
    count_half = jnp.sum(member_all * (halves * halves).astype(F32)[None, :], axis=1)
    counts = jnp.broadcast_to(
        jnp.concatenate([count_half, count_full, jnp.ones((8 - 2 * subs,), F32)])[:, None], (8, LANES)
    )
    pick = jnp.asarray(geo.rows[:, 0:1] == np.arange(crops)[None, :])
    side_row = jnp.sum(jnp.where(pick, sides[None, :], 0), axis=1, keepdims=True)
    id_row = jnp.sum(jnp.where(pick, ids[None, :], 0), axis=1, keepdims=True)
    row_i, row_j = jnp.asarray(geo.rows[:, 1:2]), jnp.asarray(geo.rows[:, 2:3])
    own = id_row == labels[None, :]
    seg_half = (own & (row_i < side_row // 2) & (row_j < side_row // 2)).astype(F32)
    seg_full = jnp.stack(
        [
            (own & (2 * row_i + p < side_row) & (2 * row_j + q < side_row)).astype(F32)
            for p in range(2)
            for q in range(2)
        ]
    )
    channel = jnp.arange(whole_mid, dtype=jnp.int32).reshape(nc, 1, mid)
    limits = jnp.concatenate([subnet_widths, jnp.zeros((8 - subs,), jnp.int32)])
    active = (channel < limits[None, :, None]).astype(F32)
    source = jnp.asarray(geo.source)
    own_params = jnp.concatenate([first_mid_gain, first_mid_bias, second_mid_gain, second_mid_bias], axis=0)
    params = jnp.stack(slots_of(own_params))

    def norm_slots(p_ref, raw, st_ref, par_ref, active_ref, seg, count, which, put, keep_slot):
        block, layer = which
        chan = p_ref[0]
        for r in range(nc):
            ch = chan ^ r
            total = st_ref[ch]
            for b in range(1, nb):
                total = total + st_ref[b * nc + ch]
            average, inverse = moments(row_list(total, 0, 2 * subs), count, subs)
            gain = par_ref[r, 4 * block + layer : 4 * block + layer + 1, :]
            bias = par_ref[r, 4 * block + 2 + layer : 4 * block + 3 + layer, :]
            act_rows = row_list(active_ref[ch], 0, subs)
            xhat = (raw(r).astype(F32) - select(seg, average)) * select(seg, inverse)
            keep = select(seg, act_rows)
            value, slope = silu_and_slope(gain * xhat + bias)
            put(r, (value * keep).astype(BF16))
            keep_slot(r, xhat, slope * keep, inverse)

    def send_sums(st_ref, seg, raw):
        value = raw.astype(F32)
        put_sums(st_ref, sums(seg, value) + sums(seg, value * value))
        fan_out(st_ref)

    every = nb * nc

    def joined(ref, *at):
        return jnp.concatenate([ref[(*at, r)] for r in range(nc)], axis=1)

    def block_rows(p_ref, ref, r):
        return jnp.concatenate([ref[(p_ref[0] ^ r) * spread + j] for j in range(spread)], axis=0)

    def joined_weight(p_ref, ref):
        return jnp.concatenate([block_rows(p_ref, ref, r) for r in range(nc)], axis=1)

    def tap_weight(p_ref, ref, per):
        return jnp.concatenate([ref[(p_ref[0] ^ r) * per + j] for r in range(nc) for j in range(per)], axis=0)

    def reduce_rows(ref, c):
        return jnp.concatenate([ref[c * spread + j] for j in range(spread)], axis=0)

    def shortcut_rows(ref, c):
        return jnp.concatenate(
            [
                jnp.concatenate(
                    [ref[c * spread + j, k * in_rows : (k + 1) * in_rows, :] for k in range(wide_blocks)], axis=1
                )
                for j in range(spread)
            ],
            axis=0,
        )

    def reduce_kernel(p_ref, e0, e1_, e2_, e3, w_ref, seg_ref, raw_ref, st_ref):
        w = jnp.concatenate([reduce_rows(w_ref, c) for c in range(nc)], axis=0)
        rows = [jnp.zeros((1, LANES), F32)] * (2 * subs)
        for k in range(4):
            seg = columns_of(seg_ref[k], subs)
            mask = mask_of(seg)
            raw = (dot(jnp.concatenate([e[k] for e in (e0, e1_, e2_, e3)], axis=1), w) * mask).astype(BF16)
            raw_ref[k] = raw
            value = raw.astype(F32)
            new = sums(seg, value) + sums(seg, value * value)
            rows = [a + b for a, b in zip(rows, new)]
        put_sums(st_ref, rows)
        fan_out(st_ref)

    def short_kernel(p_ref, e0, e1_, e2_, e3, w_ref, segh_ref, out_ref):
        w = jnp.concatenate([shortcut_rows(w_ref, c) for c in range(nc)], axis=0)
        got = dot(jnp.concatenate([e[...] for e in (e0, e1_, e2_, e3)], axis=1), w)
        out_ref[...] = got * jnp.sum(segh_ref[...], axis=1, keepdims=True)

    def spatial_one_kernel(
        p_ref, r0, r1_, r2_, r3, st_ref, par_ref, act_ref, segf_ref, segh_ref, cnt_ref, src_ref, *rest
    ):
        w_refs, (out_ref, xhat_ref, slope_ref, inv_ref, raw_ref, sto_ref) = rest[:9], rest[9:]
        refs = (r0, r1_, r2_, r3)
        count = row_list(cnt_ref[...], subs, subs)
        for k in range(4):
            seg = columns_of(segf_ref[k], subs)

            def put(r, value):
                out_ref[k, r] = value

            def keep_slot(r, xhat, slope, inverse):
                xhat_ref[r, k] = xhat.astype(BF16)
                slope_ref[r, k] = slope.astype(BF16)
                if k == 0 and r == 0:
                    put_rows(inv_ref, inverse)

            norm_slots(
                p_ref, lambda r: refs[r][k], st_ref, par_ref, act_ref, seg, count, (0, 0), put, keep_slot
            )
        src = src_ref[...]
        total = jnp.zeros((px, mid), F32)
        for tap in range(9):
            plane, shift = STRIDED_TAPS[tap]
            total = total + dot(shifted(src, shift, joined(out_ref, plane)), tap_weight(p_ref, w_refs[tap], s1_w[1]))
        raw = total.astype(BF16)
        raw_ref[...] = raw
        send_sums(sto_ref, columns_of(segh_ref[...], subs), raw)

    def mid_inputs(raws, st):
        return (*raws, st, params, active, seg_half, counts)

    def mid_outs():
        return (
            struct((nc, px, mid), BF16),
            struct((nc, px, mid)),
            struct((nc, px, mid)),
            struct((8, mid)),
        )

    def mid_part(which, p_ref, refs, st_ref, par_ref, act_ref, segh_ref, cnt_ref, out_ref, xhat_ref, slope_ref, inv_ref):
        seg = columns_of(segh_ref[...], subs)

        def put(r, value):
            out_ref[r] = value

        def keep_slot(r, xhat, slope, inverse):
            xhat_ref[r] = xhat
            slope_ref[r] = slope
            if r == 0:
                put_rows(inv_ref, inverse)

        norm_slots(
            p_ref, lambda r: refs[r][...], st_ref, par_ref, act_ref, seg,
            row_list(cnt_ref[...], 0, subs), which, put, keep_slot,
        )
        return seg

    def wide_sums(st_ref, seg, fields):
        for k in range(wide_blocks):
            rows = fields(k)
            put_sums(st_ref, rows, k * len(rows))
        fan_out(st_ref)

    def expand_one_kernel(
        p_ref, r0, r1_, r2_, r3, st_ref, par_ref, act_ref, segh_ref, cnt_ref, w_ref, short_ref,
        out_ref, xhat_ref, slope_ref, inv_ref, pre_ref, sto_ref,
    ):
        seg = mid_part(
            (0, 1), p_ref, (r0, r1_, r2_, r3), st_ref, par_ref, act_ref, segh_ref, cnt_ref,
            out_ref, xhat_ref, slope_ref, inv_ref,
        )
        pre_ref[...] = dot_nt(joined(out_ref), joined_weight(p_ref, w_ref))

        def fields(k):
            a, b = pre_ref[:, block_lanes(k)], short_ref[:, block_lanes(k)]
            return sums(seg, a) + sums(seg, a * a) + sums(seg, b) + sums(seg, b * b)

        wide_sums(sto_ref, seg, fields)

    def summed(st_ref, k=0, rows=2 * subs):
        total = st_ref[0, k * rows : (k + 1) * rows, :]
        for b in range(1, nb):
            total = total + st_ref[b, k * rows : (k + 1) * rows, :]
        return total

    def to_slots(slot_refs, value):
        for r in range(nc):
            slot_refs[r][...] = value[:, r * mid : (r + 1) * mid].astype(BF16)

    def send_upstream(p_ref, slot_refs, st_ref, seg, back, slope_ref, xhat_ref):
        for r in range(nc):
            u = (back[:, r * mid : (r + 1) * mid] * slope_ref[r]).astype(BF16)
            slot_refs[r][...] = u
            u = u.astype(F32)
            send_block(p_ref, st_ref, r, sums(seg, u) + sums(seg, u * xhat_ref[r]))

    def send_block(p_ref, st_ref, r, rows):
        block = jnp.concatenate(rows + [jnp.zeros((8 - len(rows), LANES), F32)], axis=0)
        for b in range(nb):
            st_ref[b * nc + (p_ref[0] ^ r)] = block

    def received(refs, *at):
        total = refs[0][at or ...].astype(F32)
        for ref in refs[1:]:
            total = total + ref[at or ...].astype(F32)
        return total

    def all_summed(st_ref):
        total = st_ref[0]
        for b in range(1, every):
            total = total + st_ref[b]
        return total

    def section_kernel(
        p_ref, st_ref, three_ref, short_ref, gain_ref, bias_ref, segh_ref, cnt_ref, w_ref,
        xh3_ref, xhs_ref, out_ref, slope_ref, inv_ref, low_ref, *slot_refs,
    ):
        seg = columns_of(segh_ref[...], subs)
        mask = mask_of(seg)
        count = row_list(cnt_ref[...], 0, subs)
        for k in range(wide_blocks):
            ln = block_lanes(k)
            total = summed(st_ref, k, 4 * subs)
            both = None
            for n, (pre, keep) in enumerate(((three_ref, xh3_ref), (short_ref, xhs_ref))):
                average, inverse = moments(row_list(total, 2 * subs * n, 2 * subs), count, subs)
                xhat = (pre[:, ln] - select(seg, average)) * select(seg, inverse)
                keep[:, ln] = xhat
                for s in range(subs):
                    inv_ref[n * subs + s : n * subs + s + 1, ln] = inverse[s]
                norm = gain_ref[n : n + 1, ln] * xhat + bias_ref[n : n + 1, ln]
                both = norm if both is None else both + norm
            value, slope = silu_and_slope(both)
            value = value * mask
            out_ref[:, ln] = value
            slope_ref[:, ln] = slope * mask
            low_ref[:, ln] = value.astype(BF16)
        to_slots(slot_refs, dot(low_ref[...], joined_weight(p_ref, w_ref)))

    def four_kernel(p_ref, s0, s1_, s2_, s3, segh_ref, raw_ref, sto_ref):
        total = s0[...].astype(F32)
        for ref in (s1_, s2_, s3):
            total = total + ref[...].astype(F32)
        raw = total.astype(BF16)
        raw_ref[...] = raw
        send_sums(sto_ref, columns_of(segh_ref[...], subs), raw)

    def spatial_two_kernel(
        p_ref, r0, r1_, r2_, r3, st_ref, par_ref, act_ref, segh_ref, cnt_ref, src_ref, *rest
    ):
        w_refs, (out_ref, xhat_ref, slope_ref, inv_ref, raw_ref, sto_ref) = rest[:9], rest[9:]
        seg = mid_part(
            (1, 0), p_ref, (r0, r1_, r2_, r3), st_ref, par_ref, act_ref, segh_ref, cnt_ref,
            out_ref, xhat_ref, slope_ref, inv_ref,
        )
        src = src_ref[...]
        total = jnp.zeros((px, mid), F32)
        whole = joined(out_ref)
        for tap in range(9):
            total = total + dot(shifted(src, tap, whole), tap_weight(p_ref, w_refs[tap], s2_w[1]))
        raw = total.astype(BF16)
        raw_ref[...] = raw
        send_sums(sto_ref, seg, raw)

    def expand_two_kernel(
        p_ref, r0, r1_, r2_, r3, st_ref, par_ref, act_ref, segh_ref, cnt_ref, w_ref,
        out_ref, xhat_ref, slope_ref, inv_ref, pre_ref, sto_ref,
    ):
        seg = mid_part(
            (1, 1), p_ref, (r0, r1_, r2_, r3), st_ref, par_ref, act_ref, segh_ref, cnt_ref,
            out_ref, xhat_ref, slope_ref, inv_ref,
        )
        pre_ref[...] = dot_nt(joined(out_ref), joined_weight(p_ref, w_ref))

        def fields(k):
            a = pre_ref[:, block_lanes(k)]
            return sums(seg, a) + sums(seg, a * a)

        wide_sums(sto_ref, seg, fields)

    def final_kernel(
        p_ref, st_ref, pre_ref, section_ref, cot_ref, gain_ref, bias_ref, segh_ref, cnt_ref, pick_ref,
        out_ref, grad_ref, xhat_ref, inv_ref, sto_ref,
    ):
        seg = columns_of(segh_ref[...], subs)
        mask = mask_of(seg)
        count = row_list(cnt_ref[...], 0, subs)
        picked = pick_ref[...]
        for k in range(wide_blocks):
            ln = block_lanes(k)
            average, inverse = moments(row_list(summed(st_ref, k), 0, 2 * subs), count, subs)
            xhat = (pre_ref[:, ln] - select(seg, average)) * select(seg, inverse)
            xhat_ref[:, ln] = xhat
            for s in range(subs):
                inv_ref[s : s + 1, ln] = inverse[s]
            both = gain_ref[:, ln] * xhat + bias_ref[:, ln] + section_ref[:, ln]
            value, slope = silu_and_slope(both)
            value = value * mask

            def place_out(i, j, first, rows):
                out_ref[i, j, first : first + rows.shape[0], ln] = rows

            geo.unpack(lambda first, count: value[first : first + count], place_out)
            parts = []
            geo.pack(picked, lambda i, j: cot_ref[i, j, :, ln], lambda first, rows: parts.append(rows))
            grad = jnp.concatenate(parts, axis=0).astype(F32) * mask * slope
            grad_ref[:, ln] = grad
            put_sums(sto_ref, sums(seg, grad) + sums(seg, grad * xhat), k * 2 * subs)
        fan_out(sto_ref)

    def norm_back(total, at, gain, inverse, u, xhat, seg, count):
        g = [total[s : s + 1] / count[s] for s in range(subs)]
        x = [total[at + s : at + s + 1] / count[s] for s in range(subs)]
        scale = select(seg, [gain * row for row in inverse])
        return (scale * (u - (select(seg, g) + xhat * select(seg, x)))).astype(BF16)

    def put_param_grads(ref, ln, total, pairs):
        for n, first in enumerate(pairs):
            row = total[first : first + 1]
            for s in range(1, subs):
                row = row + total[first + s : first + s + 1]
            ref[n : n + 1, ln] = row

    def back_six_kernel(
        p_ref, st_ref, u_ref, xhat_ref, inv_ref, gain_ref, segh_ref, cnt_ref, w_ref, slope_ref, xh5_ref, low_ref, par_ref, sto_ref, *slot_refs
    ):
        seg = columns_of(segh_ref[...], subs)
        count = row_list(cnt_ref[...], 0, subs)
        for k in range(wide_blocks):
            ln = block_lanes(k)
            total = summed(st_ref, k)
            put_param_grads(par_ref, ln, total, (subs, 0))
            low_ref[:, ln] = norm_back(
                total, subs, gain_ref[:, ln], row_list(inv_ref[:, ln], 0, subs), u_ref[:, ln], xhat_ref[:, ln], seg, count
            )
        send_upstream(p_ref, slot_refs, sto_ref, seg, dot(low_ref[...], joined_weight(p_ref, w_ref)), slope_ref, xh5_ref)

    def own_gain(ref, which):
        block, layer = which
        return ref[0, 4 * block + layer : 4 * block + layer + 1, :]

    def back_own(st_ref, u_refs, xhat_ref, inv_ref, params_ref, which, segh_ref, cnt_ref, par_ref):
        seg = columns_of(segh_ref[...], subs)
        total = all_summed(st_ref)
        put_param_grads(par_ref, slice(0, LANES), total, (subs, 0))
        return seg, norm_back(
            total, subs, own_gain(params_ref, which), row_list(inv_ref[...], 0, subs), received(u_refs), xhat_ref[...],
            seg, row_list(cnt_ref[...], 0, subs),
        )

    def back_spatial_kernel(which, taps, order, per, with_grads):
        def kernel(
            p_ref, st_ref, u0, u1, u2, u3, xhat_ref, inv_ref, params_ref, segh_ref, cnt_ref, src_ref,
            slope_ref, xhats_ref, segs_ref, *rest
        ):
            w_refs, rest = rest[:9], rest[9:]
            if with_grads:
                act_ref, keep_ref, send_ref, par_ref, sto_ref, *slot_refs = rest
            else:
                cols_ref, par_ref, sto_ref, *slot_refs = rest
            shifts = []
            _, low = back_own(
                st_ref, (u0, u1, u2, u3), xhat_ref, inv_ref, params_ref, which, segh_ref, cnt_ref, par_ref
            )
            src = src_ref[...]
            rows = [None] * nc
            back = None
            for n, tap in enumerate(order):
                plane, shift = taps[tap]
                g = shifted(src, 8 - shift, low)
                shifts.append(g)
                if not with_grads:
                    cols_ref[:, n * mid : (n + 1) * mid] = g
                new = dot_nt(g, tap_weight(p_ref, w_refs[tap], per))
                back = new if back is None else back + new
                if n < 8 and taps[order[n + 1]][0] == plane:
                    continue
                seg = columns_of(segs_ref[plane], subs)
                for r in range(nc):
                    u = (back[:, r * mid : (r + 1) * mid] * slope_ref[r, plane].astype(F32)).astype(BF16)
                    slot_refs[r][plane] = u
                    u = u.astype(F32)
                    got = sums(seg, u) + sums(seg, u * xhats_ref[r, plane].astype(F32))
                    rows[r] = got if rows[r] is None else [a + b for a, b in zip(rows[r], got)]
                back = None
            for r in range(nc):
                send_block(p_ref, sto_ref, r, rows[r])
            if with_grads:
                put_strided(p_ref, act_ref, shifts, keep_ref, send_ref)

        return kernel

    def back_plain_kernel(which):
        def kernel(p_ref, st_ref, u0, u1, u2, u3, xhat_ref, inv_ref, params_ref, segh_ref, cnt_ref, low_ref, par_ref):
            _, low_ref[...] = back_own(
                st_ref, (u0, u1, u2, u3), xhat_ref, inv_ref, params_ref, which, segh_ref, cnt_ref, par_ref
            )

        return kernel

    def back_section_kernel(
        p_ref, g0, g1, g2, g3, w_ref, grad_ref, slope_ref, xh3_ref, xhs_ref, segh_ref,
        whole_ref, u_ref, sto_ref,
    ):
        for r, ref in enumerate((g0, g1, g2, g3)):
            whole_ref[r] = ref[...]
        u_ref[...] = dot_nt(joined(whole_ref), joined_weight(p_ref, w_ref))
        seg = columns_of(segh_ref[...], subs)
        for k in range(wide_blocks):
            ln = block_lanes(k)
            u = (u_ref[:, ln] + grad_ref[:, ln]) * slope_ref[:, ln]
            u_ref[:, ln] = u
            rows = sums(seg, u) + sums(seg, u * xh3_ref[:, ln]) + sums(seg, u * xhs_ref[:, ln])
            put_sums(sto_ref, rows, k * 3 * subs)
        fan_out(sto_ref)

    def back_wide_kernel(
        p_ref, st_ref, u_ref, xh3_ref, xhs_ref, inv_ref, gain_ref, segh_ref, cnt_ref, w_ref, slope_ref, xh2_ref,
        three_ref, short_ref, par_ref, sto_ref, *slot_refs,
    ):
        seg = columns_of(segh_ref[...], subs)
        count = row_list(cnt_ref[...], 0, subs)
        for k in range(wide_blocks):
            ln = block_lanes(k)
            total = summed(st_ref, k, 3 * subs)
            put_param_grads(par_ref, ln, total, (subs, 2 * subs, 0))
            u = u_ref[:, ln]
            inverse = inv_ref[:, ln]
            three_ref[:, ln] = norm_back(
                total, subs, gain_ref[0:1, ln], row_list(inverse, 0, subs), u, xh3_ref[:, ln], seg, count
            )
            short_ref[:, ln] = norm_back(
                total, 2 * subs, gain_ref[1:2, ln], row_list(inverse, subs, subs), u, xhs_ref[:, ln], seg, count
            )
        send_upstream(p_ref, slot_refs, sto_ref, seg, dot(three_ref[...], joined_weight(p_ref, w_ref)), slope_ref, xh2_ref)

    def back_one_kernel(
        p_ref, st_ref, u0, u1, u2, u3, xhat_ref, inv_ref, params_ref, segf_ref, cnt_ref, w_ref, short_ref, sc_ref,
        low_ref, par_ref, *slot_refs,
    ):
        count = row_list(cnt_ref[...], subs, subs)
        total = all_summed(st_ref)
        put_param_grads(par_ref, slice(0, LANES), total, (subs, 0))
        for k in range(4):
            seg = columns_of(segf_ref[k], subs)
            low_ref[k] = norm_back(
                total, subs, own_gain(params_ref, (0, 0)), row_list(inv_ref[...], 0, subs),
                received((u0, u1, u2, u3), k), xhat_ref[k].astype(F32), seg, count,
            )
        for r in range(nc):
            w = reduce_rows(w_ref, p_ref[0] ^ r)
            for k in range(4):
                got = dot_nt(low_ref[k], w)
                if k == 0:
                    got = got + dot_nt(short_ref[...], shortcut_rows(sc_ref, p_ref[0] ^ r))
                slot_refs[r][k] = got.astype(BF16)

    def input_kernel(p_ref, a_ref, b_ref, c_ref, segf_ref, out_ref):
        for k in range(4):
            mask = jnp.sum(segf_ref[k], axis=1, keepdims=True)
            total = a_ref[k].astype(F32) + b_ref[k].astype(F32) + c_ref[k].astype(F32)
            total = total * mask

            def place_out(i, j, first, rows):
                out_ref[2 * i + k // 2, 2 * j + k % 2, first : first + rows.shape[0], :] = rows

            geo.unpack(lambda first, count: total[first : first + count], place_out)

    def put_expand(p_ref, out_ref, at, grad_ref, act_ref):
        for k in range(nc):
            got = dot_tn(grad_ref[...], act_ref[p_ref[0] ^ k]).astype(BF16)
            for j in range(spread):
                out_ref[k * spread + j, at : at + e_cols, :] = got[j * e_cols : (j + 1) * e_cols]

    def put_spatial(out_ref, at, k, taps, got):
        for j in range(spread):
            for n, tap in enumerate(taps):
                first = at + tap * s_rows
                out_ref[k * spread + j, first : first + s_rows, :] = got[
                    j * s_rows : (j + 1) * s_rows, n * mid : (n + 1) * mid
                ]

    def grads_two_kernel(p_ref, six_ref, act5_ref, act4_ref, cols_ref, out_ref):
        put_expand(p_ref, out_ref, 0, six_ref, act5_ref)
        for k in range(nc):
            got = dot_tn(act4_ref[p_ref[0] ^ k], cols_ref[...]).astype(BF16)
            put_spatial(out_ref, e_cols, k, range(9), got)

    def grads_mixed_kernel(p_ref, low_ref, four_ref, three_ref, act2_ref, e0, e1_, e2_, e3, short_ref, out_ref):
        for k in range(nc):
            got = dot_tn(low_ref[...], four_ref[p_ref[0] ^ k]).astype(BF16)
            for j in range(spread):
                out_ref[k * spread + j, 0:r2_rows, :] = got[j * r2_rows : (j + 1) * r2_rows]
        put_expand(p_ref, out_ref, r2_rows, three_ref, act2_ref)
        first = r2_rows + e_cols
        for c, entry_ref in enumerate((e0, e1_, e2_, e3)):
            got = dot_tn(entry_ref[...], short_ref[...]).astype(BF16)
            for j in range(spread):
                for k in range(wide_blocks):
                    out_ref[c * spread + j, first + k * in_rows : first + (k + 1) * in_rows, :] = got[
                        j * in_rows : (j + 1) * in_rows, block_lanes(k)
                    ]

    def grads_reduce_kernel(p_ref, e0, e1_, e2_, e3, grad_ref, out_ref):
        for c, entry_ref in enumerate((e0, e1_, e2_, e3)):
            got = dot_tn(entry_ref[0], grad_ref[0])
            for k in range(1, 4):
                got = got + dot_tn(entry_ref[k], grad_ref[k])
            for j in range(spread):
                out_ref[c * spread + j] = got[j * in_rows : (j + 1) * in_rows].astype(BF16)

    def put_strided(p_ref, act_ref, shifts, keep_ref, send_ref):
        odd = lax.rem(p_ref[1], 2) == 1
        for k in range(nc):
            first = 0
            for plane in range(4):
                taps = [t for t in STRIDED_ORDER if STRIDED_TAPS[t][0] == plane]
                cols = jnp.concatenate(shifts[first : first + len(taps)], axis=1)
                first += len(taps)
                got = dot_tn(act_ref[plane, p_ref[0] ^ k], cols)
                for j in range(0, spread, 2):
                    one, two = got[j * s_rows : (j + 1) * s_rows], got[(j + 1) * s_rows : (j + 2) * s_rows]
                    keep, send = jnp.where(odd, two, one).astype(BF16), jnp.where(odd, one, two).astype(BF16)
                    for n, tap in enumerate(taps):
                        rows = slice(tap * s_rows, (tap + 1) * s_rows)
                        keep_ref[(k * spread + j) // 2, rows, :] = keep[:, block_lanes(n)]
                        send_ref[(k * spread + j) // 2, rows, :] = send[:, block_lanes(n)]

    def mine(p_ref, pair_ref, got_ref):
        return pair_ref[lax.rem(p_ref[1], 2)].astype(F32) + got_ref[...].astype(F32)

    def total_kernel(p_ref, *refs):
        total = refs[0][...].astype(F32)
        for ref in refs[1:-1]:
            total = total + ref[...].astype(F32)
        refs[-1][...] = total.astype(refs[-1].dtype)

    def turn_kernel(p_ref, two_ref, two_got, mixed_ref, mixed_got, turn_out, s2_out, sc_out):
        two, mixed = mine(p_ref, two_ref, two_got), mine(p_ref, mixed_ref, mixed_got)
        turn_out[0:e_cols] = mixed[r2_rows : r2_rows + e_cols].astype(BF16)
        turn_out[e_cols : e_cols + r2_rows] = mixed[0:r2_rows].astype(BF16)
        turn_out[e_cols + r2_rows :] = two[0:e_cols].astype(BF16)
        s2_out[...] = two[e_cols:]
        first = r2_rows + e_cols
        for k in range(wide_blocks):
            sc_out[:, block_lanes(k)] = mixed[first + k * in_rows : first + (k + 1) * in_rows]

    def param_kernel(p_ref, one, two, wide_one, four, five, six, g1, b1, gw1, bw1, g2, b2, gw2, bw2):
        for first, second, gain, bias in ((one, two, g1, b1), (four, five, g2, b2)):
            for n, ref in enumerate((first, second)):
                gain[n : n + 1, :] = ref[0:1, :]
                bias[n : n + 1, :] = ref[1:2, :]
        gw1[...] = wide_one[0:2, :]
        bw1[0:1, :] = wide_one[2:3, :]
        bw1[1:2, :] = wide_one[2:3, :]
        gw2[...] = six[0:1, :]
        bw2[...] = six[1:2, :]

    def own_kernel(p_ref, turned_ref, one_ref, reduce_ref, e1_out, r2_out, e2_out, s1_out, r1_out):
        s1_out[...] = one_ref[...].astype(F32)
        total = reduce_ref[0].astype(F32)
        for b in range(1, nb):
            total = total + reduce_ref[b].astype(F32)
        r1_out[...] = total
        e1_out[...] = turned_ref[0:e_cols].astype(F32).T
        r2_out[...] = turned_ref[e_cols : e_cols + r2_rows].astype(F32)
        e2_out[...] = turned_ref[e_cols + r2_rows :].astype(F32).T

    def to_owners(shares):
        rows = shares.shape[1]
        groups = [list(range(first, nb, 2)) for first in range(2)]
        pair = lax.psum_scatter(
            shares.reshape(nb // 2, 2 * rows, mid), "batch", scatter_dimension=0, axis_index_groups=groups, tiled=False
        ).reshape(2, rows, mid)
        send = lax.dynamic_index_in_dim(pair, 1 - ber % 2, 0, False)
        return pair, lax.ppermute(send, "batch", [(i, i ^ 1) for i in range(nb)])

    st_mid, st_own, st_wide = (
        struct((every, 8, LANES)),
        struct((nb, 8, LANES)),
        struct((nb, whole_tiles(2 * subs * wide_blocks), LANES)),
    )
    matmul = 2 * px * whole_mid * wide
    mid_slots = [struct((px, mid), BF16)] * nc
    half = side // 2

    raw_one, st = call(
        reduce_kernel, (struct((4, px, mid), BF16), st_mid), place, *entries, r1_w, seg_full, flops=4 * matmul
    )
    (st,) = call(total_kernel, (st_mid,), place, st, after=[later])
    raws, st = slots_of(raw_one), to_all(st)
    act_one, xhat_one, slope_one, inv_one, raw_two, st = call(
        spatial_one_kernel,
        (
            struct((4, nc, px, mid), BF16),
            struct((nc, 4, px, mid), BF16),
            struct((nc, 4, px, mid), BF16),
            struct((8, mid)),
            struct((px, mid), BF16),
            st_mid,
        ),
        place, *raws, st, params, active, seg_full, seg_half, counts, source, *s1_w[0],
        flops=10 * matmul,
    )
    shorts = [part(entry, (None, None, px, part_in), (c, 0, 0, 0)) for c in range(nc)]
    (pre_short,) = call(short_kernel, (struct((px, wide)),), place, *shorts, sc_w, seg_half, flops=4 * matmul)
    raws, st = slots_of(raw_two), to_all(st)
    act_two, xhat_two, slope_two, inv_two, pre_three, st = call(
        expand_one_kernel,
        (*mid_outs(), struct((px, wide)), struct((nb, whole_tiles(4 * subs * wide_blocks), LANES))),
        place, *mid_inputs(raws, st), e1_w, pre_short,
        flops=2 * matmul,
    )
    xhat_three, xhat_short, section_out, slope_section, inv_wide, section_low, *slots = call(
        section_kernel,
        (
            *[struct((px, wide))] * 4,
            struct((8, wide)),
            struct((px, wide), BF16),
            *mid_slots,
        ),
        place, to_batch(st), pre_three, pre_short, first_wide_gain, first_wide_bias, seg_half, counts, r2_w,
        flops=2 * matmul,
    )

    raw_four, st = call(
        four_kernel, (struct((px, mid), BF16), st_mid), place, *swap_slots(slots), seg_half
    )
    raws, st = slots_of(raw_four), to_all(st)
    act_four, xhat_four, slope_four, inv_four, raw_five, st = call(
        spatial_two_kernel,
        (*mid_outs(), struct((px, mid), BF16), st_mid),
        place, *mid_inputs(raws, st), source, *s2_w[0],
        flops=8 * matmul,
    )
    raws, st = slots_of(raw_five), to_all(st)
    act_five, xhat_five, slope_five, inv_five, pre_six, st = call(
        expand_two_kernel,
        (*mid_outs(), struct((px, wide)), st_wide),
        place, *mid_inputs(raws, st), e2_w,
        flops=2 * matmul,
    )
    gain_six, bias_six = second_wide_gain[None], second_wide_bias[None]
    out_rows, grad_final, xhat_six, inv_six, st = call(
        final_kernel,
        (struct((half, half, crops, wide)), *[struct((px, wide))] * 2, struct((8, wide)), st_wide),
        place, to_batch(st), pre_six, section_out, cotangent.transpose(1, 2, 0, 3), gain_six, bias_six, seg_half, counts,
        pick_large,
    )
    output = out_rows.transpose(2, 0, 1, 3)

    grad_six, par_six, st, *slots = call(
        back_six_kernel,
        (struct((px, wide), BF16), struct((8, wide)), st_mid, *mid_slots),
        place, to_batch(st), grad_final, xhat_six, inv_six, gain_six, seg_half, counts, e2_w, slope_five, xhat_five,
        flops=2 * matmul,
    )

    def own(xhat):
        return part(xhat, (None, *xhat.shape[1:]), (0,) * xhat.ndim)

    raws, st = swap_slots(slots), to_all(st)
    cols_five, par_five, st, *slots = call(
        back_spatial_kernel((1, 1), UNIT_TAPS, list(range(9)), s2_w[1], False),
        (struct((px, 9 * mid), BF16), struct((8, mid)), st_mid, *[struct((1, px, mid), BF16)] * nc),
        place, st, *raws, own(xhat_five), inv_five, params, seg_half, counts, source, slope_four[:, None],
        xhat_four[:, None], seg_half[None], *s2_w[0],
        flops=8 * matmul,
    )
    raws, st = swap_slots([x.reshape(px, mid) for x in slots]), to_all(st)
    (shares_two,) = call(
        grads_two_kernel, (struct((nb, e_cols + 9 * s_rows, mid), BF16),),
        place, grad_six, act_five, act_four, cols_five, flops=10 * matmul,
    )
    grad_four, par_four = call(
        back_plain_kernel((1, 0)),
        (struct((px, mid), BF16), struct((8, mid))),
        place, st, *raws, own(xhat_four), inv_four, params, seg_half, counts, after=[shares_two],
    )
    whole_grad_four, u_wide, st = call(
        back_section_kernel,
        (struct((nc, px, mid), BF16), struct((px, wide)), struct((nb, whole_tiles(3 * subs * wide_blocks), LANES))),
        place, *slots_of(grad_four), r2_w, grad_final, slope_section, xhat_three, xhat_short, seg_half,
        flops=2 * matmul,
    )

    grad_three, grad_short, par_wide, st, *slots = call(
        back_wide_kernel,
        (
            struct((px, wide), BF16),
            struct((px, wide), BF16),
            struct((8, wide)),
            st_mid,
            *mid_slots,
        ),
        place, to_batch(st), u_wide, xhat_three, xhat_short, inv_wide, first_wide_gain, seg_half, counts, e1_w,
        slope_two, xhat_two,
        flops=2 * matmul,
    )
    raws, st = swap_slots(slots), to_all(st)
    (shares_mixed,) = call(
        grads_mixed_kernel, (struct((nb, b_rows, mid), BF16),),
        place, section_low, whole_grad_four, grad_three, act_two, *shorts, grad_short, flops=8 * matmul,
    )
    owned_two, owned_mixed = to_owners(shares_two), to_owners(shares_mixed)
    half_one = struct((nb // 2, 9 * s_rows, mid), BF16)
    keep, send, par_two, st, *slots = call(
        back_spatial_kernel((0, 1), STRIDED_TAPS, STRIDED_ORDER, s1_w[1], True),
        (half_one, half_one, struct((8, mid)), st_mid, *[struct((4, px, mid), BF16)] * nc),
        place, st, *raws, own(xhat_two), inv_two, params, seg_half, counts, source, slope_one, xhat_one, seg_full,
        *s1_w[0], act_one,
        flops=16 * matmul, after=[shares_mixed, owned_two[0]],
    )
    raws, st = swap_slots(slots), to_all(st)
    send = lax.ppermute(send, "batch", [(i, i ^ 1) for i in range(nb)])
    (sum_one,) = call(total_kernel, (half_one,), place, keep, send)
    grad_one, par_one, *slots = call(
        back_one_kernel,
        (struct((4, px, mid), BF16), struct((8, mid)), *[struct((4, px, part_in), BF16)] * nc),
        place, st, *raws, own(xhat_one), inv_one, params, seg_full, counts, r1_w, grad_short, sc_w,
        flops=8 * matmul, after=[sum_one],
    )
    far_first, own_back = chan_swap(slots[3], 1), chan_swap(slots[1], 1)
    far_sum = (slots[2].astype(F32) + far_first.astype(F32)).astype(BF16)
    far_back = chan_swap(far_sum, 2)

    (shares,) = call(
        grads_reduce_kernel, (struct((nb, in_rows, mid), BF16),),
        place, *entries, grad_one, flops=4 * matmul, after=[far_sum, owned_mixed[0]],
    )
    turned, s2_own, sc_own = call(
        turn_kernel,
        (struct((turn_rows, mid), BF16), struct((9 * s_rows, mid)), struct((in_rows, wide))),
        place, *owned_two, *owned_mixed,
    )
    s1_total = lax.psum_scatter(
        sum_one, "batch", scatter_dimension=0, tiled=False,
        axis_index_groups=[list(range(first, nb, 2)) for first in range(2)],
    )
    e1_own, r2_own, e2_own, s1_total, r1_out = call(
        own_kernel,
        (
            struct((mid, e_cols)),
            struct((r2_rows, mid)),
            struct((mid, e_cols)),
            struct((9 * s_rows, mid)),
            struct((in_rows, mid)),
        ),
        place, turn_share(turned), s1_total, to_batch(shares),
    )
    mid_pair, wide_pair, wide_row = struct((2, mid)), struct((2, wide)), struct((1, wide))
    own_params_grad = call(
        param_kernel,
        (mid_pair, mid_pair, wide_pair, wide_pair, mid_pair, mid_pair, wide_row, wide_row),
        place, par_one, par_two, par_wide, par_four, par_five, par_six, after=[far_sum],
    )
    outs = (
        output,
        s1_total.reshape(3, 3, s_rows, mid),
        e1_own,
        sc_own,
        r2_own,
        s2_own.reshape(3, 3, s_rows, mid),
        e2_own,
        *own_params_grad[:-2],
        own_params_grad[-2][0],
        own_params_grad[-1][0],
    )
    (input_grad,) = call(
        input_kernel, (struct((side, side, crops, part_in)),), place, slots[0], own_back, far_back, seg_full,
        after=[own_params_grad[0]],
    )
    return outs[:1] + (input_grad.transpose(2, 0, 1, 3), r1_out) + outs[1:]


def solution(mesh):
    placed = (
        P("batch", None, None, "chan"),
        P("batch", "chan"),
        P(None, None, "batch", "chan"),
        P("chan", "batch"),
        P("batch", "chan"),
        P("batch", "chan"),
        P(None, None, "batch", "chan"),
        P("chan", "batch"),
        P(None, "chan"),
        P(None, "chan"),
        P(None, "chan"),
        P(None, "chan"),
        P(None, "chan"),
        P(None, "chan"),
        P("chan"),
        P("chan"),
        P(),
        P(),
        P(),
        P("batch", None, None, "chan"),
    )
    outs = (
        P("batch", None, None, "chan"),
        P("batch", None, None, "chan"),
        P("batch", "chan"),
        P(None, None, "batch", "chan"),
        P("chan", "batch"),
        P("batch", "chan"),
        P("batch", "chan"),
        P(None, None, "batch", "chan"),
        P("chan", "batch"),
        P(None, "chan"),
        P(None, "chan"),
        P(None, "chan"),
        P(None, "chan"),
        P(None, "chan"),
        P(None, "chan"),
        P("chan"),
        P("chan"),
    )
    return jax.shard_map(local, mesh=mesh, in_specs=placed, out_specs=outs, check_vma=False)
```

```python
import jax
import jax.numpy as jnp
import numpy as np
from jax import lax
from jax.experimental import pallas as pl
from jax.experimental.pallas import tpu as pltpu
from jax.sharding import PartitionSpec as P

F32, BF16 = jnp.float32, jnp.bfloat16
EPS = 1e-05
SMALL = 6
LANES = 128
ALL = ("batch", "chan")


class Geometry:
    def __init__(self, crops, side):
        self.crops, self.side = crops, side
        self.half, self.small = side // 2, SMALL // 2
        self.large = [c for c in range(crops) if c % 8 < 2]
        grid = [(i, j) for i in range(self.half) for j in range(self.half)]
        self.common = [at for at in grid if max(at) < self.small]
        self.others = [at for at in grid if max(at) >= self.small]
        rows = [(c, i, j) for i, j in self.common for c in range(crops)]
        rows += [(c, i, j) for i, j in self.others for c in self.large]
        self.cut = len(self.common) * crops
        self.rows = np.array(rows, np.int32)
        self.pixels = len(rows)
        where = {tuple(r): n for n, r in enumerate(rows)}
        source = np.full((self.pixels, 16), -1, np.int32)
        for n, (crop, i, j) in enumerate(rows):
            for shift in range(9):
                source[n, shift] = where.get((crop, i + shift // 3 - 1, j + shift % 3 - 1), -1)
        self.source = source
        self.group = 8
        wanted = len(self.large)
        pick = np.zeros((self.group * wanted, self.group * crops), np.float32)
        for n in range(self.group):
            for m, c in enumerate(self.large):
                pick[n * wanted + m, n * crops + c] = 1.0
        self.pick = pick

    def pack(self, pick, load, store):
        for n, (i, j) in enumerate(self.common):
            store(n * self.crops, load(i, j))
        wanted = len(self.large)
        for n in range(0, len(self.others), self.group):
            rows = jnp.concatenate([load(i, j) for i, j in self.others[n : n + self.group]], axis=0)
            store(self.cut + n * wanted, dot(pick, rows).astype(rows.dtype))

    def unpack(self, load, store):
        for n, (i, j) in enumerate(self.common):
            store(i, j, 0, load(n * self.crops, self.crops))
        wanted = len(self.large)
        for n, (i, j) in enumerate(self.others):
            rows = load(self.cut + n * wanted, wanted)
            store(i, j, 0, jnp.zeros((self.crops, rows.shape[1]), rows.dtype))
            for m in range(0, wanted, 2):
                store(i, j, self.large[m], rows[m : m + 2])


UNIT_TAPS = [(0, tap) for tap in range(9)]
STRIDED_TAPS = [
    (2 * int(r != 1) + int(c != 1), 3 * (0 if r == 0 else 1) + (0 if c == 0 else 1))
    for r in range(3)
    for c in range(3)
]
STRIDED_ORDER = [tap for plane in range(4) for tap in range(9) if STRIDED_TAPS[tap][0] == plane]

SM = pl.BlockSpec(memory_space=pltpu.SMEM)


def struct(shape, dtype=F32):
    return jax.ShapeDtypeStruct(tuple(shape), dtype)


def whole_block(shape, at=None):
    at = at or (0,) * len(shape)
    return pl.BlockSpec(tuple(shape), lambda _: at)


def part(array, shape, at):
    return array, whole_block(shape, at)


def corner(array):
    shape = (1,) * (array.ndim - 2) + (16, LANES) if array.ndim > 1 else array.shape
    return array, whole_block([min(a, b) for a, b in zip(shape, array.shape)], (0,) * array.ndim)


def call(kernel, outs, place, *args, flops=10**8, mib=64, after=()):
    args = [a if isinstance(a, tuple) else (a, whole_block(a.shape)) for a in args]
    moved = sum(int(np.prod([n or 1 for n in b.block_shape])) * a.dtype.itemsize for a, b in args)
    moved += sum(int(np.prod(o.shape)) * o.dtype.itemsize for o in outs)
    used, args = len(args), args + [corner(a) for a in after]

    def body(p_ref, *refs):
        kernel(p_ref, *refs[:used], *refs[len(args) :])

    return pl.pallas_call(
        body,
        grid=(1,),
        out_shape=tuple(outs),
        in_specs=[SM] + [b for _, b in args],
        out_specs=tuple(whole_block(o.shape) for o in outs),
        compiler_params=pltpu.CompilerParams(vmem_limit_bytes=mib * 1024 * 1024),
        cost_estimate=pl.CostEstimate(flops=flops, bytes_accessed=moved, transcendentals=0),
    )(place, *[a for a, _ in args])


def dot(a, b):
    return jnp.dot(a, b, preferred_element_type=F32)


def dot_nt(a, b):
    return lax.dot_general(a, b, (((1,), (1,)), ((), ())), preferred_element_type=F32)


def dot_tn(a, b):
    return lax.dot_general(a, b, (((0,), (0,)), ((), ())), preferred_element_type=F32)


def columns_of(seg, subs):
    return [jnp.broadcast_to(seg[:, s : s + 1], (seg.shape[0], LANES)) for s in range(subs)]


def select(seg, rows):
    total = seg[0] * rows[0]
    for s in range(1, len(rows)):
        total = total + seg[s] * rows[s]
    return total


def mask_of(seg):
    mask = seg[0]
    for other in seg[1:]:
        mask = mask + other
    return mask


def sums(seg, field):
    return [jnp.sum(field * g, axis=0, keepdims=True) for g in seg]


def moments(total, count, subs):
    average = [total[s] / count[s] for s in range(subs)]
    inverse = [
        lax.rsqrt(total[subs + s] / count[s] - average[s] * average[s] + EPS) for s in range(subs)
    ]
    return average, inverse


def silu_and_slope(norm):
    sigmoid = jax.nn.sigmoid(norm)
    return norm * sigmoid, sigmoid * (1.0 + norm * (1.0 - sigmoid))


def shifted(source, shift, value):
    if shift == 4:
        return value
    rows = value.shape[0]
    at = lax.broadcasted_iota(jnp.int32, (rows, rows), 1)
    move = jnp.where(at == source[:, shift : shift + 1], 1.0, 0.0).astype(BF16)
    return dot(move, value).astype(BF16)


def put_rows(ref, rows):
    for n, row in enumerate(rows):
        ref[n : n + 1, :] = row


def put_sums(ref, rows, first=0):
    for n, row in enumerate(rows):
        ref[0, first + n : first + n + 1, :] = row


def fan_out(ref):
    block = ref[0]
    for b in range(1, ref.shape[0]):
        ref[b] = block


def whole_tiles(rows):
    return -(-rows // 8) * 8


def block_lanes(k):
    return slice(k * LANES, (k + 1) * LANES)


def row_list(block, first, count):
    return [block[n : n + 1] for n in range(first, first + count)]


def local(
    block_input,
    first_reduce,
    first_spatial,
    first_expand,
    first_shortcut,
    second_reduce,
    second_spatial,
    second_expand,
    first_mid_gain,
    first_mid_bias,
    first_wide_gain,
    first_wide_bias,
    second_mid_gain,
    second_mid_bias,
    second_wide_gain,
    second_wide_bias,
    subnet_widths,
    subnet_ids,
    crop_sides,
    cotangent,
):
    nb, nc = lax.axis_size("batch"), lax.axis_size("chan")
    spread = nb // nc
    crops, side = block_input.shape[0], block_input.shape[1]
    geo = Geometry(crops, side)
    px = geo.pixels
    subs = subnet_widths.shape[0]
    me, ber = lax.axis_index("chan"), lax.axis_index("batch")
    mid = first_reduce.shape[1]
    wide = first_shortcut.shape[1]
    part_in = block_input.shape[3]
    whole_mid = nc * mid
    wide_blocks = wide // LANES

    def chan_swap(x, r):
        return lax.ppermute(x, "chan", [(i, i ^ r) for i in range(nc)])

    def slots_of(x):
        return [x] + [chan_swap(x, r) for r in range(1, nc)]

    def swap_slots(x):
        return [x[0]] + [chan_swap(x[r], r) for r in range(1, nc)]

    def to_batch(x):
        return lax.all_to_all(x, "batch", 0, 0, tiled=True)

    def to_all(x):
        return lax.all_to_all(x, ALL, 0, 0, tiled=True)

    turn = []
    for zc in range(nc):
        for j in range(spread):
            for c in range(nc):
                turn.append(((zc * spread + j) * nc + c, (c * spread + j) * nc + zc))

    def turn_share(x):
        return lax.ppermute(x, ALL, turn)

    s_rows, e_cols, r2_rows = first_spatial.shape[2], first_expand.shape[1], second_reduce.shape[0]
    in_rows, part_in = first_reduce.shape[0], block_input.shape[3]
    early = 2

    def prepare_kernel(
        p_ref, x_ref, pick_ref, r1_ref, s1_ref, e1_ref, sc_ref, r2_ref, s2_ref, e2_ref,
        entry_ref, first_out, later_out, turn_out, mine_out, s2_out,
    ):
        picked = pick_ref[...]
        for k in range(4):

            def store(first, rows):
                entry_ref[k, first : first + rows.shape[0], :] = rows

            geo.pack(picked, lambda i, j: x_ref[2 * i + k // 2, 2 * j + k % 2], store)
        r1, s1 = r1_ref[...].astype(BF16), s1_ref[...].astype(BF16)
        for b in range(nb):
            first_out[b, 0:in_rows] = r1
            first_out[b, in_rows:] = s1[: early * s_rows]
            later_out[b] = s1[early * s_rows :]
        s2_out[...] = s2_ref[...].astype(BF16)
        turn_out[0:e_cols] = e1_ref[...].T.astype(BF16)
        turn_out[e_cols : e_cols + r2_rows] = r2_ref[...].astype(BF16)
        turn_out[e_cols + r2_rows :] = e2_ref[...].T.astype(BF16)
        for k in range(wide_blocks):
            mine_out[k * in_rows : (k + 1) * in_rows] = sc_ref[:, block_lanes(k)].astype(BF16)

    def gather_batch(x):
        return lax.all_gather(x, "batch", axis=0, tiled=False)

    place = jnp.stack([me, ber]).astype(jnp.int32)
    pick_large = jnp.asarray(geo.pick, BF16)
    b_rows, turn_rows = e_cols + r2_rows + wide_blocks * in_rows, 2 * e_cols + r2_rows
    entry, first, later, turned, mine, s2_rows = call(
        prepare_kernel,
        (
            struct((4, px, part_in), BF16),
            struct((nb, in_rows + early * s_rows, mid), BF16),
            struct((nb, (9 - early) * s_rows, mid), BF16),
            struct((turn_rows, mid), BF16),
            struct((wide_blocks * in_rows, mid), BF16),
            struct((9 * s_rows, mid), BF16),
        ),
        place, block_input.transpose(1, 2, 0, 3), pick_large, first_reduce, first_spatial.reshape(9 * s_rows, mid),
        first_expand, first_shortcut, second_reduce, second_spatial.reshape(9 * s_rows, mid), second_expand,
    )
    entry = lax.all_gather(entry, "chan", axis=0, tiled=False)
    entries = [part(entry, (None, 4, px, part_in), (c, 0, 0, 0)) for c in range(nc)]
    first, later, turned = to_batch(first), to_batch(later), turn_share(turned)
    r1_w = part(first, (nb, in_rows, mid), (0, 0, 0))

    def shares_kernel(p_ref, turned_ref, mine_ref, s2_ref, b_out, c_out):
        b_out[0 : e_cols + r2_rows] = turned_ref[0 : e_cols + r2_rows]
        b_out[e_cols + r2_rows :] = mine_ref[...]
        c_out[0:e_cols] = turned_ref[e_cols + r2_rows :]
        c_out[e_cols:] = s2_ref[...]

    b_share, c_share = call(
        shares_kernel,
        (struct((b_rows, mid), BF16), struct((e_cols + 9 * s_rows, mid), BF16)),
        place, turned, mine, s2_rows, after=[first],
    )
    group_b, group_c = gather_batch(b_share), gather_batch(c_share)
    e1_w = part(group_b, (nb, e_cols, mid), (0, 0, 0))
    r2_w = part(group_b, (nb, r2_rows, mid), (0, e_cols // r2_rows, 0))
    sc_w = part(group_b, (nb, wide_blocks * in_rows, mid), (0, (e_cols + r2_rows) // (wide_blocks * in_rows), 0))
    e2_w = part(group_c, (nb, e_cols, mid), (0, 0, 0))

    def spatial_weight(x, at):
        rows, per = s_rows, spread
        if s_rows % 16:
            x = x[:, at:].reshape(nc, spread, 9, s_rows, mid).transpose(0, 2, 1, 3, 4)
            x, at, rows, per = x.reshape(nc, 9 * mid, mid), 0, mid, 1
        return [part(x, (x.shape[0], rows, mid), (0, at // rows + tap, 0)) for tap in range(9)], per

    if s_rows % 16:
        s1_w = spatial_weight(jnp.concatenate([first[:, in_rows:], later], axis=1), 0)
    else:
        one, two = spatial_weight(first, in_rows), spatial_weight(later, -early * s_rows)
        s1_w = one[0][:early] + two[0][early:], spread
    s2_w = spatial_weight(group_c, e_cols)

    start = ber * crops
    sides = lax.dynamic_slice_in_dim(crop_sides, start, crops)
    ids = lax.dynamic_slice_in_dim(subnet_ids, start, crops)
    labels = jnp.arange(8, dtype=jnp.int32)
    member_all = (subnet_ids[None, :] == labels[:subs, None]).astype(F32)
    halves = crop_sides // 2
    count_full = jnp.sum(member_all * (crop_sides * crop_sides).astype(F32)[None, :], axis=1)
    count_half = jnp.sum(member_all * (halves * halves).astype(F32)[None, :], axis=1)
    counts = jnp.broadcast_to(
        jnp.concatenate([count_half, count_full, jnp.ones((8 - 2 * subs,), F32)])[:, None], (8, LANES)
    )
    pick = jnp.asarray(geo.rows[:, 0:1] == np.arange(crops)[None, :])
    side_row = jnp.sum(jnp.where(pick, sides[None, :], 0), axis=1, keepdims=True)
    id_row = jnp.sum(jnp.where(pick, ids[None, :], 0), axis=1, keepdims=True)
    row_i, row_j = jnp.asarray(geo.rows[:, 1:2]), jnp.asarray(geo.rows[:, 2:3])
    own = id_row == labels[None, :]
    seg_half = (own & (row_i < side_row // 2) & (row_j < side_row // 2)).astype(F32)
    seg_full = jnp.stack(
        [
            (own & (2 * row_i + p < side_row) & (2 * row_j + q < side_row)).astype(F32)
            for p in range(2)
            for q in range(2)
        ]
    )
    channel = jnp.arange(whole_mid, dtype=jnp.int32).reshape(nc, 1, mid)
    limits = jnp.concatenate([subnet_widths, jnp.zeros((8 - subs,), jnp.int32)])
    active = (channel < limits[None, :, None]).astype(F32)
    source = jnp.asarray(geo.source)
    own_params = jnp.concatenate([first_mid_gain, first_mid_bias, second_mid_gain, second_mid_bias], axis=0)
    params = jnp.stack(slots_of(own_params))

    def norm_slots(p_ref, raw, st_ref, par_ref, active_ref, seg, count, which, put, keep_slot):
        block, layer = which
        chan = p_ref[0]
        for r in range(nc):
            ch = chan ^ r
            total = st_ref[ch]
            for b in range(1, nb):
                total = total + st_ref[b * nc + ch]
            average, inverse = moments(row_list(total, 0, 2 * subs), count, subs)
            gain = par_ref[r, 4 * block + layer : 4 * block + layer + 1, :]
            bias = par_ref[r, 4 * block + 2 + layer : 4 * block + 3 + layer, :]
            act_rows = row_list(active_ref[ch], 0, subs)
            xhat = (raw(r).astype(F32) - select(seg, average)) * select(seg, inverse)
            keep = select(seg, act_rows)
            value, slope = silu_and_slope(gain * xhat + bias)
            put(r, (value * keep).astype(BF16))
            keep_slot(r, xhat, slope * keep, inverse)

    def send_sums(st_ref, seg, raw):
        value = raw.astype(F32)
        put_sums(st_ref, sums(seg, value) + sums(seg, value * value))
        fan_out(st_ref)

    every = nb * nc

    def joined(ref, *at):
        return jnp.concatenate([ref[(*at, r)] for r in range(nc)], axis=1)

    def block_rows(p_ref, ref, r):
        return jnp.concatenate([ref[(p_ref[0] ^ r) * spread + j] for j in range(spread)], axis=0)

    def joined_weight(p_ref, ref):
        return jnp.concatenate([block_rows(p_ref, ref, r) for r in range(nc)], axis=1)

    def tap_weight(p_ref, ref, per):
        return jnp.concatenate([ref[(p_ref[0] ^ r) * per + j] for r in range(nc) for j in range(per)], axis=0)

    def reduce_rows(ref, c):
        return jnp.concatenate([ref[c * spread + j] for j in range(spread)], axis=0)

    def shortcut_rows(ref, c):
        return jnp.concatenate(
            [
                jnp.concatenate(
                    [ref[c * spread + j, k * in_rows : (k + 1) * in_rows, :] for k in range(wide_blocks)], axis=1
                )
                for j in range(spread)
            ],
            axis=0,
        )

    def reduce_kernel(p_ref, e0, e1_, e2_, e3, w_ref, seg_ref, raw_ref, st_ref):
        w = jnp.concatenate([reduce_rows(w_ref, c) for c in range(nc)], axis=0)
        rows = [jnp.zeros((1, LANES), F32)] * (2 * subs)
        for k in range(4):
            seg = columns_of(seg_ref[k], subs)
            mask = mask_of(seg)
            raw = (dot(jnp.concatenate([e[k] for e in (e0, e1_, e2_, e3)], axis=1), w) * mask).astype(BF16)
            raw_ref[k] = raw
            value = raw.astype(F32)
            new = sums(seg, value) + sums(seg, value * value)
            rows = [a + b for a, b in zip(rows, new)]
        put_sums(st_ref, rows)
        fan_out(st_ref)

    def short_kernel(p_ref, e0, e1_, e2_, e3, w_ref, segh_ref, out_ref):
        w = jnp.concatenate([shortcut_rows(w_ref, c) for c in range(nc)], axis=0)
        got = dot(jnp.concatenate([e[...] for e in (e0, e1_, e2_, e3)], axis=1), w)
        out_ref[...] = got * jnp.sum(segh_ref[...], axis=1, keepdims=True)

    def spatial_one_kernel(
        p_ref, r0, r1_, r2_, r3, st_ref, par_ref, act_ref, segf_ref, segh_ref, cnt_ref, src_ref, *rest
    ):
        w_refs, (out_ref, xhat_ref, slope_ref, inv_ref, raw_ref, sto_ref) = rest[:9], rest[9:]
        refs = (r0, r1_, r2_, r3)
        count = row_list(cnt_ref[...], subs, subs)
        for k in range(4):
            seg = columns_of(segf_ref[k], subs)

            def put(r, value):
                out_ref[k, r] = value

            def keep_slot(r, xhat, slope, inverse):
                xhat_ref[r, k] = xhat.astype(BF16)
                slope_ref[r, k] = slope.astype(BF16)
                if k == 0 and r == 0:
                    put_rows(inv_ref, inverse)

            norm_slots(
                p_ref, lambda r: refs[r][k], st_ref, par_ref, act_ref, seg, count, (0, 0), put, keep_slot
            )
        src = src_ref[...]
        total = jnp.zeros((px, mid), F32)
        for tap in range(9):
            plane, shift = STRIDED_TAPS[tap]
            total = total + dot(shifted(src, shift, joined(out_ref, plane)), tap_weight(p_ref, w_refs[tap], s1_w[1]))
        raw = total.astype(BF16)
        raw_ref[...] = raw
        send_sums(sto_ref, columns_of(segh_ref[...], subs), raw)

    def mid_inputs(raws, st):
        return (*raws, st, params, active, seg_half, counts)

    def mid_outs():
        return (
            struct((nc, px, mid), BF16),
            struct((nc, px, mid)),
            struct((nc, px, mid)),
            struct((8, mid)),
        )

    def mid_part(which, p_ref, refs, st_ref, par_ref, act_ref, segh_ref, cnt_ref, out_ref, xhat_ref, slope_ref, inv_ref):
        seg = columns_of(segh_ref[...], subs)

        def put(r, value):
            out_ref[r] = value

        def keep_slot(r, xhat, slope, inverse):
            xhat_ref[r] = xhat
            slope_ref[r] = slope
            if r == 0:
                put_rows(inv_ref, inverse)

        norm_slots(
            p_ref, lambda r: refs[r][...], st_ref, par_ref, act_ref, seg,
            row_list(cnt_ref[...], 0, subs), which, put, keep_slot,
        )
        return seg

    def wide_sums(st_ref, seg, fields):
        for k in range(wide_blocks):
            rows = fields(k)
            put_sums(st_ref, rows, k * len(rows))
        fan_out(st_ref)

    def expand_one_kernel(
        p_ref, r0, r1_, r2_, r3, st_ref, par_ref, act_ref, segh_ref, cnt_ref, w_ref, short_ref,
        out_ref, xhat_ref, slope_ref, inv_ref, pre_ref, sto_ref,
    ):
        seg = mid_part(
            (0, 1), p_ref, (r0, r1_, r2_, r3), st_ref, par_ref, act_ref, segh_ref, cnt_ref,
            out_ref, xhat_ref, slope_ref, inv_ref,
        )
        pre_ref[...] = dot_nt(joined(out_ref), joined_weight(p_ref, w_ref))

        def fields(k):
            a, b = pre_ref[:, block_lanes(k)], short_ref[:, block_lanes(k)]
            return sums(seg, a) + sums(seg, a * a) + sums(seg, b) + sums(seg, b * b)

        wide_sums(sto_ref, seg, fields)

    def summed(st_ref, k=0, rows=2 * subs):
        total = st_ref[0, k * rows : (k + 1) * rows, :]
        for b in range(1, nb):
            total = total + st_ref[b, k * rows : (k + 1) * rows, :]
        return total

    def to_slots(slot_refs, value):
        for r in range(nc):
            slot_refs[r][...] = value[:, r * mid : (r + 1) * mid].astype(BF16)

    def send_upstream(p_ref, slot_refs, st_ref, seg, back, slope_ref, xhat_ref):
        for r in range(nc):
            u = (back[:, r * mid : (r + 1) * mid] * slope_ref[r]).astype(BF16)
            slot_refs[r][...] = u
            u = u.astype(F32)
            send_block(p_ref, st_ref, r, sums(seg, u) + sums(seg, u * xhat_ref[r]))

    def send_block(p_ref, st_ref, r, rows):
        block = jnp.concatenate(rows + [jnp.zeros((8 - len(rows), LANES), F32)], axis=0)
        for b in range(nb):
            st_ref[b * nc + (p_ref[0] ^ r)] = block

    def received(refs, *at):
        total = refs[0][at or ...].astype(F32)
        for ref in refs[1:]:
            total = total + ref[at or ...].astype(F32)
        return total

    def all_summed(st_ref):
        total = st_ref[0]
        for b in range(1, every):
            total = total + st_ref[b]
        return total

    def section_kernel(
        p_ref, st_ref, three_ref, short_ref, gain_ref, bias_ref, segh_ref, cnt_ref, w_ref,
        xh3_ref, xhs_ref, out_ref, slope_ref, inv_ref, low_ref, *slot_refs,
    ):
        seg = columns_of(segh_ref[...], subs)
        mask = mask_of(seg)
        count = row_list(cnt_ref[...], 0, subs)
        for k in range(wide_blocks):
            ln = block_lanes(k)
            total = summed(st_ref, k, 4 * subs)
            both = None
            for n, (pre, keep) in enumerate(((three_ref, xh3_ref), (short_ref, xhs_ref))):
                average, inverse = moments(row_list(total, 2 * subs * n, 2 * subs), count, subs)
                xhat = (pre[:, ln] - select(seg, average)) * select(seg, inverse)
                keep[:, ln] = xhat
                for s in range(subs):
                    inv_ref[n * subs + s : n * subs + s + 1, ln] = inverse[s]
                norm = gain_ref[n : n + 1, ln] * xhat + bias_ref[n : n + 1, ln]
                both = norm if both is None else both + norm
            value, slope = silu_and_slope(both)
            value = value * mask
            out_ref[:, ln] = value
            slope_ref[:, ln] = slope * mask
            low_ref[:, ln] = value.astype(BF16)
        to_slots(slot_refs, dot(low_ref[...], joined_weight(p_ref, w_ref)))

    def four_kernel(p_ref, s0, s1_, s2_, s3, segh_ref, raw_ref, sto_ref):
        total = s0[...].astype(F32)
        for ref in (s1_, s2_, s3):
            total = total + ref[...].astype(F32)
        raw = total.astype(BF16)
        raw_ref[...] = raw
        send_sums(sto_ref, columns_of(segh_ref[...], subs), raw)

    def spatial_two_kernel(
        p_ref, r0, r1_, r2_, r3, st_ref, par_ref, act_ref, segh_ref, cnt_ref, src_ref, *rest
    ):
        w_refs, (out_ref, xhat_ref, slope_ref, inv_ref, raw_ref, sto_ref) = rest[:9], rest[9:]
        seg = mid_part(
            (1, 0), p_ref, (r0, r1_, r2_, r3), st_ref, par_ref, act_ref, segh_ref, cnt_ref,
            out_ref, xhat_ref, slope_ref, inv_ref,
        )
        src = src_ref[...]
        total = jnp.zeros((px, mid), F32)
        whole = joined(out_ref)
        for tap in range(9):
            total = total + dot(shifted(src, tap, whole), tap_weight(p_ref, w_refs[tap], s2_w[1]))
        raw = total.astype(BF16)
        raw_ref[...] = raw
        send_sums(sto_ref, seg, raw)

    def expand_two_kernel(
        p_ref, r0, r1_, r2_, r3, st_ref, par_ref, act_ref, segh_ref, cnt_ref, w_ref,
        out_ref, xhat_ref, slope_ref, inv_ref, pre_ref, sto_ref,
    ):
        seg = mid_part(
            (1, 1), p_ref, (r0, r1_, r2_, r3), st_ref, par_ref, act_ref, segh_ref, cnt_ref,
            out_ref, xhat_ref, slope_ref, inv_ref,
        )
        pre_ref[...] = dot_nt(joined(out_ref), joined_weight(p_ref, w_ref))

        def fields(k):
            a = pre_ref[:, block_lanes(k)]
            return sums(seg, a) + sums(seg, a * a)

        wide_sums(sto_ref, seg, fields)

    def final_kernel(
        p_ref, st_ref, pre_ref, section_ref, cot_ref, gain_ref, bias_ref, segh_ref, cnt_ref, pick_ref,
        out_ref, grad_ref, xhat_ref, inv_ref, sto_ref,
    ):
        seg = columns_of(segh_ref[...], subs)
        mask = mask_of(seg)
        count = row_list(cnt_ref[...], 0, subs)
        picked = pick_ref[...]
        for k in range(wide_blocks):
            ln = block_lanes(k)
            average, inverse = moments(row_list(summed(st_ref, k), 0, 2 * subs), count, subs)
            xhat = (pre_ref[:, ln] - select(seg, average)) * select(seg, inverse)
            xhat_ref[:, ln] = xhat
            for s in range(subs):
                inv_ref[s : s + 1, ln] = inverse[s]
            both = gain_ref[:, ln] * xhat + bias_ref[:, ln] + section_ref[:, ln]
            value, slope = silu_and_slope(both)
            value = value * mask

            def place_out(i, j, first, rows):
                out_ref[i, j, first : first + rows.shape[0], ln] = rows

            geo.unpack(lambda first, count: value[first : first + count], place_out)
            parts = []
            geo.pack(picked, lambda i, j: cot_ref[i, j, :, ln], lambda first, rows: parts.append(rows))
            grad = jnp.concatenate(parts, axis=0).astype(F32) * mask * slope
            grad_ref[:, ln] = grad
            put_sums(sto_ref, sums(seg, grad) + sums(seg, grad * xhat), k * 2 * subs)
        fan_out(sto_ref)

    def norm_back(total, at, gain, inverse, u, xhat, seg, count):
        g = [total[s : s + 1] / count[s] for s in range(subs)]
        x = [total[at + s : at + s + 1] / count[s] for s in range(subs)]
        scale = select(seg, [gain * row for row in inverse])
        return (scale * (u - (select(seg, g) + xhat * select(seg, x)))).astype(BF16)

    def put_param_grads(ref, ln, total, pairs):
        for n, first in enumerate(pairs):
            row = total[first : first + 1]
            for s in range(1, subs):
                row = row + total[first + s : first + s + 1]
            ref[n : n + 1, ln] = row

    def back_six_kernel(
        p_ref, st_ref, u_ref, xhat_ref, inv_ref, gain_ref, segh_ref, cnt_ref, w_ref, slope_ref, xh5_ref, low_ref, par_ref, sto_ref, *slot_refs
    ):
        seg = columns_of(segh_ref[...], subs)
        count = row_list(cnt_ref[...], 0, subs)
        for k in range(wide_blocks):
            ln = block_lanes(k)
            total = summed(st_ref, k)
            put_param_grads(par_ref, ln, total, (subs, 0))
            low_ref[:, ln] = norm_back(
                total, subs, gain_ref[:, ln], row_list(inv_ref[:, ln], 0, subs), u_ref[:, ln], xhat_ref[:, ln], seg, count
            )
        send_upstream(p_ref, slot_refs, sto_ref, seg, dot(low_ref[...], joined_weight(p_ref, w_ref)), slope_ref, xh5_ref)

    def own_gain(ref, which):
        block, layer = which
        return ref[0, 4 * block + layer : 4 * block + layer + 1, :]

    def back_own(st_ref, u_refs, xhat_ref, inv_ref, params_ref, which, segh_ref, cnt_ref, par_ref):
        seg = columns_of(segh_ref[...], subs)
        total = all_summed(st_ref)
        put_param_grads(par_ref, slice(0, LANES), total, (subs, 0))
        return seg, norm_back(
            total, subs, own_gain(params_ref, which), row_list(inv_ref[...], 0, subs), received(u_refs), xhat_ref[...],
            seg, row_list(cnt_ref[...], 0, subs),
        )

    def back_spatial_kernel(which, taps, order, per, with_grads):
        def kernel(
            p_ref, st_ref, u0, u1, u2, u3, xhat_ref, inv_ref, params_ref, segh_ref, cnt_ref, src_ref,
            slope_ref, xhats_ref, segs_ref, *rest
        ):
            w_refs, rest = rest[:9], rest[9:]
            if with_grads:
                act_ref, keep_ref, send_ref, par_ref, sto_ref, *slot_refs = rest
            else:
                cols_ref, par_ref, sto_ref, *slot_refs = rest
            shifts = []
            _, low = back_own(
                st_ref, (u0, u1, u2, u3), xhat_ref, inv_ref, params_ref, which, segh_ref, cnt_ref, par_ref
            )
            src = src_ref[...]
            rows = [None] * nc
            back = None
            for n, tap in enumerate(order):
                plane, shift = taps[tap]
                g = shifted(src, 8 - shift, low)
                shifts.append(g)
                if not with_grads:
                    cols_ref[:, n * mid : (n + 1) * mid] = g
                new = dot_nt(g, tap_weight(p_ref, w_refs[tap], per))
                back = new if back is None else back + new
                if n < 8 and taps[order[n + 1]][0] == plane:
                    continue
                seg = columns_of(segs_ref[plane], subs)
                for r in range(nc):
                    u = (back[:, r * mid : (r + 1) * mid] * slope_ref[r, plane].astype(F32)).astype(BF16)
                    slot_refs[r][plane] = u
                    u = u.astype(F32)
                    got = sums(seg, u) + sums(seg, u * xhats_ref[r, plane].astype(F32))
                    rows[r] = got if rows[r] is None else [a + b for a, b in zip(rows[r], got)]
                back = None
            for r in range(nc):
                send_block(p_ref, sto_ref, r, rows[r])
            if with_grads:
                put_strided(p_ref, act_ref, shifts, keep_ref, send_ref)

        return kernel

    def back_plain_kernel(which):
        def kernel(p_ref, st_ref, u0, u1, u2, u3, xhat_ref, inv_ref, params_ref, segh_ref, cnt_ref, low_ref, par_ref):
            _, low_ref[...] = back_own(
                st_ref, (u0, u1, u2, u3), xhat_ref, inv_ref, params_ref, which, segh_ref, cnt_ref, par_ref
            )

        return kernel

    def back_section_kernel(
        p_ref, g0, g1, g2, g3, w_ref, grad_ref, slope_ref, xh3_ref, xhs_ref, segh_ref,
        whole_ref, u_ref, sto_ref,
    ):
        for r, ref in enumerate((g0, g1, g2, g3)):
            whole_ref[r] = ref[...]
        u_ref[...] = dot_nt(joined(whole_ref), joined_weight(p_ref, w_ref))
        seg = columns_of(segh_ref[...], subs)
        for k in range(wide_blocks):
            ln = block_lanes(k)
            u = (u_ref[:, ln] + grad_ref[:, ln]) * slope_ref[:, ln]
            u_ref[:, ln] = u
            rows = sums(seg, u) + sums(seg, u * xh3_ref[:, ln]) + sums(seg, u * xhs_ref[:, ln])
            put_sums(sto_ref, rows, k * 3 * subs)
        fan_out(sto_ref)

    def back_wide_kernel(
        p_ref, st_ref, u_ref, xh3_ref, xhs_ref, inv_ref, gain_ref, segh_ref, cnt_ref, w_ref, slope_ref, xh2_ref,
        three_ref, short_ref, par_ref, sto_ref, *slot_refs,
    ):
        seg = columns_of(segh_ref[...], subs)
        count = row_list(cnt_ref[...], 0, subs)
        for k in range(wide_blocks):
            ln = block_lanes(k)
            total = summed(st_ref, k, 3 * subs)
            put_param_grads(par_ref, ln, total, (subs, 2 * subs, 0))
            u = u_ref[:, ln]
            inverse = inv_ref[:, ln]
            three_ref[:, ln] = norm_back(
                total, subs, gain_ref[0:1, ln], row_list(inverse, 0, subs), u, xh3_ref[:, ln], seg, count
            )
            short_ref[:, ln] = norm_back(
                total, 2 * subs, gain_ref[1:2, ln], row_list(inverse, subs, subs), u, xhs_ref[:, ln], seg, count
            )
        send_upstream(p_ref, slot_refs, sto_ref, seg, dot(three_ref[...], joined_weight(p_ref, w_ref)), slope_ref, xh2_ref)

    def back_one_kernel(
        p_ref, st_ref, u0, u1, u2, u3, xhat_ref, inv_ref, params_ref, segf_ref, cnt_ref, w_ref, short_ref, sc_ref,
        low_ref, par_ref, *slot_refs,
    ):
        count = row_list(cnt_ref[...], subs, subs)
        total = all_summed(st_ref)
        put_param_grads(par_ref, slice(0, LANES), total, (subs, 0))
        for k in range(4):
            seg = columns_of(segf_ref[k], subs)
            low_ref[k] = norm_back(
                total, subs, own_gain(params_ref, (0, 0)), row_list(inv_ref[...], 0, subs),
                received((u0, u1, u2, u3), k), xhat_ref[k].astype(F32), seg, count,
            )
        for r in range(nc):
            w = reduce_rows(w_ref, p_ref[0] ^ r)
            for k in range(4):
                got = dot_nt(low_ref[k], w)
                if k == 0:
                    got = got + dot_nt(short_ref[...], shortcut_rows(sc_ref, p_ref[0] ^ r))
                slot_refs[r][k] = got.astype(BF16)

    def input_kernel(p_ref, a_ref, b_ref, c_ref, segf_ref, out_ref):
        for k in range(4):
            mask = jnp.sum(segf_ref[k], axis=1, keepdims=True)
            total = a_ref[k].astype(F32) + b_ref[k].astype(F32) + c_ref[k].astype(F32)
            total = total * mask

            def place_out(i, j, first, rows):
                out_ref[2 * i + k // 2, 2 * j + k % 2, first : first + rows.shape[0], :] = rows

            geo.unpack(lambda first, count: total[first : first + count], place_out)

    def put_expand(p_ref, out_ref, at, grad_ref, act_ref):
        for k in range(nc):
            got = dot_tn(grad_ref[...], act_ref[p_ref[0] ^ k]).astype(BF16)
            for j in range(spread):
                out_ref[k * spread + j, at : at + e_cols, :] = got[j * e_cols : (j + 1) * e_cols]

    def put_spatial(out_ref, at, k, taps, got):
        for j in range(spread):
            for n, tap in enumerate(taps):
                first = at + tap * s_rows
                out_ref[k * spread + j, first : first + s_rows, :] = got[
                    j * s_rows : (j + 1) * s_rows, n * mid : (n + 1) * mid
                ]

    def grads_two_kernel(p_ref, six_ref, act5_ref, act4_ref, cols_ref, out_ref):
        put_expand(p_ref, out_ref, 0, six_ref, act5_ref)
        for k in range(nc):
            got = dot_tn(act4_ref[p_ref[0] ^ k], cols_ref[...]).astype(BF16)
            put_spatial(out_ref, e_cols, k, range(9), got)

    def grads_mixed_kernel(p_ref, low_ref, four_ref, three_ref, act2_ref, e0, e1_, e2_, e3, short_ref, out_ref):
        for k in range(nc):
            got = dot_tn(low_ref[...], four_ref[p_ref[0] ^ k]).astype(BF16)
            for j in range(spread):
                out_ref[k * spread + j, 0:r2_rows, :] = got[j * r2_rows : (j + 1) * r2_rows]
        put_expand(p_ref, out_ref, r2_rows, three_ref, act2_ref)
        first = r2_rows + e_cols
        for c, entry_ref in enumerate((e0, e1_, e2_, e3)):
            got = dot_tn(entry_ref[...], short_ref[...]).astype(BF16)
            for j in range(spread):
                for k in range(wide_blocks):
                    out_ref[c * spread + j, first + k * in_rows : first + (k + 1) * in_rows, :] = got[
                        j * in_rows : (j + 1) * in_rows, block_lanes(k)
                    ]

    def grads_reduce_kernel(p_ref, e0, e1_, e2_, e3, grad_ref, out_ref):
        for c, entry_ref in enumerate((e0, e1_, e2_, e3)):
            got = dot_tn(entry_ref[0], grad_ref[0])
            for k in range(1, 4):
                got = got + dot_tn(entry_ref[k], grad_ref[k])
            for j in range(spread):
                out_ref[c * spread + j] = got[j * in_rows : (j + 1) * in_rows].astype(BF16)

    def put_strided(p_ref, act_ref, shifts, keep_ref, send_ref):
        odd = lax.rem(p_ref[1], 2) == 1
        for k in range(nc):
            first = 0
            for plane in range(4):
                taps = [t for t in STRIDED_ORDER if STRIDED_TAPS[t][0] == plane]
                cols = jnp.concatenate(shifts[first : first + len(taps)], axis=1)
                first += len(taps)
                got = dot_tn(act_ref[plane, p_ref[0] ^ k], cols)
                for j in range(0, spread, 2):
                    one, two = got[j * s_rows : (j + 1) * s_rows], got[(j + 1) * s_rows : (j + 2) * s_rows]
                    keep, send = jnp.where(odd, two, one).astype(BF16), jnp.where(odd, one, two).astype(BF16)
                    for n, tap in enumerate(taps):
                        rows = slice(tap * s_rows, (tap + 1) * s_rows)
                        keep_ref[(k * spread + j) // 2, rows, :] = keep[:, block_lanes(n)]
                        send_ref[(k * spread + j) // 2, rows, :] = send[:, block_lanes(n)]

    def mine(p_ref, pair_ref, got_ref):
        return pair_ref[lax.rem(p_ref[1], 2)].astype(F32) + got_ref[...].astype(F32)

    def total_kernel(p_ref, *refs):
        total = refs[0][...].astype(F32)
        for ref in refs[1:-1]:
            total = total + ref[...].astype(F32)
        refs[-1][...] = total.astype(refs[-1].dtype)

    def turn_kernel(p_ref, two_ref, two_got, mixed_ref, mixed_got, turn_out, s2_out, sc_out):
        two, mixed = mine(p_ref, two_ref, two_got), mine(p_ref, mixed_ref, mixed_got)
        turn_out[0:e_cols] = mixed[r2_rows : r2_rows + e_cols].astype(BF16)
        turn_out[e_cols : e_cols + r2_rows] = mixed[0:r2_rows].astype(BF16)
        turn_out[e_cols + r2_rows :] = two[0:e_cols].astype(BF16)
        s2_out[...] = two[e_cols:]
        first = r2_rows + e_cols
        for k in range(wide_blocks):
            sc_out[:, block_lanes(k)] = mixed[first + k * in_rows : first + (k + 1) * in_rows]

    def param_kernel(p_ref, one, two, wide_one, four, five, six, g1, b1, gw1, bw1, g2, b2, gw2, bw2):
        for first, second, gain, bias in ((one, two, g1, b1), (four, five, g2, b2)):
            for n, ref in enumerate((first, second)):
                gain[n : n + 1, :] = ref[0:1, :]
                bias[n : n + 1, :] = ref[1:2, :]
        gw1[...] = wide_one[0:2, :]
        bw1[0:1, :] = wide_one[2:3, :]
        bw1[1:2, :] = wide_one[2:3, :]
        gw2[...] = six[0:1, :]
        bw2[...] = six[1:2, :]

    def own_kernel(p_ref, turned_ref, one_ref, reduce_ref, *rest):
        params_in, (e1_out, r2_out, e2_out, s1_out, r1_out, *params_out) = rest[:6], rest[6:]
        param_kernel(p_ref, *params_in, *params_out)
        s1_out[...] = one_ref[...].astype(F32)
        total = reduce_ref[0].astype(F32)
        for b in range(1, nb):
            total = total + reduce_ref[b].astype(F32)
        r1_out[...] = total
        e1_out[...] = turned_ref[0:e_cols].astype(F32).T
        r2_out[...] = turned_ref[e_cols : e_cols + r2_rows].astype(F32)
        e2_out[...] = turned_ref[e_cols + r2_rows :].astype(F32).T

    def to_owners(shares):
        rows = shares.shape[1]
        groups = [list(range(first, nb, 2)) for first in range(2)]
        pair = lax.psum_scatter(
            shares.reshape(nb // 2, 2 * rows, mid), "batch", scatter_dimension=0, axis_index_groups=groups, tiled=False
        ).reshape(2, rows, mid)
        send = lax.dynamic_index_in_dim(pair, 1 - ber % 2, 0, False)
        return pair, lax.ppermute(send, "batch", [(i, i ^ 1) for i in range(nb)])

    st_mid, st_own, st_wide = (
        struct((every, 8, LANES)),
        struct((nb, 8, LANES)),
        struct((nb, whole_tiles(2 * subs * wide_blocks), LANES)),
    )
    matmul = 2 * px * whole_mid * wide
    mid_slots = [struct((px, mid), BF16)] * nc
    half = side // 2

    raw_one, st = call(
        reduce_kernel, (struct((4, px, mid), BF16), st_mid), place, *entries, r1_w, seg_full, flops=4 * matmul
    )
    (st,) = call(total_kernel, (st_mid,), place, st, after=[later])
    raws, st = slots_of(raw_one), to_all(st)
    act_one, xhat_one, slope_one, inv_one, raw_two, st = call(
        spatial_one_kernel,
        (
            struct((4, nc, px, mid), BF16),
            struct((nc, 4, px, mid), BF16),
            struct((nc, 4, px, mid), BF16),
            struct((8, mid)),
            struct((px, mid), BF16),
            st_mid,
        ),
        place, *raws, st, params, active, seg_full, seg_half, counts, source, *s1_w[0],
        flops=10 * matmul,
    )
    shorts = [part(entry, (None, None, px, part_in), (c, 0, 0, 0)) for c in range(nc)]
    (pre_short,) = call(short_kernel, (struct((px, wide)),), place, *shorts, sc_w, seg_half, flops=4 * matmul)
    raws, st = slots_of(raw_two), to_all(st)
    act_two, xhat_two, slope_two, inv_two, pre_three, st = call(
        expand_one_kernel,
        (*mid_outs(), struct((px, wide)), struct((nb, whole_tiles(4 * subs * wide_blocks), LANES))),
        place, *mid_inputs(raws, st), e1_w, pre_short,
        flops=2 * matmul,
    )
    xhat_three, xhat_short, section_out, slope_section, inv_wide, section_low, *slots = call(
        section_kernel,
        (
            *[struct((px, wide))] * 4,
            struct((8, wide)),
            struct((px, wide), BF16),
            *mid_slots,
        ),
        place, to_batch(st), pre_three, pre_short, first_wide_gain, first_wide_bias, seg_half, counts, r2_w,
        flops=2 * matmul,
    )

    raw_four, st = call(
        four_kernel, (struct((px, mid), BF16), st_mid), place, *swap_slots(slots), seg_half
    )
    raws, st = slots_of(raw_four), to_all(st)
    act_four, xhat_four, slope_four, inv_four, raw_five, st = call(
        spatial_two_kernel,
        (*mid_outs(), struct((px, mid), BF16), st_mid),
        place, *mid_inputs(raws, st), source, *s2_w[0],
        flops=8 * matmul,
    )
    raws, st = slots_of(raw_five), to_all(st)
    act_five, xhat_five, slope_five, inv_five, pre_six, st = call(
        expand_two_kernel,
        (*mid_outs(), struct((px, wide)), st_wide),
        place, *mid_inputs(raws, st), e2_w,
        flops=2 * matmul,
    )
    gain_six, bias_six = second_wide_gain[None], second_wide_bias[None]
    out_rows, grad_final, xhat_six, inv_six, st = call(
        final_kernel,
        (struct((half, half, crops, wide)), *[struct((px, wide))] * 2, struct((8, wide)), st_wide),
        place, to_batch(st), pre_six, section_out, cotangent.transpose(1, 2, 0, 3), gain_six, bias_six, seg_half, counts,
        pick_large,
    )
    output = out_rows.transpose(2, 0, 1, 3)

    grad_six, par_six, st, *slots = call(
        back_six_kernel,
        (struct((px, wide), BF16), struct((8, wide)), st_mid, *mid_slots),
        place, to_batch(st), grad_final, xhat_six, inv_six, gain_six, seg_half, counts, e2_w, slope_five, xhat_five,
        flops=2 * matmul,
    )

    def own(xhat):
        return part(xhat, (None, *xhat.shape[1:]), (0,) * xhat.ndim)

    raws, st = swap_slots(slots), to_all(st)
    cols_five, par_five, st, *slots = call(
        back_spatial_kernel((1, 1), UNIT_TAPS, list(range(9)), s2_w[1], False),
        (struct((px, 9 * mid), BF16), struct((8, mid)), st_mid, *[struct((1, px, mid), BF16)] * nc),
        place, st, *raws, own(xhat_five), inv_five, params, seg_half, counts, source, slope_four[:, None],
        xhat_four[:, None], seg_half[None], *s2_w[0],
        flops=8 * matmul,
    )
    raws, st = swap_slots([x.reshape(px, mid) for x in slots]), to_all(st)
    (shares_two,) = call(
        grads_two_kernel, (struct((nb, e_cols + 9 * s_rows, mid), BF16),),
        place, grad_six, act_five, act_four, cols_five, flops=10 * matmul,
    )
    grad_four, par_four = call(
        back_plain_kernel((1, 0)),
        (struct((px, mid), BF16), struct((8, mid))),
        place, st, *raws, own(xhat_four), inv_four, params, seg_half, counts, after=[shares_two],
    )
    whole_grad_four, u_wide, st = call(
        back_section_kernel,
        (struct((nc, px, mid), BF16), struct((px, wide)), struct((nb, whole_tiles(3 * subs * wide_blocks), LANES))),
        place, *slots_of(grad_four), r2_w, grad_final, slope_section, xhat_three, xhat_short, seg_half,
        flops=2 * matmul,
    )

    grad_three, grad_short, par_wide, st, *slots = call(
        back_wide_kernel,
        (
            struct((px, wide), BF16),
            struct((px, wide), BF16),
            struct((8, wide)),
            st_mid,
            *mid_slots,
        ),
        place, to_batch(st), u_wide, xhat_three, xhat_short, inv_wide, first_wide_gain, seg_half, counts, e1_w,
        slope_two, xhat_two,
        flops=2 * matmul,
    )
    raws, st = swap_slots(slots), to_all(st)
    (shares_mixed,) = call(
        grads_mixed_kernel, (struct((nb, b_rows, mid), BF16),),
        place, section_low, whole_grad_four, grad_three, act_two, *shorts, grad_short, flops=8 * matmul,
    )
    owned_two, owned_mixed = to_owners(shares_two), to_owners(shares_mixed)
    half_one = struct((nb // 2, 9 * s_rows, mid), BF16)
    keep, send, par_two, st, *slots = call(
        back_spatial_kernel((0, 1), STRIDED_TAPS, STRIDED_ORDER, s1_w[1], True),
        (half_one, half_one, struct((8, mid)), st_mid, *[struct((4, px, mid), BF16)] * nc),
        place, st, *raws, own(xhat_two), inv_two, params, seg_half, counts, source, slope_one, xhat_one, seg_full,
        *s1_w[0], act_one,
        flops=16 * matmul, after=[shares_mixed, owned_two[0]],
    )
    raws, st = swap_slots(slots), to_all(st)
    send = lax.ppermute(send, "batch", [(i, i ^ 1) for i in range(nb)])
    (sum_one,) = call(total_kernel, (half_one,), place, keep, send)
    grad_one, par_one, *slots = call(
        back_one_kernel,
        (struct((4, px, mid), BF16), struct((8, mid)), *[struct((4, px, part_in), BF16)] * nc),
        place, st, *raws, own(xhat_one), inv_one, params, seg_full, counts, r1_w, grad_short, sc_w,
        flops=8 * matmul, after=[sum_one],
    )
    far_first, own_back = chan_swap(slots[3], 1), chan_swap(slots[1], 1)
    far_sum = (slots[2].astype(F32) + far_first.astype(F32)).astype(BF16)
    far_back = chan_swap(far_sum, 2)

    (shares,) = call(
        grads_reduce_kernel, (struct((nb, in_rows, mid), BF16),),
        place, *entries, grad_one, flops=4 * matmul, after=[far_sum, owned_mixed[0]],
    )
    turned, s2_own, sc_own = call(
        turn_kernel,
        (struct((turn_rows, mid), BF16), struct((9 * s_rows, mid)), struct((in_rows, wide))),
        place, *owned_two, *owned_mixed,
    )
    s1_total = lax.psum_scatter(
        sum_one, "batch", scatter_dimension=0, tiled=False,
        axis_index_groups=[list(range(first, nb, 2)) for first in range(2)],
    )
    mid_pair, wide_pair, wide_row = struct((2, mid)), struct((2, wide)), struct((1, wide))
    e1_own, r2_own, e2_own, s1_total, r1_out, *own_params_grad = call(
        own_kernel,
        (
            struct((mid, e_cols)),
            struct((r2_rows, mid)),
            struct((mid, e_cols)),
            struct((9 * s_rows, mid)),
            struct((in_rows, mid)),
            mid_pair, mid_pair, wide_pair, wide_pair, mid_pair, mid_pair, wide_row, wide_row,
        ),
        place, turn_share(turned), s1_total, to_batch(shares), par_one, par_two, par_wide, par_four, par_five, par_six,
    )
    outs = (
        output,
        s1_total.reshape(3, 3, s_rows, mid),
        e1_own,
        sc_own,
        r2_own,
        s2_own.reshape(3, 3, s_rows, mid),
        e2_own,
        *own_params_grad[:-2],
        own_params_grad[-2][0],
        own_params_grad[-1][0],
    )
    (input_grad,) = call(
        input_kernel, (struct((side, side, crops, part_in)),), place, slots[0], own_back, far_back, seg_full,
    )
    return outs[:1] + (input_grad.transpose(2, 0, 1, 3), r1_out) + outs[1:]


def solution(mesh):
    placed = (
        P("batch", None, None, "chan"),
        P("batch", "chan"),
        P(None, None, "batch", "chan"),
        P("chan", "batch"),
        P("batch", "chan"),
        P("batch", "chan"),
        P(None, None, "batch", "chan"),
        P("chan", "batch"),
        P(None, "chan"),
        P(None, "chan"),
        P(None, "chan"),
        P(None, "chan"),
        P(None, "chan"),
        P(None, "chan"),
        P("chan"),
        P("chan"),
        P(),
        P(),
        P(),
        P("batch", None, None, "chan"),
    )
    outs = (
        P("batch", None, None, "chan"),
        P("batch", None, None, "chan"),
        P("batch", "chan"),
        P(None, None, "batch", "chan"),
        P("chan", "batch"),
        P("batch", "chan"),
        P("batch", "chan"),
        P(None, None, "batch", "chan"),
        P("chan", "batch"),
        P(None, "chan"),
        P(None, "chan"),
        P(None, "chan"),
        P(None, "chan"),
        P(None, "chan"),
        P(None, "chan"),
        P("chan"),
        P("chan"),
    )
    return jax.shard_map(local, mesh=mesh, in_specs=placed, out_specs=outs, check_vma=False)
```
